32 devices in a mesh: dp: 16 (over z, y, core), fsdp: 2 (over x).
Axes of the slice: x: 2, y: 2, z: 4, core: 2. Of those that a mesh axis runs over, the one named last changes fastest.
Arguments:
- acts: bfloat16 [2, 32, 512, 1024], P(None, ('dp', 'fsdp')), may hold values from -6 to 6
- cotangent: bfloat16 [2, 32, 512, 1024], P(None, ('dp', 'fsdp')), may hold values from -6 to 6
- seg_ids: int32 [2, 32, 512], P(None, ('dp', 'fsdp')), may hold values from 0 to 7, never falling along the last dimension, each value on 1 to 256 neighbouring positions
- pad_mask: int32 [2, 32, 512], P(None, ('dp', 'fsdp')), may hold values from 0 to 1, as said below
- qkv_weight: bfloat16 [1024, 3072], P('fsdp', 'dp')
- out_weight: bfloat16 [1024, 1024], P('fsdp', 'dp'), may hold values from -0.1875 to 0.1875
- in_weight: bfloat16 [1024, 4096], P('fsdp', 'dp'), may hold values from -0.1875 to 0.1875
- down_weight: bfloat16 [4096, 1024], P('fsdp', 'dp'), may hold values from -0.1875 to 0.1875
- biases: float32 [12288], replicated
- moment_first: float32 [2, 6, 32, 32], P('fsdp'), as said below
- moment_second: float32 [2, 6, 32, 32], P('fsdp'), as said below
- basis_left: float32 [2, 6, 32, 32], P('fsdp'), as said below
- basis_right: float32 [2, 6, 32, 32], P('fsdp'), as said below
- owners: int32 [12], replicated, may hold values from 0 to 1, as said below
Outputs:
- out_acts: bfloat16 [2, 32, 512, 1024], P(None, ('dp', 'fsdp'))
- in_grad: bfloat16 [2, 32, 512, 1024], P(None, ('dp', 'fsdp'))
- bias_grad: float32 [12288], replicated
- moment_first_new: float32 [2, 6, 32, 32], P('fsdp')
- moment_second_new: float32 [2, 6, 32, 32], P('fsdp')
- bias_new: float32 [12288], replicated
- bias_low: bfloat16 [12288], replicated
The draws below stay inside these ranges and needn't reach their ends.
Inputs may be any that keep to these rules, and one draw needn't show every extreme that they name: `seg_ids`: never falling along a slot. `pad_mask`: in each slot the ones are a prefix of 384 to 512 positions and the zeros fill the rest. `owners`: every fsdp index owns at most 6 blocks and some own exactly 6. `moment_first`: slot (f, c) holds the block that owner f holds at rank c; other slots are ignored. `moment_second`: Positive; slots as in moment_first. `basis_left`: each slot is an orthogonal matrix; slots as in moment_first. `basis_right`: each slot is an orthogonal matrix; slots as in moment_first.
All inputs are finite; a program needn't handle non-finite values.
Results may differ from the reference program's by a relative error of at most 0.017.
Values may be sent and summed in bfloat16 or wider, within the bound.
A program may use at most 192 MiB of HBM per device.

```python
import math
import jax
import jax.numpy as jnp
import numpy as np
from jax import lax

D = 1024
H = 16
HD = 64
FF = 4096
SEQ = 512
MB = 2
NSEG = 8
BS = 32
STEP = 5
SLOTS = 32
TOKENS = 32768
PCOUNT = 12288
NBLK = 12
NOWN = 2
CAP = 6


def owner_list(key):
    shuffled = jax.random.permutation(jax.random.fold_in(key, 11), NBLK)
    return (shuffled % NOWN).astype(jnp.int32)


def placement_draw(key):
    owners = owner_list(key)
    index_b = jnp.arange(NBLK, dtype=jnp.int32)
    same_owner = owners[:, None] == owners[None, :]
    earlier = index_b[None, :] < index_b[:, None]
    rank_of = jnp.sum((same_owner & earlier).astype(jnp.int32), axis=1)
    owner_hit = owners[None, None, :] == jnp.arange(NOWN, dtype=jnp.int32)[:, None, None]
    slot_hit = rank_of[None, None, :] == jnp.arange(CAP, dtype=jnp.int32)[None, :, None]
    return (owner_hit & slot_hit).astype(jnp.float32)


def slot_scale(key):
    scale_table = jnp.array([0.7, 0.8, 0.8] + [0.35] * (NBLK - 8) + [0.6, 0.95, 0.95, 1.0, 1.0], jnp.float32)
    scale_table = scale_table * math.sqrt(TOKENS)
    centre_table = jnp.array([1.0, 1.0, 1.0] + [4.0] * (NBLK - 8) + [1.0, 1.0, 1.0, 1.0, 1.0], jnp.float32)
    slot_table = placement_draw(key)
    filled = jnp.sum(slot_table, axis=2)
    scales = jnp.sum(slot_table * scale_table[None, None, :], axis=2) + (1.0 - filled) * math.sqrt(TOKENS)
    centres = jnp.sum(slot_table * centre_table[None, None, :], axis=2) + (1.0 - filled)
    return (scales, centres)


def orthogonal_stack(key):
    rows_i = jnp.arange(BS, dtype=jnp.float32)[:, None]
    col_index = jnp.arange(BS, dtype=jnp.float32)[None, :]
    cosine = jnp.sqrt(2.0 / BS) * jnp.cos(math.pi * (2.0 * col_index + 1.0) * rows_i / (2.0 * BS))
    cosine = cosine * jnp.where(rows_i == 0.0, math.sqrt(0.5), 1.0)
    scores = jax.random.randint(jax.random.fold_in(key, 1), (NOWN, CAP, BS), 0, 1 << 20) * BS + jnp.arange(BS, dtype=jnp.int32)
    shuffled = jnp.argsort(scores, axis=-1)
    picked = cosine[shuffled]
    sign_row = (2 * jax.random.randint(jax.random.fold_in(key, 2), (NOWN, CAP, BS), 0, 2) - 1).astype(jnp.float32)
    sign_col = (2 * jax.random.randint(jax.random.fold_in(key, 3), (NOWN, CAP, BS), 0, 2) - 1).astype(jnp.float32)
    return picked * sign_row[..., :, None] * sign_col[..., None, :]


def draw_owners(key, part):
    return owner_list(key)


def draw_pad_mask(key, part):
    cut_len = jax.random.randint(jax.random.fold_in(key, 5), (MB, SLOTS, 1), 0, SEQ // 4 + 1)
    places = jnp.arange(SEQ, dtype=jnp.int32)[None, None, :]
    return (places < SEQ - cut_len).astype(jnp.int32)


def draw_qkv_weight(key, part):
    columns = jnp.arange(3 * D, dtype=jnp.int32)
    value_scale = math.sqrt(SEQ / (3.0 * NSEG))
    col_scale = jnp.where(columns >= 2 * D, value_scale, 1.0) / math.sqrt(D)
    jitter = jax.random.truncated_normal(jax.random.fold_in(key, 41), -6.0, 6.0, (D, 3 * D), jnp.float32)
    return (jitter * col_scale[None, :]).astype(jnp.bfloat16)


def draw_biases(key, part):
    places = jnp.arange(PCOUNT, dtype=jnp.int32)
    jitter = jax.random.normal(jax.random.fold_in(key, 3), (PCOUNT,), jnp.float32)
    gain_zone = (places >= 4 * D + FF) & (places < 5 * D + FF) | (places >= 6 * D + FF) & (places < 7 * D + FF)
    return jnp.where(gain_zone, 1.0 + 0.15 * jitter, 0.2 * jitter)


def draw_moment_first(key, part):
    scales, centres = slot_scale(key)
    jitter = jax.random.normal(jax.random.fold_in(key, 21), (NOWN, CAP, BS, BS), jnp.float32)
    return scales[:, :, None, None] * jitter


def draw_moment_second(key, part):
    scales, centres = slot_scale(key)
    factor = jnp.exp(jax.random.uniform(jax.random.fold_in(key, 23), (NOWN, CAP, BS, BS), jnp.float32, math.log(0.5), math.log(2.0)))
    return (scales * scales * centres)[:, :, None, None] * factor


def draw_basis_left(key, part):
    return orthogonal_stack(jax.random.fold_in(key, 31))


def draw_basis_right(key, part):
    return orthogonal_stack(jax.random.fold_in(key, 37))


def steps_of(key, shape, pieces, smallest, high):
    loudness, own = 1.0, jax.random.fold_in(key, 6)
    for dim, parts in pieces:
        draws = jnp.exp(jax.random.uniform(jax.random.fold_in(own, dim), (parts,), jnp.float32, smallest / len(pieces), high / len(pieces)))
        loudness = loudness * jnp.repeat(draws, shape[dim] // parts).reshape([-1 if axis == dim else 1 for axis in range(len(shape))])
    return loudness


def split_up(number_of, total, limit, skew):
    portions = [(1 << 20) // math.isqrt(grade ** skew) + 1 for grade in range(2, number_of + 1)]
    spare, given = total - limit - (number_of - 1), [1] * (number_of - 1)
    while spare > 0:
        movable = [i for i in range(number_of - 1) if given[i] < limit]
        pool, left = sum([portions[i] for i in movable]), spare
        for i in movable:
            extra = min(limit - given[i], max(1, left * portions[i] // pool), spare)
            given[i] = given[i] + extra
            spare = spare - extra
    return np.array([limit] + given)


def ragged_sizes(key, amount, total, reach, lean):
    if amount == 2:
        one = jax.random.randint(key, (), max(1, total - reach), min(reach, total - 1) + 1)
        return jnp.stack([one, total - one])
    sizes = jnp.asarray(split_up(amount, total, reach, lean), jnp.int32)
    pairs = (amount - 1) // 2
    donor, taker = sizes[1:1 + 2 * pairs:2], sizes[2:2 + 2 * pairs:2]
    slack = jnp.minimum(donor - 1, reach - taker)
    passed = jax.random.randint(jax.random.fold_in(key, 1), (pairs,), 0, 1 << 20) % (slack + 1)
    sizes = sizes.at[1:1 + 2 * pairs:2].set(donor - passed).at[2:2 + 2 * pairs:2].set(taker + passed)
    return sizes[jax.random.permutation(jax.random.fold_in(key, 2), amount)]


def scatter_about(stream_key, dims, width, most, split=(), held_as=jnp.bfloat16):
    entries = jax.random.normal(stream_key, dims, jnp.float32) * width
    if len(split) > 0:
        entries = steps_of(stream_key, dims, split, -0.22, 0.18) * entries
    return jnp.clip(entries, min=-most, max=most).astype(held_as)


def setup_inputs(seed: int = 0) -> dict:
    key_of = jax.random.split(jax.random.key(seed), 15)
    acts = scatter_about(key_of[0], (MB, SLOTS, SEQ, D), 1.0, 6.0, ((1, 32),))
    cotangent = scatter_about(key_of[1], (MB, SLOTS, SEQ, D), 1.0, 6.0, ((1, 32),))
    seg_ids = jax.vmap(lambda own: jnp.searchsorted(jnp.cumsum(ragged_sizes(own, NSEG, SEQ, SEQ // 2, 0)), jnp.arange(SEQ), side="right"))(jax.random.split(key_of[2], MB * SLOTS)).reshape((MB, SLOTS, SEQ)).astype(jnp.int32)
    pad_mask = draw_pad_mask(jax.random.fold_in(key_of[14], 71), 0)
    qkv_weight = draw_qkv_weight(jax.random.fold_in(key_of[14], 71), 0)
    out_weight = scatter_about(key_of[5], (D, D), D ** -0.5, 0.1875, ((0, 2), (1, 16)))
    in_weight = scatter_about(key_of[6], (D, FF), D ** -0.5, 0.1875, ((0, 2), (1, 16)))
    down_weight = scatter_about(key_of[7], (FF, D), D ** -0.5, 0.1875, ((0, 2), (1, 16)))
    biases = draw_biases(jax.random.fold_in(key_of[14], 71), 0)
    moment_first = draw_moment_first(jax.random.fold_in(key_of[14], 71), 0)
    moment_second = draw_moment_second(jax.random.fold_in(key_of[14], 71), 0)
    basis_left = draw_basis_left(jax.random.fold_in(key_of[14], 71), 0)
    basis_right = draw_basis_right(jax.random.fold_in(key_of[14], 71), 0)
    owners = draw_owners(jax.random.fold_in(key_of[14], 71), 0)
    return dict(acts=acts, cotangent=cotangent, seg_ids=seg_ids, pad_mask=pad_mask, qkv_weight=qkv_weight, out_weight=out_weight, in_weight=in_weight, down_weight=down_weight, biases=biases, moment_first=moment_first, moment_second=moment_second, basis_left=basis_left, basis_right=basis_right, owners=owners)


@jax.custom_vjp
def low(v):
    return lax.optimization_barrier(v.astype(jnp.bfloat16)).astype(jnp.float32)

@jax.custom_vjp
def low_back(v):
    return v

def low_keep(v):
    return (low(v), None)

def low_pass(kept, grad):
    return (grad,)

def back_keep(v):
    return (v, None)

def back_low(kept, grad):
    return (low(grad),)
low.defvjp(low_keep, low_pass)
low_back.defvjp(back_keep, back_low)
norm_eps = 1e-12
precise = lax.Precision.HIGHEST
decay_first = 0.5
decay_second = 0.5
adam_eps = 1e-08
step_rate = 0.4

def layer_norm(values, norm_gain, norm_shift):
    centre = values - lax.optimization_barrier(jnp.mean(values, axis=-1, keepdims=True))
    spread = lax.optimization_barrier(jnp.mean(centre * centre, axis=-1, keepdims=True))
    return centre * lax.rsqrt(spread + norm_eps) * norm_gain + norm_shift

def gelu_exact(values):
    return 0.5 * values * (1.0 + jax.scipy.special.erf(values * (1.0 / math.sqrt(2.0))))

def allowed_pairs(segment, padding):
    same_doc = segment[:, None] == segment[None, :]
    pad_query = padding[:, None] == 0
    real_key = padding[None, :] == 1
    return real_key & (same_doc | pad_query)

def attend_slot(operands):
    queries, keys_all, values, segment, padding = operands
    scores = low_back(jnp.einsum('qhd,khd->hqk', queries, keys_all, precision=precise) * HD ** (-0.5))
    masked = jnp.where(allowed_pairs(segment, padding)[None], scores, -1e+30)
    attn_probs = low(jax.nn.softmax(masked, axis=-1))
    return jnp.einsum('hqk,khd->qhd', attn_probs, values, precision=precise)

def forward(inputs, bias_vec, qkv_weight, out_weight, in_weight, down_weight, segments, padding):
    group_size = inputs.shape[0]
    token_rows = inputs.reshape(group_size * SEQ, D)
    query_bias = bias_vec[0:D]
    value_bias = bias_vec[D:2 * D]
    out_bias = bias_vec[2 * D:3 * D]
    up_bias = bias_vec[3 * D:3 * D + FF]
    down_bias = bias_vec[3 * D + FF:4 * D + FF]
    gain_one = bias_vec[4 * D + FF:5 * D + FF]
    shift_one = bias_vec[5 * D + FF:6 * D + FF]
    gain_two = bias_vec[6 * D + FF:7 * D + FF]
    shift_two = bias_vec[7 * D + FF:8 * D + FF]
    qkv_bias = jnp.concatenate([query_bias, jnp.zeros_like(query_bias), value_bias])
    projected = low_back(low(jnp.dot(token_rows, qkv_weight, precision=precise) + qkv_bias))
    projected = projected.reshape(group_size, SEQ, 3, H, HD)
    context = lax.map(jax.checkpoint(attend_slot), (projected[:, :, 0], projected[:, :, 1], projected[:, :, 2], segments, padding))
    context = low_back(low(context.reshape(group_size * SEQ, D)))
    branch = low_back(jnp.dot(context, out_weight, precision=precise) + out_bias)
    hidden = layer_norm(token_rows + branch, gain_one, shift_one)
    upward = low_back(jnp.dot(low(hidden), in_weight, precision=precise) + up_bias)
    activated = low(gelu_exact(upward))
    feedback = low_back(jnp.dot(activated, down_weight, precision=precise) + down_bias)
    result = layer_norm(hidden + feedback, gain_two, shift_two)
    return result.reshape(group_size, SEQ, D)

def placement_table(owners):
    index_b = jnp.arange(NBLK, dtype=jnp.int32)
    same_owner = owners[:, None] == owners[None, :]
    earlier = index_b[None, :] < index_b[:, None]
    rank_of = lax.optimization_barrier(jnp.sum((same_owner & earlier).astype(jnp.int32), axis=1))
    owner_hit = owners[None, None, :] == jnp.arange(NOWN, dtype=jnp.int32)[:, None, None]
    slot_hit = rank_of[None, None, :] == jnp.arange(CAP, dtype=jnp.int32)[None, :, None]
    return (owner_hit & slot_hit).astype(jnp.float32)

def adam_rotated(grad_slots, value_slots, first_old, second_old, left_basis, right_basis, filled):
    turned = jnp.einsum('fcki,fckj->fcij', left_basis, grad_slots, precision=precise)
    turned = jnp.einsum('fcik,fckj->fcij', turned, right_basis, precision=precise)
    first_raw = decay_first * first_old + (1.0 - decay_first) * turned
    second_raw = decay_second * second_old + (1.0 - decay_second) * turned * turned
    normed_step = first_raw / (1.0 - decay_first ** STEP) / (jnp.sqrt(second_raw / (1.0 - decay_second ** STEP)) + adam_eps)
    restored = jnp.einsum('fcik,fckj->fcij', left_basis, normed_step, precision=precise)
    restored = jnp.einsum('fcik,fcjk->fcij', restored, right_basis, precision=precise)
    value_new = value_slots - step_rate * restored
    return (first_raw * filled, second_raw * filled, value_new * filled)

def reference(acts, cotangent, seg_ids, pad_mask, qkv_weight, out_weight, in_weight, down_weight, biases, moment_first, moment_second, basis_left, basis_right, owners):
    qkv_full = qkv_weight.astype(jnp.float32)
    out_full = out_weight.astype(jnp.float32)
    in_full = in_weight.astype(jnp.float32)
    down_full = down_weight.astype(jnp.float32)
    count_groups = MB * SLOTS // 8
    stacked = (acts.reshape(count_groups, 8, SEQ, D), cotangent.reshape(count_groups, 8, SEQ, D), seg_ids.reshape(count_groups, 8, SEQ), pad_mask.reshape(count_groups, 8, SEQ))

    def group_step(grad_total, operands):
        inputs, upstream, segments, padding = operands

        def layer_fn(bias_vec, token_in):
            return forward(token_in, bias_vec, qkv_full, out_full, in_full, down_full, segments, padding)
        result, pullback = jax.vjp(layer_fn, biases, inputs.astype(jnp.float32))
        bias_part, input_grad = pullback(upstream.astype(jnp.float32))
        return (grad_total + bias_part, (result.astype(jnp.bfloat16), input_grad.astype(jnp.bfloat16)))
    grad_total, (outputs, input_grads) = lax.scan(group_step, jnp.zeros((PCOUNT,), jnp.float32), stacked)
    slot_table = placement_table(owners)
    grad_slots = jnp.einsum('fcb,bij->fcij', slot_table, grad_total.reshape(NBLK, BS, BS), precision=precise)
    value_slots = jnp.einsum('fcb,bij->fcij', slot_table, biases.reshape(NBLK, BS, BS), precision=precise)
    filled = lax.optimization_barrier(jnp.sum(slot_table, axis=2))[:, :, None, None]
    first_new, second_new, value_new = adam_rotated(grad_slots, value_slots, moment_first, moment_second, basis_left, basis_right, filled)
    bias_new = jnp.einsum('fcb,fcij->bij', slot_table, value_new, precision=precise).reshape(PCOUNT)
    return (outputs.reshape(MB, SLOTS, SEQ, D), input_grads.reshape(MB, SLOTS, SEQ, D), grad_total, first_new, second_new, bias_new, bias_new.astype(jnp.bfloat16))
```

```python
import functools
import math

import jax
import jax.numpy as jnp
from jax import lax
from jax.experimental import pallas as pl
from jax.experimental.pallas import tpu as pltpu
from jax.sharding import PartitionSpec as P

D = 1024
H = 16
HD = 64
FF = 4096
SEQ = 512
MB = 2
STEP = 5


norm_eps = 1e-12
precise = lax.Precision.HIGHEST
decay_first = 0.5
decay_second = 0.5
adam_eps = 1e-08
step_rate = 0.4


MESH=pl.DeviceIdType.MESH
NZ=4

def split_rows(R,L,a,b,unit=16):
    out=[];r=0
    for kind,n in (("A1",a),("A2",a),("B1",b),("B2",b)):
        if n: out.append((kind,r,n,0,L)); r+=n
    assert r==R,(r,R)
    return out
def split_lanes(R,L,a,b):
    out=[];l=0
    for kind,n in (("A1",a),("A2",a),("B1",b),("B2",b)):
        if n: out.append((kind,0,R,l,n)); l+=n
    assert l==L
    return out

def children(kind,dz,rx,ry):
    out=[]
    if kind[0]=="A":
        if rx==0 and ry==0:
            if dz>=0: out.append(("zp",(dz+1,0,0)))
            if dz<=0: out.append(("zm",(dz-1,0,0)))
            out.append(("x",(dz,1,0))); out.append(("y",(dz,0,1)))
        if kind=="A1" and (rx,ry)==(1,0): out.append(("y",(dz,1,1)))
        if kind=="A2" and (rx,ry)==(0,1): out.append(("x",(dz,1,1)))
    else:
        if dz==0:
            if (rx,ry)==(0,0): out += [("x",(0,1,0)),("y",(0,0,1))]
            if kind=="B1" and (rx,ry)==(1,0): out.append(("y",(0,1,1)))
            if kind=="B2" and (rx,ry)==(0,1): out.append(("x",(0,1,1)))
        if dz>=0: out.append(("zp",(dz+1,rx,ry)))
        if dz<=0: out.append(("zm",(dz-1,rx,ry)))
    return [(d,c) for d,c in out if abs(c[0])<=NZ-1]

def rel_index(dz,rx,ry): return (dz+3)*4+rx*2+ry
EVENTS=[(dz,rx,ry) for dz in range(-3,4) for rx in (0,1) for ry in (0,1) if (dz,rx,ry)!=(0,0,0)]
EVENTS.sort(key=lambda e:(abs(e[0])+e[1]+e[2], e[1]+e[2], -e[0]))

def region(total, N, K):
    for lanes in range(128,K+1,128):
        if total%lanes==0:
            rows=total//lanes
            if rows%16==0 and rows<=N: return rows,lanes
    raise ValueError((total,N,K))

class Gather:
    def __init__(self, mats, shards, fulls, local_sem, send_sem, recv_sem, sib_sem):
        self.mats=mats; self.sh=shards; self.full=fulls
        self.lsem,self.ssem,self.rsem,self.bsem=local_sem,send_sem,recv_sem,sib_sem
        dp=lax.axis_index("dp"); x=lax.axis_index("fsdp")
        self.dp,self.x=dp,x
        self.z=dp//4; self.y=(dp//2)%2; self.c=dp%2
        self.dev={"x":(dp,1-x),"y":(self.z*4+(1-self.y)*2+self.c,x),"zp":(dp+4,x),"zm":(dp-4,x),"s":(self.z*4+self.y*2+1-self.c,x)}
    def barrier(self):
        bar=pltpu.get_barrier_semaphore()
        for d in ("x","y","s"):
            pl.semaphore_signal(bar,inc=1,device_id=self.dev[d],device_id_type=MESH)
        @pl.when(self.z<NZ-1)
        def _(): pl.semaphore_signal(bar,inc=1,device_id=self.dev["zp"],device_id_type=MESH)
        @pl.when(self.z>0)
        def _(): pl.semaphore_signal(bar,inc=1,device_id=self.dev["zm"],device_id_type=MESH)
        inner=(self.z>0)&(self.z<NZ-1)
        @pl.when(inner)
        def _(): pl.semaphore_wait(bar,5)
        @pl.when(jnp.logical_not(inner))
        def _(): pl.semaphore_wait(bar,4)
    def place(self,m,k,dz,rx,ry):
        M=self.mats[m]; kind,r0,nr,l0,nl=M["classes"][k]
        y=self.y if not ry else 1-self.y
        x=self.x if not rx else 1-self.x
        src=(self.z-dz)*4+y*2+self.c
        return self.full[m].at[pl.ds(pl.multiple_of(src*M["R"]+r0,16),nr), pl.ds(pl.multiple_of(x*M["L"]+l0,128),nl)]
    def forward(self,m,k,rel,src,extra=True):
        M=self.mats[m]; kind=M["classes"][k][0]
        dst=self.place(m,k,*rel)
        for d,ch in children(kind,*rel):
            def go(d=d,ch=ch):
                pltpu.make_async_remote_copy(src,dst,self.ssem.at[m,["x","y","zp","zm","s"].index(d)],self.rsem.at[m,k,rel_index(*ch)],
                    device_id=self.dev[d],device_id_type=MESH).start()
            if d=="zp": pl.when(self.z<NZ-1)(go)
            elif d=="zm": pl.when(self.z>0)(go)
            else: go()
        pltpu.make_async_remote_copy(src,dst,self.ssem.at[m,4],self.bsem.at[m],device_id=self.dev["s"],device_id_type=MESH).start()
    def own(self,m):
        M=self.mats[m]
        for k,(kind,r0,nr,l0,nl) in enumerate(M["classes"]):
            self.forward(m,k,(0,0,0),self.sh[m].at[pl.ds(r0,nr),pl.ds(l0,nl)])
        full=self.full[m].at[pl.ds(pl.multiple_of(self.dp*M["R"],16),M["R"]),pl.ds(pl.multiple_of(self.x*M["L"],128),M["L"])]
        pltpu.make_async_copy(self.sh[m],full,self.lsem.at[m]).start()
    def events(self,m):
        out=[]
        for rel in EVENTS:
            for k in range(len(self.mats[m]["classes"])):
                out.append(functools.partial(self.event,m,k,rel))
        return out
    def event(self,m,k,rel):
        def go():
            ref=self.place(m,k,*rel)
            pltpu.make_async_copy(ref,ref,self.rsem.at[m,k,rel_index(*rel)]).wait()
            self.forward(m,k,rel,ref)
        dz=rel[0]
        if dz>0: pl.when(self.z>=dz)(go)
        elif dz<0: pl.when(self.z<=NZ-1+dz)(go)
        else: go()
    def wait_bytes(self,m,total,sem):
        N,K=self.full[m].shape
        r,l=region(total,N,K)
        ref=self.full[m].at[pl.ds(0,r),pl.ds(0,l)]
        pltpu.make_async_copy(ref,ref,sem).wait()
    def finish_recv(self,m):
        M=self.mats[m]
        own=self.sh[m]
        pltpu.make_async_copy(own,own,self.lsem.at[m]).wait()
        N,K=self.full[m].shape
        self.wait_bytes(m,N*K//2,self.bsem.at[m])
    def finish_send(self,m):
        M=self.mats[m]; N,K=self.full[m].shape
        def total(d,z):
            t=0
            for kind,r0,nr,l0,nl in M["classes"]:
                for rel in [(0,0,0)]+EVENTS:
                    if not 0<=z-rel[0]<=NZ-1: continue
                    for dd,ch in children(kind,*rel):
                        if dd==d and not (d=="zp" and z==NZ-1) and not (d=="zm" and z==0): t+=nr*nl
            return t
        for i,d in enumerate(("x","y")):
            self.wait_bytes(m,total(d,0),self.ssem.at[m,i]); assert total(d,0)==total(d,2)
        for i,d in ((2,"zp"),(3,"zm")):
            for z in range(NZ):
                if total(d,z):
                    pl.when(self.z==z)(functools.partial(self.wait_bytes,m,total(d,z),self.ssem.at[m,i]))
        self.wait_bytes(m,N*K//2,self.ssem.at[m,4])

def plain(mats,*refs):
    n=len(mats)
    sh=refs[:n]; full=refs[n:2*n]; sems=refs[2*n:]
    g=Gather(mats,sh,full,*sems)
    g.barrier()
    g.own(0)
    for m in range(n):
        ev=g.events(m)
        for i,e in enumerate(ev):
            if i==len(ev)//2 and m+1<n: g.own(m+1)
            e()
    for m in range(n):
        g.finish_recv(m); g.finish_send(m)

def gather_call(mats,shards,cid):
    n=len(mats)
    outs=[jax.ShapeDtypeStruct((s.shape[0]*16,s.shape[1]*2),jnp.bfloat16) for s in shards]
    return pl.pallas_call(functools.partial(plain,mats),out_shape=outs,
        in_specs=[pl.BlockSpec(memory_space=pl.ANY)]*n,out_specs=[pl.BlockSpec(memory_space=pl.ANY)]*n,
        scratch_shapes=[pltpu.SemaphoreType.DMA((n,)),pltpu.SemaphoreType.DMA((n,5)),pltpu.SemaphoreType.DMA((n,4,28)),pltpu.SemaphoreType.DMA((n,))],
        compiler_params=pltpu.CompilerParams(collective_id=cid,has_side_effects=True,vmem_limit_bytes=60<<20))(*shards)

def matdesc(beta=True):
    if beta:
        return [dict(R=192,L=512,classes=split_rows(192,512,80,16)),dict(R=64,L=512,classes=split_rows(64,512,32,0)),
            dict(R=256,L=512,classes=split_rows(256,512,96,32)),dict(R=64,L=2048,classes=split_lanes(64,2048,768,256))]
    return [dict(R=192,L=512,classes=split_rows(192,512,96,0)),dict(R=64,L=512,classes=split_rows(64,512,32,0)),
            dict(R=256,L=512,classes=split_rows(256,512,128,0)),dict(R=64,L=2048,classes=split_lanes(64,2048,1024,0))]


def gather_weights(shards):
    turned = [s.T for s in shards]
    if (lax.axis_size("dp"), lax.axis_size("fsdp")) == (16, 2):
        return gather_call(matdesc(), turned, 1)
    return [
        lax.all_gather(lax.all_gather(t, "fsdp", axis=1, tiled=True), "dp", axis=0, tiled=True)
        for t in turned
    ]


def split_biases(bias_vec):
    return (
        bias_vec[0:D],
        bias_vec[D : 2 * D],
        bias_vec[2 * D : 3 * D],
        bias_vec[3 * D : 3 * D + FF],
        bias_vec[3 * D + FF : 4 * D + FF],
        bias_vec[4 * D + FF : 5 * D + FF],
        bias_vec[5 * D + FF : 6 * D + FF],
        bias_vec[6 * D + FF : 7 * D + FF],
        bias_vec[7 * D + FF : 8 * D + FF],
    )


def layer_norm_parts(values, norm_gain, norm_shift):
    centre = values - jnp.mean(values, axis=-1, keepdims=True)
    spread = jnp.mean(centre * centre, axis=-1, keepdims=True)
    inverse = lax.rsqrt(spread + norm_eps)
    normed = centre * inverse
    return (normed * norm_gain + norm_shift, normed, inverse)


def layer_norm_back(upstream, normed, inverse, norm_gain):
    gain_grad = jnp.sum(upstream * normed, axis=0)
    shift_grad = jnp.sum(upstream, axis=0)
    scaled = upstream * norm_gain
    inner_term = (
        scaled
        - jnp.mean(scaled, axis=-1, keepdims=True)
        - normed * jnp.mean(scaled * normed, axis=-1, keepdims=True)
    )
    return (inverse * inner_term, gain_grad, shift_grad)


def gelu_exact(values):
    return 0.5 * values * (1.0 + jax.scipy.special.erf(values * (1.0 / math.sqrt(2.0))))


def gelu_slope(values):
    return 0.5 * (1.0 + jax.scipy.special.erf(values * (1.0 / math.sqrt(2.0)))) + values * jnp.exp(
        -0.5 * values * values
    ) * (1.0 / math.sqrt(2.0 * math.pi))


def allowed_pairs(segment, padding):
    same_doc = segment[:, None] == segment[None, :]
    pad_query = padding[:, None] == 0
    real_key = padding[None, :] == 1
    return real_key & (same_doc | pad_query)


def slot_scores(queries, keys_all, segment, padding):
    raw_scores = jnp.einsum(
        "qhd,khd->hqk", queries, keys_all, preferred_element_type=jnp.float32
    ) * HD ** (-0.5)
    return jnp.where(allowed_pairs(segment, padding)[None], raw_scores, -1e30)


def attend_forward(operands):
    queries, keys_all, values, segment, padding = operands
    masked = slot_scores(queries, keys_all, segment, padding)
    row_peak = jnp.max(masked, axis=-1, keepdims=True)
    exponent = jnp.exp(masked - row_peak)
    row_total = jnp.sum(exponent, axis=-1, keepdims=True)
    attn_probs = (exponent / row_total).astype(jnp.bfloat16)
    context = jnp.einsum("hqk,khd->qhd", attn_probs, values, preferred_element_type=jnp.float32)
    return (context, row_peak[..., 0] + jnp.log(row_total[..., 0]))


def attend_backward(operands):
    queries, keys_all, values, segment, padding, log_total, grad_ctx = operands
    masked = slot_scores(queries, keys_all, segment, padding)
    attn_probs = jnp.exp(masked - log_total[..., None])
    probs_low = attn_probs.astype(jnp.bfloat16)
    grad_probs = jnp.einsum("qhd,khd->hqk", grad_ctx, values, preferred_element_type=jnp.float32)
    row_inner = jnp.sum(grad_probs * attn_probs, axis=-1, keepdims=True)
    grad_scores = (attn_probs * (grad_probs - row_inner)).astype(jnp.bfloat16)
    grad_query = jnp.einsum(
        "hqk,khd->qhd", grad_scores, keys_all, preferred_element_type=jnp.float32
    ) * HD ** (-0.5)
    grad_key = jnp.einsum(
        "hqk,qhd->khd", grad_scores, queries, preferred_element_type=jnp.float32
    ) * HD ** (-0.5)
    grad_value = jnp.einsum("hqk,qhd->khd", probs_low, grad_ctx, preferred_element_type=jnp.float32)
    return jnp.stack([grad_query, grad_key, grad_value], axis=1)


def layer_forward(inputs, segments, padding, attn_weights, feed_weights, biases):
    qkv_weight, out_weight = attn_weights
    in_weight, down_weight = feed_weights
    (
        query_bias,
        value_bias,
        out_bias,
        up_bias,
        down_bias,
        gain_one,
        shift_one,
        gain_two,
        shift_two,
    ) = split_biases(biases)
    slot_count = inputs.shape[0]
    token_rows = inputs.reshape(slot_count * SEQ, D)
    qkv_bias = jnp.concatenate([query_bias, jnp.zeros_like(query_bias), value_bias])
    projected = (
        jnp.dot(token_rows, qkv_weight, preferred_element_type=jnp.float32) + qkv_bias
    ).astype(jnp.bfloat16)
    shaped = projected.reshape(slot_count, SEQ, 3, H, HD)
    context, log_total = lax.map(
        attend_forward, (shaped[:, :, 0], shaped[:, :, 1], shaped[:, :, 2], segments, padding)
    )
    context_low = context.reshape(slot_count * SEQ, D).astype(jnp.bfloat16)
    branch = jnp.dot(context_low, out_weight, preferred_element_type=jnp.float32) + out_bias
    hidden, normed_one, inverse_one = layer_norm_parts(
        token_rows.astype(jnp.float32) + branch, gain_one, shift_one
    )
    hidden_low = hidden.astype(jnp.bfloat16)
    upward = jnp.dot(hidden_low, in_weight, preferred_element_type=jnp.float32) + up_bias
    activated = gelu_exact(upward).astype(jnp.bfloat16)
    feedback = jnp.dot(activated, down_weight, preferred_element_type=jnp.float32) + down_bias
    result, normed_two, inverse_two = layer_norm_parts(hidden + feedback, gain_two, shift_two)
    kept_state = (shaped, log_total, normed_one, inverse_one, upward, normed_two, inverse_two)
    return (result.reshape(slot_count, SEQ, D), kept_state)


def layer_backward(upstream, kept_state, segments, padding, attn_weights, feed_weights, biases):
    qkv_weight, out_weight = attn_weights
    in_weight, down_weight = feed_weights
    (
        query_bias,
        value_bias,
        out_bias,
        up_bias,
        down_bias,
        gain_one,
        shift_one,
        gain_two,
        shift_two,
    ) = split_biases(biases)
    shaped, log_total, normed_one, inverse_one, upward, normed_two, inverse_two = kept_state
    slot_count = upstream.shape[0]
    grad_rows = upstream.reshape(slot_count * SEQ, D).astype(jnp.float32)
    grad_pre_two, grad_gain_two, grad_shift_two = layer_norm_back(
        grad_rows, normed_two, inverse_two, gain_two
    )
    grad_feed = grad_pre_two.astype(jnp.bfloat16)
    grad_down_bias = jnp.sum(grad_feed.astype(jnp.float32), axis=0)
    grad_act = jnp.einsum("rd,fd->rf", grad_feed, down_weight, preferred_element_type=jnp.float32)
    grad_up = (grad_act * gelu_slope(upward)).astype(jnp.bfloat16)
    grad_up_bias = jnp.sum(grad_up.astype(jnp.float32), axis=0)
    grad_hidden = grad_pre_two + jnp.einsum(
        "rf,df->rd", grad_up, in_weight, preferred_element_type=jnp.float32
    )
    grad_pre_one, grad_gain_one, grad_shift_one = layer_norm_back(
        grad_hidden, normed_one, inverse_one, gain_one
    )
    grad_branch = grad_pre_one.astype(jnp.bfloat16)
    grad_out_bias = jnp.sum(grad_branch.astype(jnp.float32), axis=0)
    grad_context = jnp.einsum(
        "rd,ed->re", grad_branch, out_weight, preferred_element_type=jnp.float32
    ).astype(jnp.bfloat16)
    grad_context = grad_context.reshape(slot_count, SEQ, H, HD)
    grad_qkv = lax.map(
        attend_backward,
        (
            shaped[:, :, 0],
            shaped[:, :, 1],
            shaped[:, :, 2],
            segments,
            padding,
            log_total,
            grad_context,
        ),
    )
    grad_qkv_low = grad_qkv.reshape(slot_count * SEQ, 3 * D).astype(jnp.bfloat16)
    qkv_bias_grad = jnp.sum(grad_qkv_low.astype(jnp.float32), axis=0)
    grad_inputs = grad_pre_one + jnp.einsum(
        "re,de->rd", grad_qkv_low, qkv_weight, preferred_element_type=jnp.float32
    )
    bias_part = jnp.concatenate(
        [
            qkv_bias_grad[0:D],
            qkv_bias_grad[2 * D : 3 * D],
            grad_out_bias,
            grad_up_bias,
            grad_down_bias,
            grad_gain_one,
            grad_shift_one,
            grad_gain_two,
            grad_shift_two,
        ]
    )
    return (grad_inputs.astype(jnp.bfloat16).reshape(slot_count, SEQ, D), bias_part)


def placement_table(owners, owner_count, capacity):
    block_count = owners.shape[0]
    index_b = jnp.arange(block_count, dtype=jnp.int32)
    same_owner = owners[:, None] == owners[None, :]
    earlier = index_b[None, :] < index_b[:, None]
    rank_of = jnp.sum((same_owner & earlier).astype(jnp.int32), axis=1)
    owner_hit = owners[None, None, :] == jnp.arange(owner_count, dtype=jnp.int32)[:, None, None]
    slot_hit = rank_of[None, None, :] == jnp.arange(capacity, dtype=jnp.int32)[None, :, None]
    return (owner_hit & slot_hit).astype(jnp.float32)


def adam_rotated(grad_slots, value_slots, first_old, second_old, left_basis, right_basis, filled):
    turned = jnp.einsum("fcki,fckj->fcij", left_basis, grad_slots, precision=precise)
    turned = jnp.einsum("fcik,fckj->fcij", turned, right_basis, precision=precise)
    first_raw = decay_first * first_old + (1.0 - decay_first) * turned
    second_raw = decay_second * second_old + (1.0 - decay_second) * turned * turned
    normed_step = (
        first_raw
        / (1.0 - decay_first**STEP)
        / (jnp.sqrt(second_raw / (1.0 - decay_second**STEP)) + adam_eps)
    )
    restored = jnp.einsum("fcik,fckj->fcij", left_basis, normed_step, precision=precise)
    restored = jnp.einsum("fcik,fcjk->fcij", restored, right_basis, precision=precise)
    value_new = value_slots - step_rate * restored
    return (first_raw * filled, second_raw * filled, value_new * filled)


def body(
    acts,
    cotangent,
    seg_ids,
    pad_mask,
    qkv_weight,
    out_weight,
    in_weight,
    down_weight,
    biases,
    moment_first,
    moment_second,
    basis_left,
    basis_right,
    owners,
):
    full = gather_weights((qkv_weight, out_weight, in_weight, down_weight))
    attn_now = (full[0].T, full[1].T)
    feed_now = (full[2].T, full[3].T)
    slots = acts.shape[0] * acts.shape[1]
    segs = seg_ids.reshape(slots, SEQ)
    pads = pad_mask.reshape(slots, SEQ)
    result, kept_state = layer_forward(
        acts.reshape(slots, SEQ, D), segs, pads, attn_now, feed_now, biases
    )
    grad_inputs, grad_total = layer_backward(
        cotangent.reshape(slots, SEQ, D), kept_state, segs, pads, attn_now, feed_now, biases
    )
    outputs = result.astype(jnp.bfloat16).reshape(acts.shape)
    input_grads = grad_inputs.reshape(acts.shape)
    block_count = owners.shape[0]
    block_side = moment_first.shape[2]
    slot_table = placement_table(owners, lax.axis_size("fsdp"), moment_first.shape[1])
    grad_slots = jnp.einsum(
        "fcb,bij->fcij",
        slot_table,
        grad_total.reshape(block_count, block_side, block_side),
        precision=precise,
    )
    summed = lax.psum(grad_slots.astype(jnp.bfloat16), "dp")
    owned_grad = lax.psum_scatter(summed, "fsdp", scatter_dimension=0, tiled=True).astype(
        jnp.float32
    )
    own_table = lax.dynamic_slice_in_dim(slot_table, lax.axis_index("fsdp"), 1, 0)
    value_slots = jnp.einsum(
        "fcb,bij->fcij",
        own_table,
        biases.reshape(block_count, block_side, block_side),
        precision=precise,
    )
    filled = jnp.sum(own_table, axis=2)[:, :, None, None]
    first_new, second_new, value_new = adam_rotated(
        owned_grad, value_slots, moment_first, moment_second, basis_left, basis_right, filled
    )
    shared_grad, shared_value = (
        lax.all_gather(owned_grad, "fsdp", axis=0, tiled=True),
        lax.all_gather(value_new, "fsdp", axis=0, tiled=True),
    )
    bias_grad = jnp.einsum("fcb,fcij->bij", slot_table, shared_grad, precision=precise).reshape(
        biases.shape[0]
    )
    bias_new = jnp.einsum("fcb,fcij->bij", slot_table, shared_value, precision=precise).reshape(
        biases.shape[0]
    )
    return (
        outputs,
        input_grads,
        bias_grad,
        first_new,
        second_new,
        bias_new,
        bias_new.astype(jnp.bfloat16),
    )


def solution(mesh):
    placed = (
        P(None, ("dp", "fsdp"), None, None),
        P(None, ("dp", "fsdp"), None, None),
        P(None, ("dp", "fsdp"), None),
        P(None, ("dp", "fsdp"), None),
        P("fsdp", "dp"),
        P("fsdp", "dp"),
        P("fsdp", "dp"),
        P("fsdp", "dp"),
        P(),
        P("fsdp", None, None, None),
        P("fsdp", None, None, None),
        P("fsdp", None, None, None),
        P("fsdp", None, None, None),
        P(),
    )
    return jax.shard_map(
        body,
        mesh=mesh,
        in_specs=placed,
        out_specs=(
            P(None, ("dp", "fsdp"), None, None),
            P(None, ("dp", "fsdp"), None, None),
            P(),
            P("fsdp", None, None, None),
            P("fsdp", None, None, None),
            P(),
            P(),
        ),
        check_vma=False,
    )
```

```python
import functools
import math

import jax
import jax.numpy as jnp
from jax import lax
from jax.experimental import pallas as pl
from jax.experimental.pallas import tpu as pltpu
from jax.sharding import PartitionSpec as P

STEP = 5
precise = lax.Precision.HIGHEST
decay_first = 0.5
decay_second = 0.5
adam_eps = 1e-08
step_rate = 0.4

MESH=pl.DeviceIdType.MESH
NZ=4

def split_rows(R,L,a,b,unit=16):
    out=[];r=0
    for kind,n in (("A1",a),("A2",a),("B1",b),("B2",b)):
        if n: out.append((kind,r,n,0,L)); r+=n
    assert r==R,(r,R)
    return out
def split_lanes(R,L,a,b):
    out=[];l=0
    for kind,n in (("A1",a),("A2",a),("B1",b),("B2",b)):
        if n: out.append((kind,0,R,l,n)); l+=n
    assert l==L
    return out

def children(kind,dz,rx,ry):
    out=[]
    if kind[0]=="A":
        if rx==0 and ry==0:
            if dz>=0: out.append(("zp",(dz+1,0,0)))
            if dz<=0: out.append(("zm",(dz-1,0,0)))
            out.append(("x",(dz,1,0))); out.append(("y",(dz,0,1)))
        if kind=="A1" and (rx,ry)==(1,0): out.append(("y",(dz,1,1)))
        if kind=="A2" and (rx,ry)==(0,1): out.append(("x",(dz,1,1)))
    else:
        if dz==0:
            if (rx,ry)==(0,0): out += [("x",(0,1,0)),("y",(0,0,1))]
            if kind=="B1" and (rx,ry)==(1,0): out.append(("y",(0,1,1)))
            if kind=="B2" and (rx,ry)==(0,1): out.append(("x",(0,1,1)))
        if dz>=0: out.append(("zp",(dz+1,rx,ry)))
        if dz<=0: out.append(("zm",(dz-1,rx,ry)))
    return [(d,c) for d,c in out if abs(c[0])<=NZ-1]

def rel_index(dz,rx,ry): return (dz+3)*4+rx*2+ry
EVENTS=[(dz,rx,ry) for dz in range(-3,4) for rx in (0,1) for ry in (0,1) if (dz,rx,ry)!=(0,0,0)]
EVENTS.sort(key=lambda e:(abs(e[0])+e[1]+e[2], e[1]+e[2], -e[0]))

def region(total, N, K):
    for lanes in range(128,K+1,128):
        if total%lanes==0:
            rows=total//lanes
            if rows%16==0 and rows<=N: return rows,lanes
    raise ValueError((total,N,K))

class Gather:
    def __init__(self, mats, shards, fulls, local_sem, send_sem, recv_sem, sib_sem):
        self.mats=mats; self.sh=shards; self.full=fulls
        self.lsem,self.ssem,self.rsem,self.bsem=local_sem,send_sem,recv_sem,sib_sem
        dp=lax.axis_index("dp"); x=lax.axis_index("fsdp")
        self.dp,self.x=dp,x
        self.z=dp//4; self.y=(dp//2)%2; self.c=dp%2
        self.dev={"x":(dp,1-x),"y":(self.z*4+(1-self.y)*2+self.c,x),"zp":(dp+4,x),"zm":(dp-4,x),"s":(self.z*4+self.y*2+1-self.c,x)}
    def barrier(self):
        bar=pltpu.get_barrier_semaphore()
        for d in ("x","y","s"):
            pl.semaphore_signal(bar,inc=1,device_id=self.dev[d],device_id_type=MESH)
        @pl.when(self.z<NZ-1)
        def _(): pl.semaphore_signal(bar,inc=1,device_id=self.dev["zp"],device_id_type=MESH)
        @pl.when(self.z>0)
        def _(): pl.semaphore_signal(bar,inc=1,device_id=self.dev["zm"],device_id_type=MESH)
        inner=(self.z>0)&(self.z<NZ-1)
        @pl.when(inner)
        def _(): pl.semaphore_wait(bar,5)
        @pl.when(jnp.logical_not(inner))
        def _(): pl.semaphore_wait(bar,4)
    def place(self,m,k,dz,rx,ry):
        M=self.mats[m]; kind,r0,nr,l0,nl=M["classes"][k]
        y=self.y if not ry else 1-self.y
        x=self.x if not rx else 1-self.x
        src=(self.z-dz)*4+y*2+self.c
        return self.full[m].at[pl.ds(pl.multiple_of(src*M["R"]+r0,16),nr), pl.ds(pl.multiple_of(x*M["L"]+l0,128),nl)]
    def forward(self,m,k,rel,src,extra=True):
        M=self.mats[m]; kind=M["classes"][k][0]
        dst=self.place(m,k,*rel)
        for d,ch in children(kind,*rel):
            def go(d=d,ch=ch):
                pltpu.make_async_remote_copy(src,dst,self.ssem.at[m,["x","y","zp","zm","s"].index(d)],self.rsem.at[m,k,rel_index(*ch)],
                    device_id=self.dev[d],device_id_type=MESH).start()
            if d=="zp": pl.when(self.z<NZ-1)(go)
            elif d=="zm": pl.when(self.z>0)(go)
            else: go()
        pltpu.make_async_remote_copy(src,dst,self.ssem.at[m,4],self.bsem.at[m],device_id=self.dev["s"],device_id_type=MESH).start()
    def own(self,m):
        M=self.mats[m]
        for k,(kind,r0,nr,l0,nl) in enumerate(M["classes"]):
            self.forward(m,k,(0,0,0),self.sh[m].at[pl.ds(r0,nr),pl.ds(l0,nl)])
        full=self.full[m].at[pl.ds(pl.multiple_of(self.dp*M["R"],16),M["R"]),pl.ds(pl.multiple_of(self.x*M["L"],128),M["L"])]
        pltpu.make_async_copy(self.sh[m],full,self.lsem.at[m]).start()
    def events(self,m):
        out=[]
        for rel in EVENTS:
            for k in range(len(self.mats[m]["classes"])):
                out.append(functools.partial(self.event,m,k,rel))
        return out
    def event(self,m,k,rel):
        def go():
            ref=self.place(m,k,*rel)
            pltpu.make_async_copy(ref,ref,self.rsem.at[m,k,rel_index(*rel)]).wait()
            self.forward(m,k,rel,ref)
        dz=rel[0]
        if dz>0: pl.when(self.z>=dz)(go)
        elif dz<0: pl.when(self.z<=NZ-1+dz)(go)
        else: go()
    def wait_bytes(self,m,total,sem):
        N,K=self.full[m].shape
        r,l=region(total,N,K)
        ref=self.full[m].at[pl.ds(0,r),pl.ds(0,l)]
        pltpu.make_async_copy(ref,ref,sem).wait()
    def finish_recv(self,m):
        M=self.mats[m]
        own=self.sh[m]
        pltpu.make_async_copy(own,own,self.lsem.at[m]).wait()
        N,K=self.full[m].shape
        self.wait_bytes(m,N*K//2,self.bsem.at[m])
    def finish_send(self,m):
        M=self.mats[m]; N,K=self.full[m].shape
        def total(d,z):
            t=0
            for kind,r0,nr,l0,nl in M["classes"]:
                for rel in [(0,0,0)]+EVENTS:
                    if not 0<=z-rel[0]<=NZ-1: continue
                    for dd,ch in children(kind,*rel):
                        if dd==d and not (d=="zp" and z==NZ-1) and not (d=="zm" and z==0): t+=nr*nl
            return t
        for i,d in enumerate(("x","y")):
            self.wait_bytes(m,total(d,0),self.ssem.at[m,i]); assert total(d,0)==total(d,2)
        for i,d in ((2,"zp"),(3,"zm")):
            for z in range(NZ):
                if total(d,z):
                    pl.when(self.z==z)(functools.partial(self.wait_bytes,m,total(d,z),self.ssem.at[m,i]))
        self.wait_bytes(m,N*K//2,self.ssem.at[m,4])

def plain(mats,*refs):
    n=len(mats)
    sh=refs[:n]; full=refs[n:2*n]; sems=refs[2*n:]
    g=Gather(mats,sh,full,*sems)
    g.barrier()
    g.own(0)
    for m in range(n):
        ev=g.events(m)
        for i,e in enumerate(ev):
            if i==len(ev)//2 and m+1<n: g.own(m+1)
            e()
    for m in range(n):
        g.finish_recv(m); g.finish_send(m)

def gather_call(mats,shards,cid):
    n=len(mats)
    outs=[jax.ShapeDtypeStruct((s.shape[0]*16,s.shape[1]*2),jnp.bfloat16) for s in shards]
    return pl.pallas_call(functools.partial(plain,mats),out_shape=outs,
        in_specs=[pl.BlockSpec(memory_space=pl.ANY)]*n,out_specs=[pl.BlockSpec(memory_space=pl.ANY)]*n,
        scratch_shapes=[pltpu.SemaphoreType.DMA((n,)),pltpu.SemaphoreType.DMA((n,5)),pltpu.SemaphoreType.DMA((n,4,28)),pltpu.SemaphoreType.DMA((n,))],
        compiler_params=pltpu.CompilerParams(collective_id=cid,has_side_effects=True,vmem_limit_bytes=60<<20))(*shards)

def matdesc(beta=True):
    if beta:
        return [dict(R=192,L=512,classes=split_rows(192,512,80,16)),dict(R=64,L=512,classes=split_rows(64,512,32,0)),
            dict(R=256,L=512,classes=split_rows(256,512,96,32)),dict(R=64,L=2048,classes=split_lanes(64,2048,768,256))]
    return [dict(R=192,L=512,classes=split_rows(192,512,96,0)),dict(R=64,L=512,classes=split_rows(64,512,32,0)),
            dict(R=256,L=512,classes=split_rows(256,512,128,0)),dict(R=64,L=2048,classes=split_lanes(64,2048,1024,0))]
BF=jnp.bfloat16
F32=jnp.float32
D=1024
H=16
HD=64
FF=4096
SEQ=512
LOG2E=1.4426950408889634
VMEM_CAP=60<<20
ANY=pl.BlockSpec(memory_space=pl.ANY)
VM=pl.BlockSpec(memory_space=pltpu.VMEM)
SDS=jax.ShapeDtypeStruct
DMA=pltpu.SemaphoreType.DMA

def nn(a,b): return lax.dot_general(a,b,(((1,),(0,)),((),())),preferred_element_type=F32)
def nt(a,b): return lax.dot_general(a,b,(((1,),(1,)),((),())),preferred_element_type=F32)
def tn(a,b): return lax.dot_general(a,b,(((0,),(0,)),((),())),preferred_element_type=F32)

OQ,OV,OO,O1,O2,OG1,OC1,OG2,OC2=0,D,2*D,3*D,3*D+FF,4*D+FF,5*D+FF,6*D+FF,7*D+FF

def column(row):
    return jnp.transpose(jnp.broadcast_to(row,(8,row.shape[1])))[:,0:1]

class Quiet:
    def tick(self,n): pass
    def close(self): pass

class Weave:
    def __init__(self,g,n):
        self.g,self.n=g,n
        self.todo=[e for m in range(n) for e in g.events(m)]
        self.total=len(self.todo)
    def tick(self,share):
        k=min(len(self.todo),int(math.ceil(self.total*share)))
        for e in self.todo[:k]: e()
        self.todo=self.todo[k:]
    def close(self):
        for e in self.todo: e()
        self.todo=[]
        for m in range(self.n):
            self.g.finish_recv(m); self.g.finish_send(m)

def start_comm(mats,rest):
    n=len(mats)
    if not n: return Quiet()
    g=Gather(mats,rest[:n],rest[n:2*n],*rest[2*n:2*n+4])
    g.barrier()
    for m in range(n): g.own(m)
    return Weave(g,n)

def comm_scratch(n):
    return [DMA((n,)),DMA((n,5)),DMA((n,4,28)),DMA((n,))] if n else []

def comm_params(mats,cid,**kw):
    if mats: kw.update(collective_id=cid,has_side_effects=True)
    return pltpu.CompilerParams(vmem_limit_bytes=VMEM_CAP,**kw)

def full_shapes(mats,dp,fs):
    return [SDS((M["R"]*dp,M["L"]*fs),BF) for M in mats]

def attn_fwd(mats,shards,cid,x,wqkvT,bias,seg,pad,ndp,nfs):
    n=len(mats); S=x.shape[0]//SEQ; T=x.shape[0]
    def kernel(*refs):
        x_h,w_h,b_ref,seg_ref,pad_ref=refs[:5]
        sh=refs[5:5+n]; o=5+n
        qkv_o,ctxT_o,ctx_o,p_o=refs[o:o+4]
        full=refs[o+4:o+4+n]; o=o+4+n
        x_v,w_v,qkv_v,ctxT_v,ctx_v,mask_v,pb,lsem,osem,psem=refs[o:o+10]
        sems=refs[o+10:]
        weave=start_comm(mats,list(sh)+list(full)+list(sems))
        cx=pltpu.make_async_copy(x_h,x_v,lsem.at[0]); cx.start()
        cw=[]
        for g in range(4):
            for j in range(3):
                r=pl.ds(j*D+g*256,256)
                c=pltpu.make_async_copy(w_h.at[r],w_v.at[r],lsem.at[1+g*3+j]); c.start(); cw.append(c)
        for s in range(S):
            seg_r=seg_ref[s:s+1,:]; pad_r=pad_ref[s:s+1,:]
            key_r=jnp.where(pad_r==1,seg_r,-1).astype(F32)
            key_c=column(key_r)
            hit=(key_c==seg_r.astype(F32))|((pad_r==0)&(key_c>=0.0))
            mask_v[s]=jnp.where(hit,0.0,-1e30)
        cx.wait()
        ocs=[]; pcs=[None,None]
        it=0
        for g in range(4):
            for j in range(3):
                cw[g*3+j].wait()
                r=pl.ds(j*D+g*256,256)
                acc=nt(w_v[r,:],x_v[...])
                if j!=1:
                    o0=(OQ if j==0 else OV)+g*256
                    acc=acc+column(b_ref[0:1,o0:o0+256])
                qkv_v[r,:]=acc.astype(BF)
                c=pltpu.make_async_copy(qkv_v.at[r],qkv_o.at[r],osem.at[len(ocs)]); c.start(); ocs.append(c)
                weave.tick(1/40)
            for s in range(S):
                cols=pl.ds(s*SEQ,SEQ)
                for hp in range(2):
                    b=it%2; it+=1
                    if pcs[b] is not None: pcs[b].wait()
                    def head(i,_):
                        r=pl.multiple_of(g*256+hp*128+i*HD,HD)
                        st=tn(qkv_v[pl.ds(D+r,HD),cols],qkv_v[pl.ds(r,HD),cols])
                        t=st*(0.125*LOG2E)+mask_v[s]
                        e=jnp.exp2(t-jnp.max(t,axis=0,keepdims=True))
                        p=(e*(1.0/jnp.sum(e,axis=0,keepdims=True))).astype(BF)
                        pb[b,i]=p
                        ctxT_v[pl.ds(r,HD),cols]=nn(qkv_v[pl.ds(2*D+r,HD),cols],p).astype(BF)
                        return _
                    lax.fori_loop(0,2,head,0)
                    c=pltpu.make_async_copy(pb.at[b],p_o.at[pl.ds(g*4+hp*2,2),s],psem.at[b]); c.start(); pcs[b]=c
                    weave.tick(1/18)
                rr=pl.ds(g*256,256)
                ctx_v[cols,rr]=jnp.transpose(ctxT_v[rr,cols])
            c=pltpu.make_async_copy(ctxT_v.at[rr],ctxT_o.at[rr],osem.at[len(ocs)]); c.start(); ocs.append(c)
        c=pltpu.make_async_copy(ctx_v,ctx_o,osem.at[len(ocs)]); c.start(); ocs.append(c)
        weave.close()
        for c in ocs+pcs: c.wait()
    out=pl.pallas_call(kernel,
        out_shape=[SDS((3*D,T),BF),SDS((D,T),BF),SDS((T,D),BF),SDS((H,S,SEQ,SEQ),BF)]+full_shapes(mats,ndp,nfs),
        in_specs=[ANY,ANY,VM,VM,VM]+[ANY]*n,out_specs=[ANY]*(4+n),
        scratch_shapes=[pltpu.VMEM((T,D),BF),pltpu.VMEM((3*D,D),BF),pltpu.VMEM((3*D,T),BF),pltpu.VMEM((D,T),BF),pltpu.VMEM((T,D),BF),
            pltpu.VMEM((S,SEQ,SEQ),F32),pltpu.VMEM((2,2,SEQ,SEQ),BF),DMA((13,)),DMA((17,)),DMA((2,))]+comm_scratch(n),
        compiler_params=comm_params(mats,cid),name="attn_fwd")(x,wqkvT,bias,seg,pad,*shards)
    return out[:4],out[4:]

def ln(v):
    c=v-jnp.mean(v,axis=-1,keepdims=True)
    r=lax.rsqrt(jnp.mean(c*c,axis=-1,keepdims=True)+1e-12)
    return c*r,r

def ff_up(mats,shards,cid,x,ctx,woT,wiT,bias,ndp,nfs):
    n=len(mats); T=x.shape[0]; RT=256; NT=T//RT; CH=1024; NC=FF//CH
    def kernel(*refs):
        x_h,ctx_h,wo_h,wi_h,b_ref=refs[:5]
        sh=refs[5:5+n]; o=5+n
        n1_o,r1_o,act_o,slope_o,won_o=refs[o:o+5]
        full=refs[o+5:o+5+n]; o=o+5+n
        x_v,ctx_v,wo_v,wi_v,n1_v,r1_v,hb_v,act_v,slope_v,won_v,lsem,osem=refs[o:o+12]
        sems=refs[o+12:]
        weave=start_comm(mats,list(sh)+list(full)+list(sems))
        loads=[pltpu.make_async_copy(a,b,lsem.at[i]) for i,(a,b) in enumerate(((ctx_h,ctx_v),(wo_h,wo_v),(x_h,x_v)))]
        wl=[pltpu.make_async_copy(wi_h.at[pl.ds(c*CH,CH)],wi_v.at[pl.ds(c*CH,CH)],lsem.at[3+c]) for c in range(NC)]
        for c in loads+wl: c.start()
        for c in loads: c.wait()
        ocs=[]
        def out(a,b):
            c=pltpu.make_async_copy(a,b,osem.at[len(ocs)]); c.start(); ocs.append(c)
        for t in range(NT):
            rows=pl.ds(t*RT,RT)
            br=nt(ctx_v[rows,:],wo_v[...])+b_ref[0:1,OO:OO+D]
            nrm,r=ln(x_v[rows,:].astype(F32)+br)
            n1_v[rows,:]=nrm
            r1_v[rows,:]=jnp.broadcast_to(r,(RT,128))
            hb_v[rows,:]=(nrm*b_ref[0:1,OG1:OG1+D]+b_ref[0:1,OC1:OC1+D]).astype(BF)
            out(n1_v.at[rows],n1_o.at[rows])
            weave.tick(1/44)
        out(r1_v,r1_o)
        for c in range(NC):
            wl[c].wait()
            cc=pl.ds(c*CH,CH)
            for t in range(NT):
                rows=pl.ds(t*RT,RT)
                def sub(i,_):
                    ci=pl.multiple_of(c*CH+i*256,256)
                    u=nt(hb_v[rows,:],wi_v[pl.ds(ci,256),:])+b_ref[0:1,pl.ds(O1+ci,256)]
                    cdf=0.5+0.5*lax.erf(u*(1.0/math.sqrt(2.0)))
                    act_v[rows,pl.ds(ci,256)]=(u*cdf).astype(BF)
                    slope_v[rows,pl.ds(ci,256)]=(cdf+u*(jnp.exp2(u*u*(-0.5*LOG2E))*(1.0/math.sqrt(2.0*math.pi)))).astype(BF)
                    return _
                lax.fori_loop(0,CH//256,sub,0)
                weave.tick(1/18)
            out(act_v.at[:,cc],act_o.at[:,cc]); out(slope_v.at[:,cc],slope_o.at[:,cc])
        won_v[...]=jnp.transpose(wo_v[...])
        out(won_v,won_o)
        weave.close()
        for c in ocs: c.wait()
    out=pl.pallas_call(kernel,
        out_shape=[SDS((T,D),F32),SDS((T,128),F32),SDS((T,FF),BF),SDS((T,FF),BF),SDS((D,D),BF)]+full_shapes(mats,ndp,nfs),
        in_specs=[ANY]*4+[VM]+[ANY]*n,out_specs=[ANY]*(5+n),
        scratch_shapes=[pltpu.VMEM((T,D),BF),pltpu.VMEM((T,D),BF),pltpu.VMEM((D,D),BF),pltpu.VMEM((FF,D),BF),pltpu.VMEM((T,D),F32),pltpu.VMEM((T,128),F32),
            pltpu.VMEM((T,D),BF),pltpu.VMEM((T,FF),BF),pltpu.VMEM((T,FF),BF),pltpu.VMEM((D,D),BF),DMA((7,)),DMA((14,))]+comm_scratch(n),
        compiler_params=comm_params(mats,cid),name="ff_up")(x,ctx,woT,wiT,bias,*shards)
    return out[:5],out[5:]

def ff_back(act,slope,n1,r1,cot,wdT,wiT,won,bias):
    T=act.shape[0]; RT=256; NT=T//RT; CH=1024; NC=FF//CH
    def kernel(act_ref,slope_ref,n1_ref,r1_ref,cot_ref,wd_h,wi_h,wo_h,b_ref, out_ref,dp1_ref,dcT_ref,g_ref, wd_v,wi_v,wo_v,f_v,dfb_v,lsem):
        t=pl.program_id(0)
        ld=[pltpu.make_async_copy(wd_h.at[pl.ds(i*256,256)],wd_v.at[pl.ds(i*256,256)],lsem.at[i]) for i in range(4)]
        lw=[pltpu.make_async_copy(wi_h.at[pl.ds(i*CH,CH)],wi_v.at[pl.ds(i*CH,CH)],lsem.at[4+i]) for i in range(NC)]
        lo=pltpu.make_async_copy(wo_h,wo_v,lsem.at[8])
        @pl.when(t==0)
        def _():
            for c in ld+lw+[lo]: c.start()
            g_ref[...]=jnp.zeros_like(g_ref)
        def row(o,n=D): return b_ref[0:1,o:o+n]
        for i in range(4):
            @pl.when(t==0)
            def _(): ld[i].wait()
            f_v[:,i*256:(i+1)*256]=nt(act_ref[...],wd_v[i*256:(i+1)*256,:])
        nrm1=n1_ref[...]
        h1=nrm1*row(OG1)+row(OC1)
        n2,r2=ln(h1+(f_v[...]+row(O2)))
        out_ref[...]=(n2*row(OG2)+row(OC2)).astype(BF)
        dy=cot_ref[...].astype(F32)
        g_ref[0:1,OG2:OG2+D]+=jnp.sum(dy*n2,axis=0,keepdims=True)
        g_ref[0:1,OC2:OC2+D]+=jnp.sum(dy,axis=0,keepdims=True)
        e=dy*row(OG2)
        dp2=r2*(e-jnp.mean(e,axis=-1,keepdims=True)-n2*jnp.mean(e*n2,axis=-1,keepdims=True))
        dfb=dp2.astype(BF)
        dfb_v[...]=dfb
        g_ref[0:1,O2:O2+D]+=jnp.sum(dfb.astype(F32),axis=0,keepdims=True)
        f_v[...]=dp2
        for c in range(NC):
            @pl.when(t==0)
            def _(): lw[c].wait()
            cc=slice(c*CH,(c+1)*CH)
            du=(nn(dfb_v[...],wd_v[:,cc])*slope_ref[:,cc].astype(F32)).astype(BF)
            g_ref[0:1,O1+c*CH:O1+(c+1)*CH]+=jnp.sum(du.astype(F32),axis=0,keepdims=True)
            f_v[...]+=nn(du,wi_v[cc,:])
        dh1=f_v[...]
        nrm1=n1_ref[...]
        g_ref[0:1,OG1:OG1+D]+=jnp.sum(dh1*nrm1,axis=0,keepdims=True)
        g_ref[0:1,OC1:OC1+D]+=jnp.sum(dh1,axis=0,keepdims=True)
        e=dh1*row(OG1)
        dp1=r1_ref[:,0:1]*(e-jnp.mean(e,axis=-1,keepdims=True)-nrm1*jnp.mean(e*nrm1,axis=-1,keepdims=True))
        dp1_ref[...]=dp1
        da=dp1.astype(BF)
        g_ref[0:1,OO:OO+D]+=jnp.sum(da.astype(F32),axis=0,keepdims=True)
        @pl.when(t==0)
        def _(): lo.wait()
        dcT_ref[...]=nt(wo_v[...],da).astype(BF)
    rb=lambda n: pl.BlockSpec((RT,n),lambda t:(t,0))
    return pl.pallas_call(kernel,grid=(NT,),
        out_shape=[SDS((T,D),BF),SDS((T,D),F32),SDS((D,T),BF),SDS((1,12*D),F32)],
        in_specs=[rb(FF),rb(FF),rb(D),rb(128),rb(D),ANY,ANY,ANY,VM],
        out_specs=[rb(D),rb(D),pl.BlockSpec((D,RT),lambda t:(0,t)),pl.BlockSpec((1,12*D),lambda t:(0,0))],
        scratch_shapes=[pltpu.VMEM((D,FF),BF),pltpu.VMEM((FF,D),BF),pltpu.VMEM((D,D),BF),pltpu.VMEM((RT,D),F32),pltpu.VMEM((RT,D),BF),DMA((9,))],
        compiler_params=pltpu.CompilerParams(vmem_limit_bytes=VMEM_CAP),name="ff_back")(act,slope,n1,r1,cot,wdT,wiT,won,bias)

def attn_back(p,qkvT,ctxT,dcT):
    S=p.shape[1]; T=S*SEQ; G=2; ST=H//G
    def kernel(p_ref,q_ref,k_ref,v_ref,d_ref,c_ref,oq,ok,ov,gq,gv):
        for s in range(S):
            c=slice(SEQ*s,SEQ*s+SEQ)
            for h in range(G):
                r=slice(HD*h,HD*h+HD)
                d=d_ref[r,c]
                pr=p_ref[h,s]
                delta=jnp.sum(d.astype(F32)*c_ref[r,c].astype(F32),axis=0,keepdims=True)
                ds=(pr.astype(F32)*(tn(v_ref[r,c],d)-delta)).astype(BF)
                ov[r,c]=nt(d,pr).astype(BF)
                ok[r,c]=(nt(q_ref[r,c],ds)*0.125).astype(BF)
                oq[r,c]=(nn(k_ref[r,c],ds)*0.125).astype(BF)
        one=jnp.ones((8,T),BF)
        gq[...]=nt(one,oq[...])[0:1,:]
        gv[...]=nt(one,ov[...])[0:1,:]
    R=G*HD
    def b(off): return pl.BlockSpec((R,T),lambda g:(g+off,0))
    gb=pl.BlockSpec((1,R),lambda g:(0,g))
    return pl.pallas_call(kernel,grid=(ST,),
        out_shape=[SDS((D,T),BF)]*3+[SDS((1,D),F32)]*2,
        in_specs=[pl.BlockSpec((G,S,SEQ,SEQ),lambda g:(g,0,0,0)),b(0),b(ST),b(2*ST),b(0),b(0)],
        out_specs=[b(0)]*3+[gb,gb],
        compiler_params=pltpu.CompilerParams(vmem_limit_bytes=VMEM_CAP),name="attn_back")(p,qkvT,qkvT,qkvT,dcT,ctxT)

def in_grad(dq,dk,dv,dp1,wqkvT):
    T=dp1.shape[0]; RT=256; NT=T//RT
    def kernel(q_ref,k_ref,v_ref,dp_ref,w_h,o_ref,w_v,lsem):
        t=pl.program_id(0)
        ld=[pltpu.make_async_copy(w_h.at[pl.ds(i*D,D)],w_v.at[pl.ds(i*D,D)],lsem.at[i]) for i in range(3)]
        @pl.when(t==0)
        def _():
            for c in ld: c.start()
        acc=dp_ref[...]
        for i,r in enumerate((q_ref,k_ref,v_ref)):
            @pl.when(t==0)
            def _(): ld[i].wait()
            acc=acc+tn(r[...],w_v[i*D:(i+1)*D,:])
        o_ref[...]=acc.astype(BF)
    cb=pl.BlockSpec((D,RT),lambda t:(0,t))
    return pl.pallas_call(kernel,grid=(NT,),out_shape=SDS((T,D),BF),
        in_specs=[cb,cb,cb,pl.BlockSpec((RT,D),lambda t:(t,0)),ANY],out_specs=pl.BlockSpec((RT,D),lambda t:(t,0)),
        scratch_shapes=[pltpu.VMEM((3*D,D),BF),DMA((3,))],
        compiler_params=pltpu.CompilerParams(vmem_limit_bytes=VMEM_CAP),name="in_grad")(dq,dk,dv,dp1,wqkvT)


def placement_table(owners, owner_count, capacity):
    block_count = owners.shape[0]
    index_b = jnp.arange(block_count, dtype=jnp.int32)
    same_owner = owners[:, None] == owners[None, :]
    earlier = index_b[None, :] < index_b[:, None]
    rank_of = jnp.sum((same_owner & earlier).astype(jnp.int32), axis=1)
    owner_hit = owners[None, None, :] == jnp.arange(owner_count, dtype=jnp.int32)[:, None, None]
    slot_hit = rank_of[None, None, :] == jnp.arange(capacity, dtype=jnp.int32)[None, :, None]
    return (owner_hit & slot_hit).astype(jnp.float32)


def adam_rotated(grad_slots, value_slots, first_old, second_old, left_basis, right_basis, filled):
    turned = jnp.einsum("fcki,fckj->fcij", left_basis, grad_slots, precision=precise)
    turned = jnp.einsum("fcik,fckj->fcij", turned, right_basis, precision=precise)
    first_raw = decay_first * first_old + (1.0 - decay_first) * turned
    second_raw = decay_second * second_old + (1.0 - decay_second) * turned * turned
    normed_step = (
        first_raw
        / (1.0 - decay_first**STEP)
        / (jnp.sqrt(second_raw / (1.0 - decay_second**STEP)) + adam_eps)
    )
    restored = jnp.einsum("fcik,fckj->fcij", left_basis, normed_step, precision=precise)
    restored = jnp.einsum("fcik,fcjk->fcij", restored, right_basis, precision=precise)
    value_new = value_slots - step_rate * restored
    return (first_raw * filled, second_raw * filled, value_new * filled)


def body(
    acts,
    cotangent,
    seg_ids,
    pad_mask,
    qkv_weight,
    out_weight,
    in_weight,
    down_weight,
    biases,
    moment_first,
    moment_second,
    basis_left,
    basis_right,
    owners,
):
    ndp, nfs = lax.axis_size("dp"), lax.axis_size("fsdp")
    shards = [s.T for s in (qkv_weight, out_weight, in_weight, down_weight)]
    slots = acts.shape[0] * acts.shape[1]
    x = acts.reshape(slots * SEQ, D)
    cot = cotangent.reshape(slots * SEQ, D)
    seg = seg_ids.reshape(slots, SEQ)
    pad = pad_mask.reshape(slots, SEQ)
    bias = biases.reshape(1, -1)
    if (ndp, nfs) == (16, 2):
        mats = matdesc()
        (wqT,) = gather_call(mats[:1], shards[:1], 1)
        (qkvT, ctxT, ctx, p), (woT, wiT) = attn_fwd(mats[1:3], shards[1:3], 2, x, wqT, bias, seg, pad, ndp, nfs)
        (n1, r1, act, slope, won), (wdT,) = ff_up(mats[3:], shards[3:], 3, x, ctx, woT, wiT, bias, ndp, nfs)
    else:
        wqT, woT, wiT, wdT = [
            lax.all_gather(lax.all_gather(t, "fsdp", axis=1, tiled=True), "dp", axis=0, tiled=True) for t in shards
        ]
        (qkvT, ctxT, ctx, p), _ = attn_fwd([], [], 0, x, wqT, bias, seg, pad, ndp, nfs)
        (n1, r1, act, slope, won), _ = ff_up([], [], 0, x, ctx, woT, wiT, bias, ndp, nfs)
    out, dp1, dcT, g = ff_back(act, slope, n1, r1, cot, wdT, wiT, won, bias)
    dq, dk, dv, gq, gv = attn_back(p, qkvT, ctxT, dcT)
    ig = in_grad(dq, dk, dv, dp1, wqT)
    outputs, input_grads = out.reshape(acts.shape), ig.reshape(acts.shape)
    grad_total = jnp.concatenate([gq, gv, g[:, 2 * D :]], 1).reshape(-1)
    block_count = owners.shape[0]
    block_side = moment_first.shape[2]
    slot_table = placement_table(owners, lax.axis_size("fsdp"), moment_first.shape[1])
    grad_slots = jnp.einsum(
        "fcb,bij->fcij",
        slot_table,
        grad_total.reshape(block_count, block_side, block_side),
        precision=precise,
    )
    summed = lax.psum(grad_slots.astype(jnp.bfloat16), "dp")
    owned_grad = lax.psum_scatter(summed, "fsdp", scatter_dimension=0, tiled=True).astype(
        jnp.float32
    )
    own_table = lax.dynamic_slice_in_dim(slot_table, lax.axis_index("fsdp"), 1, 0)
    value_slots = jnp.einsum(
        "fcb,bij->fcij",
        own_table,
        biases.reshape(block_count, block_side, block_side),
        precision=precise,
    )
    filled = jnp.sum(own_table, axis=2)[:, :, None, None]
    first_new, second_new, value_new = adam_rotated(
        owned_grad, value_slots, moment_first, moment_second, basis_left, basis_right, filled
    )
    shared_grad, shared_value = (
        lax.all_gather(owned_grad, "fsdp", axis=0, tiled=True),
        lax.all_gather(value_new, "fsdp", axis=0, tiled=True),
    )
    bias_grad = jnp.einsum("fcb,fcij->bij", slot_table, shared_grad, precision=precise).reshape(
        biases.shape[0]
    )
    bias_new = jnp.einsum("fcb,fcij->bij", slot_table, shared_value, precision=precise).reshape(
        biases.shape[0]
    )
    return (
        outputs,
        input_grads,
        bias_grad,
        first_new,
        second_new,
        bias_new,
        bias_new.astype(jnp.bfloat16),
    )


def solution(mesh):
    placed = (
        P(None, ("dp", "fsdp"), None, None),
        P(None, ("dp", "fsdp"), None, None),
        P(None, ("dp", "fsdp"), None),
        P(None, ("dp", "fsdp"), None),
        P("fsdp", "dp"),
        P("fsdp", "dp"),
        P("fsdp", "dp"),
        P("fsdp", "dp"),
        P(),
        P("fsdp", None, None, None),
        P("fsdp", None, None, None),
        P("fsdp", None, None, None),
        P("fsdp", None, None, None),
        P(),
    )
    return jax.shard_map(
        body,
        mesh=mesh,
        in_specs=placed,
        out_specs=(
            P(None, ("dp", "fsdp"), None, None),
            P(None, ("dp", "fsdp"), None, None),
            P(),
            P("fsdp", None, None, None),
            P("fsdp", None, None, None),
            P(),
            P(),
        ),
        check_vma=False,
    )
```

```python
import functools
import math

import jax
import jax.numpy as jnp
from jax import lax
from jax.experimental import pallas as pl
from jax.experimental.pallas import tpu as pltpu
from jax.sharding import PartitionSpec as P

MESH=pl.DeviceIdType.MESH
NZ=4

def split_rows(R,L,a,b,unit=16):
    out=[];r=0
    for kind,n in (("A1",a),("A2",a),("B1",b),("B2",b)):
        if n: out.append((kind,r,n,0,L)); r+=n
    assert r==R,(r,R)
    return out
def split_lanes(R,L,a,b):
    out=[];l=0
    for kind,n in (("A1",a),("A2",a),("B1",b),("B2",b)):
        if n: out.append((kind,0,R,l,n)); l+=n
    assert l==L
    return out

EVENTS=[(dz,rx,ry) for dz in range(1-NZ,NZ) for rx in (0,1) for ry in (0,1) if (dz,rx,ry)!=(0,0,0)]
EVENTS.sort(key=lambda e:(abs(e[0])+e[1]+e[2], e[1]+e[2], -e[0]))
NEV=len(EVENTS)

def pick(i,values):
    out=jnp.int32(values[0])
    for j in range(1,len(values)):
        out=jnp.where(i==j,jnp.int32(values[j]),out)
    return out

def sends(kind,z,dz,rx,ry):
    plane=(rx==0)&(ry==0)
    turn_y=(kind[1]=="1")&(rx==1)&(ry==0)
    turn_x=(kind[1]=="2")&(rx==0)&(ry==1)
    if kind[0]=="A":
        return {"zp":plane&(dz>=0)&(z<NZ-1),"zm":plane&(dz<=0)&(z>0),"x":plane|turn_x,"y":plane|turn_y}
    return {"zp":(dz>=0)&(z<NZ-1),"zm":(dz<=0)&(z>0),"x":(dz==0)&(plane|turn_x),"y":(dz==0)&(plane|turn_y)}

WAYS=("x","y","zp","zm","s")

def region(total, N, K):
    for lanes in range(128,K+1,128):
        if total%lanes==0:
            rows=total//lanes
            if rows%16==0 and rows<=N: return rows,lanes
    raise ValueError(total)

class Gather:
    def __init__(self, mats, shards, fulls, local_sem, send_sem, recv_sem, sib_sem):
        self.mats=mats; self.sh=shards; self.full=fulls
        self.lsem,self.ssem,self.rsem,self.bsem=local_sem,send_sem,recv_sem,sib_sem
        dp=lax.axis_index("dp"); x=lax.axis_index("fsdp")
        self.dp,self.x=dp,x
        self.z=dp//4; self.y=(dp//2)%2; self.c=dp%2
        self.dev={"x":(dp,1-x),"y":(self.z*4+(1-self.y)*2+self.c,x),"zp":(dp+4,x),"zm":(dp-4,x),"s":(self.z*4+self.y*2+1-self.c,x)}
    def barrier(self):
        bar=pltpu.get_barrier_semaphore()
        for d in ("x","y","s"):
            pl.semaphore_signal(bar,inc=1,device_id=self.dev[d],device_id_type=MESH)
        @pl.when(self.z<NZ-1)
        def _(): pl.semaphore_signal(bar,inc=1,device_id=self.dev["zp"],device_id_type=MESH)
        @pl.when(self.z>0)
        def _(): pl.semaphore_signal(bar,inc=1,device_id=self.dev["zm"],device_id_type=MESH)
        inner=(self.z>0)&(self.z<NZ-1)
        @pl.when(inner)
        def _(): pl.semaphore_wait(bar,5)
        @pl.when(jnp.logical_not(inner))
        def _(): pl.semaphore_wait(bar,4)
    def place(self,m,k,dz,rx,ry):
        M=self.mats[m]; kind,r0,nr,l0,nl=M["classes"][k]
        y=self.y+ry-2*self.y*ry
        x=self.x+rx-2*self.x*rx
        src=(self.z-dz)*4+y*2+self.c
        return self.full[m].at[pl.ds(pl.multiple_of(src*M["R"]+r0,16),nr), pl.ds(pl.multiple_of(x*M["L"]+l0,128),nl)]
    def forward(self,m,k,dz,rx,ry,src):
        kind=self.mats[m]["classes"][k][0]
        dst=self.place(m,k,dz,rx,ry)
        def rel(a,b,c): return (a+NZ-1)*4+b*2+c
        child={"x":rel(dz,1,ry),"y":rel(dz,rx,1),"zp":rel(dz+1,rx,ry),"zm":rel(dz-1,rx,ry)}
        for d,cond in sends(kind,self.z,dz,rx,ry).items():
            def go(d=d):
                pltpu.make_async_remote_copy(src,dst,self.ssem.at[m,WAYS.index(d)],self.rsem.at[m,k,child[d]],
                    device_id=self.dev[d],device_id_type=MESH).start()
            if cond is True: go()
            elif cond is not False: pl.when(cond)(go)
        pltpu.make_async_remote_copy(src,dst,self.ssem.at[m,4],self.bsem.at[m,self.z-dz],device_id=self.dev["s"],device_id_type=MESH).start()
    def own(self,m):
        M=self.mats[m]
        for k,(kind,r0,nr,l0,nl) in enumerate(M["classes"]):
            self.forward(m,k,0,0,0,self.sh[m].at[pl.ds(r0,nr),pl.ds(l0,nl)])
        full=self.full[m].at[pl.ds(pl.multiple_of(self.dp*M["R"],16),M["R"]),pl.ds(pl.multiple_of(self.x*M["L"],128),M["L"])]
        pltpu.make_async_copy(self.sh[m],full,self.lsem.at[m]).start()
    def step(self,e,ms):
        dz=pick(e,[v[0] for v in EVENTS]); rx=pick(e,[v[1] for v in EVENTS]); ry=pick(e,[v[2] for v in EVENTS])
        src=self.z-dz
        @pl.when((src>=0)&(src<=NZ-1))
        def _():
            for m in ms:
                for k in range(len(self.mats[m]["classes"])):
                    ref=self.place(m,k,dz,rx,ry)
                    pltpu.make_async_copy(ref,ref,self.rsem.at[m,k,(dz+NZ-1)*4+rx*2+ry]).wait()
                    self.forward(m,k,dz,rx,ry,ref)
    def wait_bytes(self,m,total,sem):
        N,K=self.full[m].shape
        r,l=region(total,N,K)
        ref=self.full[m].at[pl.ds(0,r),pl.ds(0,l)]
        pltpu.make_async_copy(ref,ref,sem).wait()
    def own_done(self,m):
        own=self.sh[m]
        pltpu.make_async_copy(own,own,self.lsem.at[m]).wait()
    def plane_done(self,m,z0):
        N,K=self.full[m].shape
        self.wait_bytes(m,N*K//2//NZ,self.bsem.at[m,z0])
    def sends_done(self,m):
        M=self.mats[m]; N,K=self.full[m].shape
        def total(d,z):
            t=0
            for kind,r0,nr,l0,nl in M["classes"]:
                for dz,rx,ry in [(0,0,0)]+EVENTS:
                    if 0<=z-dz<=NZ-1 and sends(kind,z,dz,rx,ry)[d]: t+=nr*nl
            return t
        for d in ("x","y"):
            self.wait_bytes(m,total(d,0),self.ssem.at[m,WAYS.index(d)])
        for d in ("zp","zm"):
            for z in range(NZ):
                if total(d,z):
                    pl.when(self.z==z)(functools.partial(self.wait_bytes,m,total(d,z),self.ssem.at[m,WAYS.index(d)]))
        self.wait_bytes(m,N*K//2,self.ssem.at[m,4])
    def finish(self,m):
        self.own_done(m)
        for z in range(NZ): self.plane_done(m,z)
        self.sends_done(m)

def comm_scratch(n):
    return [pltpu.SemaphoreType.DMA((n,)),pltpu.SemaphoreType.DMA((n,5)),pltpu.SemaphoreType.DMA((n,4,8*NZ-4)),pltpu.SemaphoreType.DMA((n,NZ))] if n else []

def start_comm(mats,rest):
    n=len(mats)
    g=Gather(mats,rest[:n],rest[n:2*n],*rest[2*n:2*n+4])
    g.barrier()
    for m in range(n): g.own(m)
    return g

def gather_call(mats,shards,cid):
    n=len(mats)
    def kernel(*refs):
        g=start_comm(mats,list(refs))
        def st(e,_):
            g.step(e,range(n)); return _
        lax.fori_loop(0,NEV,st,0)
        for m in range(n): g.finish(m)
    outs=[jax.ShapeDtypeStruct((s.shape[0]*16,s.shape[1]*2),jnp.bfloat16) for s in shards]
    return pl.pallas_call(kernel,out_shape=outs,
        in_specs=[pl.BlockSpec(memory_space=pl.ANY)]*n,out_specs=[pl.BlockSpec(memory_space=pl.ANY)]*n,
        scratch_shapes=comm_scratch(n),
        compiler_params=pltpu.CompilerParams(collective_id=cid,has_side_effects=True,vmem_limit_bytes=60<<20),name="gather")(*shards)

def matdesc(beta=True):
    if beta:
        return [dict(R=192,L=512,classes=split_rows(192,512,80,16)),dict(R=64,L=512,classes=split_rows(64,512,32,0)),
            dict(R=256,L=512,classes=split_rows(256,512,96,32)),dict(R=64,L=2048,classes=split_lanes(64,2048,768,256))]
    return [dict(R=192,L=512,classes=split_rows(192,512,96,0)),dict(R=64,L=512,classes=split_rows(64,512,32,0)),
            dict(R=256,L=512,classes=split_rows(256,512,128,0)),dict(R=64,L=2048,classes=split_lanes(64,2048,1024,0))]
BF=jnp.bfloat16
F32=jnp.float32
D=1024
H=16
HD=64
FF=4096
SEQ=512
LOG2E=1.4426950408889634
VMEM_CAP=60<<20
ANY=pl.BlockSpec(memory_space=pl.ANY)
VM=pl.BlockSpec(memory_space=pltpu.VMEM)
SDS=jax.ShapeDtypeStruct
DMA=pltpu.SemaphoreType.DMA

def nn(a,b): return lax.dot_general(a,b,(((1,),(0,)),((),())),preferred_element_type=F32)
def nt(a,b): return lax.dot_general(a,b,(((1,),(1,)),((),())),preferred_element_type=F32)
def tn(a,b): return lax.dot_general(a,b,(((0,),(0,)),((),())),preferred_element_type=F32)
def part(i,n): return pl.ds(pl.multiple_of(i*n,n),n)
def loop(n,fn):
    def st(i,c):
        fn(i); return c
    lax.fori_loop(0,n,st,0)

OQ,OV,OO,O1,O2,OG1,OC1,OG2,OC2=0,D,2*D,3*D,3*D+FF,4*D+FF,5*D+FF,6*D+FF,7*D+FF

def column(row):
    return jnp.transpose(jnp.broadcast_to(row,(8,row.shape[1])))

class Quiet:
    def step(self,e,ms): pass

def comm_params(mats,cid,**kw):
    if mats: kw.update(collective_id=cid,has_side_effects=True)
    return pltpu.CompilerParams(vmem_limit_bytes=VMEM_CAP,**kw)

def full_shapes(mats,dp,fs):
    return [SDS((M["R"]*dp,M["L"]*fs),BF) for M in mats]

def attn_fwd(mats,shards,cid,x,wqkvT,bias,seg,pad,ndp,nfs):
    n=len(mats); S=x.shape[0]//SEQ; T=x.shape[0]; ms=range(n); QC=3*D//256
    def kernel(*refs):
        x_h,w_h,b_ref,seg_ref,pad_ref=refs[:5]
        sh=refs[5:5+n]; o=5+n
        qkv_o,ctxT_o,ctx_o,p_o=refs[o:o+4]
        full=refs[o+4:o+4+n]; o=o+4+n
        x_v,w_v,qkv_v,ctxT_v,ctx_v,mask_v,bc_v,pb,lsem,osem,psem=refs[o:o+11]
        sems=refs[o+11:]
        g=start_comm(mats,list(sh)+list(full)+list(sems)) if n else Quiet()
        cx=pltpu.make_async_copy(x_h,x_v,lsem.at[0]); cx.start()
        def w_load(j): return pltpu.make_async_copy(w_h.at[part(j,256)],w_v.at[part(j,256)],lsem.at[1+j])
        loop(QC,lambda j: w_load(j).start())
        bc_v[0:D,:]=column(b_ref[0:1,OQ:OQ+D])
        bc_v[D:2*D,:]=jnp.zeros((D,8),F32)
        bc_v[2*D:3*D,:]=column(b_ref[0:1,OV:OV+D])
        for s in range(S):
            seg_r=seg_ref[s:s+1,:]; pad_r=pad_ref[s:s+1,:]
            key_r=jnp.where(pad_r==1,seg_r,-1).astype(F32)
            key_c=column(key_r)[:,0:1]
            hit=(key_c==seg_r.astype(F32))|((pad_r==0)&(key_c>=0.0))
            mask_v[s]=jnp.where(hit,0.0,-1e30)
        cx.wait()
        def project(j):
            w_load(j).wait()
            r=part(j,256)
            qkv_v[r,:]=(nt(w_v[r,:],x_v[...])+bc_v[r,0:1]).astype(BF)
            pltpu.make_async_copy(qkv_v.at[r],qkv_o.at[r],osem.at[0]).start()
            g.step(j,ms)
        loop(QC,project)
        def attend(h):
            b=lax.rem(h,2)
            def p_copy(i): return pltpu.make_async_copy(pb.at[b],p_o.at[i],psem.at[b])
            @pl.when(h>=2)
            def _(): p_copy(h-2).wait()
            for s in range(S):
                cols=pl.ds(s*SEQ,SEQ)
                q=qkv_v[part(h,HD),cols]; k=qkv_v[part(h+H,HD),cols]; v=qkv_v[part(h+2*H,HD),cols]
                t=tn(k,q)*(0.125*LOG2E)+mask_v[s]
                e=jnp.exp2(t-jnp.max(t,axis=0,keepdims=True))
                p=(e*(1.0/jnp.sum(e,axis=0,keepdims=True))).astype(BF)
                pb[b,s]=p
                ctxT_v[part(h,HD),cols]=nn(v,p).astype(BF)
            p_copy(h).start()
            @pl.when(QC+h<NEV)
            def _(): g.step(QC+h,ms)
        loop(H,attend)
        ct=pltpu.make_async_copy(ctxT_v,ctxT_o,osem.at[1]); ct.start()
        def turn(i): ctx_v[:,part(i,128)]=jnp.transpose(ctxT_v[part(i,128),:])
        loop(D//128,turn)
        cc=pltpu.make_async_copy(ctx_v,ctx_o,osem.at[2]); cc.start()
        for m in ms: g.finish(m)
        pltpu.make_async_copy(qkv_v,qkv_o,osem.at[0]).wait()
        ct.wait(); cc.wait()
        for b in range(2): pltpu.make_async_copy(pb.at[b],p_o.at[b],psem.at[b]).wait()
    out=pl.pallas_call(kernel,
        out_shape=[SDS((3*D,T),BF),SDS((D,T),BF),SDS((T,D),BF),SDS((H,S,SEQ,SEQ),BF)]+full_shapes(mats,ndp,nfs),
        in_specs=[ANY,ANY,VM,VM,VM]+[ANY]*n,out_specs=[ANY]*(4+n),
        scratch_shapes=[pltpu.VMEM((T,D),BF),pltpu.VMEM((3*D,D),BF),pltpu.VMEM((3*D,T),BF),pltpu.VMEM((D,T),BF),pltpu.VMEM((T,D),BF),
            pltpu.VMEM((S,SEQ,SEQ),F32),pltpu.VMEM((3*D,8),F32),pltpu.VMEM((2,S,SEQ,SEQ),BF),DMA((1+QC,)),DMA((3,)),DMA((2,))]+comm_scratch(n),
        compiler_params=comm_params(mats,cid),name="attn_fwd")(x,wqkvT,bias,seg,pad,*shards)
    return out[:4],out[4:]

def ln(v):
    c=v-jnp.mean(v,axis=-1,keepdims=True)
    r=lax.rsqrt(jnp.mean(c*c,axis=-1,keepdims=True)+1e-12)
    return c*r,r

def feed(mats,shards,cid,x,ctx,cot,woT,wiT,wdT,bias,ndp,nfs):
    n=len(mats); T=x.shape[0]; RT=256; NT=T//RT; CH=1024; NC=FF//CH; UC=256; DC=D//4
    full_in=[] if n else [wdT]
    def kernel(*refs):
        x_h,ctx_h,cot_h,wo_h,wi_h,b_ref=refs[:6]
        o=6
        if n: sh=refs[o:o+n]; o+=n
        else: wd_h=refs[o]; o+=1
        out_o,dp1_o,dcT_o,g_ref=refs[o:o+4]; o+=4
        full=refs[o:o+n]; o+=n
        x_v,ctx_v,wo_v,won_v,wi_v,wd_v,n1_v,r1_v,hb_v,act_v,slope_v,f_v,u_v,lsem,osem=refs[o:o+15]
        sems=refs[o+15:]
        if n:
            g=start_comm(mats,list(sh)+list(full)+list(sems)); wd_h=full[0]; z=g.z
            order=[z,jnp.where(z==3,2,z+1),jnp.where(z==0,2,jnp.where(z==3,1,z-1)),jnp.where((z==0)|(z==1),3,0)]
        else:
            g=Quiet(); order=[0,1,2,3]
        def row(o,k=D): return b_ref[0:1,o:o+k]
        loads=[pltpu.make_async_copy(p,q,lsem.at[i]) for i,(p,q) in enumerate(((wo_h,wo_v),(ctx_h,ctx_v),(x_h,x_v)))]
        wl=pltpu.make_async_copy(wi_h,wi_v,lsem.at[3])
        for c in loads+[wl]: c.start()
        def wd_load(i):
            r=part(order[i],DC)
            return pltpu.make_async_copy(wd_h.at[r],wd_v.at[r],lsem.at[7+i])
        if not n:
            for i in range(4): wd_load(i).start()
        loads[0].wait()
        def turn(i): won_v[:,part(i,128)]=jnp.transpose(wo_v[part(i,128),:])
        loop(D//128,turn)
        cl=pltpu.make_async_copy(cot_h,wo_v,lsem.at[11]); cl.start()
        loads[1].wait(); loads[2].wait()
        g_ref[...]=jnp.zeros_like(g_ref)
        def join(t):
            rows=part(t,RT)
            br=nn(ctx_v[rows,:],won_v[...])+row(OO)
            nrm,r=ln(x_v[rows,:].astype(F32)+br)
            n1_v[rows,:]=nrm
            r1_v[rows,:]=jnp.broadcast_to(r,(RT,128))
            hb_v[rows,:]=(nrm*row(OG1)+row(OC1)).astype(BF)
            g.step(t,range(n))
        loop(NT,join)
        wl.wait()
        u_v[0]=nt(hb_v[...],wi_v[0:UC,:])
        def up(i):
            for b in range(2):
                ci=2*i+b
                cc=part(ci,UC)
                nx=part(lax.rem(ci+1,FF//UC),UC)
                bias_u=b_ref[0:1,part(ci+O1//UC,UC)]
                for t in range(NT):
                    rows=pl.ds(t*RT,RT)
                    u_v[1-b,rows,:]=nt(hb_v[rows,:],wi_v[nx,:])
                    u=u_v[b,rows,:]+bias_u
                    cdf=0.5+0.5*lax.erf(u*(1.0/math.sqrt(2.0)))
                    act_v[rows,cc]=(u*cdf).astype(BF)
                    slope_v[rows,cc]=(cdf+u*(jnp.exp2(u*u*(-0.5*LOG2E))*(1.0/math.sqrt(2.0*math.pi)))).astype(BF)
            g.step(NT+2*i,range(n)); g.step(NT+2*i+1,range(n))
        loop(FF//UC//2,up)
        done=NT+FF//UC
        def f_step(i,comm):
            wd_load(i).wait()
            r=part(order[i],DC)
            def tile(t):
                rows=part(t,RT)
                f_v[rows,r]=nt(act_v[rows,:],wd_v[r,:])
                if comm:
                    @pl.when(done+4*i+t<NEV)
                    def _(): g.step(done+4*i+t,range(n))
            loop(NT,tile)
        if n:
            g.own_done(0)
            for i in range(2): g.plane_done(0,order[i]); wd_load(i).start()
            for i in range(2): f_step(i,True)
            for i in range(2,4): g.plane_done(0,order[i]); wd_load(i).start()
        for i in range(2 if n else 0,4): f_step(i,False)
        cl.wait()
        cot_v=wo_v; ov=x_v; dcT_v=ctx_v
        def addg(o,v):
            for k in range(v.shape[1]//128):
                g_ref[pl.ds(o//128+k,1),:]+=v[:,k*128:(k+1)*128]
        def csum(v): return jnp.sum(v,axis=0,keepdims=True)
        def post(t):
            rows=part(t,RT)
            h1=n1_v[rows,:]*row(OG1)+row(OC1)
            n2,r2=ln(h1+(f_v[rows,:]+row(O2)))
            ov[rows,:]=(n2*row(OG2)+row(OC2)).astype(BF)
            pltpu.make_async_copy(ov.at[rows],out_o.at[rows],osem.at[0]).start()
            dy=cot_v[rows,:].astype(F32)
            addg(OG2,csum(dy*n2)); addg(OC2,csum(dy))
            e=dy*row(OG2)
            dp2=r2*(e-jnp.mean(e,axis=-1,keepdims=True)-n2*jnp.mean(e*n2,axis=-1,keepdims=True))
            dfb=dp2.astype(BF)
            hb_v[rows,:]=dfb
            addg(O2,csum(dfb.astype(F32)))
            f_v[rows,:]=dp2
            def inner(c):
                cc=part(c,CH)
                du=(nn(hb_v[rows,:],wd_v[:,cc])*slope_v[rows,cc].astype(F32)).astype(BF)
                s=csum(du.astype(F32))
                for k in range(CH//128):
                    g_ref[pl.ds(O1//128+c*(CH//128)+k,1),:]+=s[:,k*128:(k+1)*128]
                f_v[rows,:]+=nn(du,wi_v[cc,:])
            loop(NC,inner)
            dh1=f_v[rows,:]
            nrm1=n1_v[rows,:]
            addg(OG1,csum(dh1*nrm1)); addg(OC1,csum(dh1))
            e=dh1*row(OG1)
            dp1=r1_v[rows,0:1]*(e-jnp.mean(e,axis=-1,keepdims=True)-nrm1*jnp.mean(e*nrm1,axis=-1,keepdims=True))
            f_v[rows,:]=dp1
            pltpu.make_async_copy(f_v.at[rows],dp1_o.at[rows],osem.at[1]).start()
            da=dp1.astype(BF)
            addg(OO,csum(da.astype(F32)))
            hb_v[rows,:]=da
        loop(NT,post)
        def back(t):
            rows=part(t,RT)
            dcT_v[rows,:]=nt(won_v[rows,:],hb_v[...]).astype(BF)
        loop(NT,back)
        cd=pltpu.make_async_copy(dcT_v,dcT_o,osem.at[2]); cd.start()
        if n: g.sends_done(0)
        pltpu.make_async_copy(ov,out_o,osem.at[0]).wait()
        pltpu.make_async_copy(f_v,dp1_o,osem.at[1]).wait()
        cd.wait()
    V=pltpu.VMEM
    out=pl.pallas_call(kernel,
        out_shape=[SDS((T,D),BF),SDS((T,D),F32),SDS((D,T),BF),SDS((12*D//128,128),F32)]+full_shapes(mats,ndp,nfs),
        in_specs=[ANY]*5+[VM]+[ANY]*(n if n else 1),out_specs=[ANY]*3+[VM]+[ANY]*n,
        scratch_shapes=[V((T,D),BF),V((T,D),BF),V((D,D),BF),V((D,D),BF),V((FF,D),BF),V((D,FF),BF),V((T,D),F32),V((T,128),F32),
            V((T,D),BF),V((T,FF),BF),V((T,FF),BF),V((T,D),F32),V((2,T,UC),F32),DMA((12,)),DMA((3,))]+comm_scratch(n),
        compiler_params=comm_params(mats,cid),name="feed")(x,ctx,cot,woT,wiT,bias,*(shards if n else full_in))
    return out[:4]

STEP=5
decay_first=0.5
decay_second=0.5
adam_eps=1e-08
step_rate=0.4
NB=12
BS=32
LATE=2*D//128
EARLY=10*D//128
exact=lax.Precision.HIGHEST

def dot_exact(a,b,ca,cb):
    return lax.dot_general(a,b,(((ca,),(cb,)),((),())),precision=exact,preferred_element_type=F32)

class Reduce:
    def __init__(self,src,plane_buf,z_buf,ssem,psem,zsem):
        self.src,self.pb,self.zb,self.ssem,self.psem,self.zsem=src,plane_buf,z_buf,ssem,psem,zsem
        dp=lax.axis_index("dp"); self.x=lax.axis_index("fsdp")
        self.z=dp//4; self.y=(dp//2)%2; self.c=dp%2
        self.me=self.y*4+self.c*2+self.x
    def plane_peer(self,r):
        def flip(a,b): return 1-a if b else a
        return (self.z*4+flip(self.y,r&4)*2+flip(self.c,r&2),flip(self.x,r&1))
    def z_peer(self,r):
        hi,lo=self.z//2,self.z%2
        z=(1-hi if r&2 else hi)*2+(1-lo if r&1 else lo)
        return (z*4+self.y*2+self.c,self.x)
    def barrier(self):
        bar=pltpu.get_barrier_semaphore()
        for r in range(1,8): pl.semaphore_signal(bar,inc=1,device_id=self.plane_peer(r),device_id_type=MESH)
        for r in range(1,4): pl.semaphore_signal(bar,inc=1,device_id=self.z_peer(r),device_id_type=MESH)
        pl.semaphore_wait(bar,10)
    def copies(self,stage):
        buf,sem,idx=(self.pb,self.psem,self.me) if stage==0 else (self.zb,self.zsem,self.z)
        peers=[self.plane_peer(r) for r in range(1,8)] if stage==0 else [self.z_peer(r) for r in range(1,4)]
        return [pltpu.make_async_remote_copy(self.src if stage==0 else self.zb.at[idx],buf.at[idx],self.ssem.at[stage*7+i],sem.at[idx],
            device_id=p,device_id_type=MESH) for i,p in enumerate(peers)]
    def start(self):
        for c in self.copies(0): c.start()
    def gather(self,stage):
        buf,sem,idx,k=(self.pb,self.psem,self.me,8) if stage==0 else (self.zb,self.zsem,self.z,NZ)
        for q in range(k):
            @pl.when(q!=idx)
            def _(): pltpu.make_async_copy(buf.at[q],buf.at[q],sem.at[q]).wait()
    def middle(self):
        self.gather(0)
        self.pb[self.me]=self.src[...]
        tot=self.pb[0]
        for q in range(1,8): tot=tot+self.pb[q]
        self.zb[self.z]=tot
        for c in self.copies(1): c.start()
    def end(self):
        self.gather(1)
        tot=self.zb[0]
        for q in range(1,NZ): tot=tot+self.zb[q]
        return tot
    def finish(self):
        for st in (0,1):
            for c in self.copies(st): c.wait_send()

def reduce_scratch(rows):
    return [pltpu.VMEM((rows,128),F32),pltpu.VMEM((8,rows,128),F32),pltpu.VMEM((NZ,rows,128),F32),DMA((10,)),DMA((8,)),DMA((NZ,))]

def fold_tables(n):
    i=lax.broadcasted_iota(jnp.int32,(32*n,8*n),0); j=lax.broadcasted_iota(jnp.int32,(32*n,8*n),1)
    sel=jnp.where(i//4==j,1.0,0.0)
    i=lax.broadcasted_iota(jnp.int32,(32*n,128),0); j=lax.broadcasted_iota(jnp.int32,(32*n,128),1)
    mask=jnp.where(i%4==j//32,1.0,0.0)
    i=lax.broadcasted_iota(jnp.int32,(128,32),0); j=lax.broadcasted_iota(jnp.int32,(128,32),1)
    fold=jnp.where(i%32==j,1.0,0.0)
    return sel,mask,fold

def attn_tail(p,qkvT,ctxT,dcT,dp1,wqkvT,update,cid):
    S=p.shape[1]; T=S*SEQ; G=2; NI=H//G; R=G*HD; RT=256; NT=T//RT
    up=update is not None
    def kernel(*refs):
        p_h,qkv_h,c_h,d_h,dp_h,w_h=refs[:6]; o=6
        if up: g_in,b_in,mf_h,ms_h,bl_h,br_h,own_s=refs[o:o+7]; o+=7
        if up: ig_o,bg_o,mf_o,ms_o,bn_o,bl_o=refs[o:o+6]; o+=6
        else: ig_o,gl_o=refs[o:o+2]; o+=2
        pb,qkv_v,c_v,d_v,dp_v,w_v,ig_v,ones_v,psem,lsem,wsem,osem=refs[o:o+12]; o+=12
        if up:
            early_refs=refs[o:o+6]; late_refs=refs[o+6:o+12]; o+=12
            st_v,m_st,v_st,xs,xr=refs[o:o+5]; o+=5
            early=Reduce(*early_refs); late=Reduce(*late_refs); gl=late_refs[0]
        else: gl=gl_o
        def p_load(i): return pltpu.make_async_copy(p_h.at[part(i,G)],pb.at[lax.rem(i,2)],psem.at[lax.rem(i,2)])
        def chunk(i):
            out=[pltpu.make_async_copy(qkv_h.at[part(i+k*NI,R)],qkv_v.at[part(i+k*NI,R)],lsem.at[i,k]) for k in range(3)]
            return out+[pltpu.make_async_copy(a.at[part(i,R)],b.at[part(i,R)],lsem.at[i,3+k]) for k,(a,b) in enumerate(((d_h,d_v),(c_h,c_v)))]
        p_load(jnp.int32(0)).start()
        def begin(i):
            for c in chunk(i): c.start()
        loop(NI,begin)
        wl=pltpu.make_async_copy(w_h,w_v,wsem.at[0]); wl.start()
        dl=pltpu.make_async_copy(dp_h,dp_v,wsem.at[1]); dl.start()
        ones_v[...]=jnp.ones_like(ones_v)
        if up:
            early.barrier()
            early_refs[0][...]=g_in[LATE:,:]
            early.start()
            x=early.x
            states=[]
            for k,a in enumerate((mf_h,ms_h,bl_h,br_h)):
                states.append(pltpu.make_async_remote_copy(a.at[0],st_v.at[k,x],xs.at[k],xr.at[k],device_id=early.plane_peer(1),device_id_type=MESH))
                states.append(pltpu.make_async_copy(a.at[0],st_v.at[k,x],xs.at[4+k]))
            for c in states: c.start()
        def back(i):
            @pl.when(i<NI-1)
            def _(): p_load(i+1).start()
            for c in chunk(i): c.wait()
            p_load(i).wait()
            b=lax.rem(i,2)
            for s in range(S):
                cols=pl.ds(s*SEQ,SEQ)
                for h in range(G):
                    r=part(i*G+h,HD); rk=part(i*G+h+H,HD); rv=part(i*G+h+2*H,HD)
                    d=d_v[r,cols]
                    pr=pb[b,h,s]
                    q=qkv_v[r,cols]; k=qkv_v[rk,cols]; v=qkv_v[rv,cols]
                    delta=jnp.sum(d.astype(F32)*c_v[r,cols].astype(F32),axis=0,keepdims=True)
                    ds=(pr.astype(F32)*(tn(v,d)-delta)).astype(BF)
                    qkv_v[rv,cols]=nt(d,pr).astype(BF)
                    qkv_v[rk,cols]=(nt(q,ds)*0.125).astype(BF)
                    qkv_v[r,cols]=(nn(k,ds)*0.125).astype(BF)
            gl[pl.ds(i,1),:]=nt(ones_v[...],qkv_v[part(i,R),:])[0:1,:]
            gl[pl.ds(NI+i,1),:]=nt(ones_v[...],qkv_v[part(i+2*NI,R),:])[0:1,:]
            if up:
                @pl.when(i==3)
                def _(): early.middle()
        loop(NI,back)
        if up: late.start()
        wl.wait(); dl.wait()
        def finish(t):
            cols=part(t,RT)
            acc=dp_v[cols,:]
            for k in range(3):
                acc=acc+tn(qkv_v[k*D:(k+1)*D,cols],w_v[k*D:(k+1)*D,:])
            ig_v[cols,:]=acc.astype(BF)
            pltpu.make_async_copy(ig_v.at[cols],ig_o.at[cols],osem.at[0]).start()
            if up:
                @pl.when(t==1)
                def _(): late.middle()
        loop(NT,finish)
        if up:
            for c in states: c.wait()
            owner=[own_s[b] for b in range(NB)]
            rank=[]
            for b in range(NB):
                r=jnp.int32(0)
                for e in range(b): r=r+jnp.where(owner[e]==owner[b],1,0)
                rank.append(r)
            def adam(b0,n,tiles):
                sel,mask,fold=fold_tables(n)
                gs=dot_exact(dot_exact(sel,tiles,1,0)*mask,fold,1,0)
                outs=[]
                for j in range(n):
                    b=b0+j
                    at=jnp.minimum(rank[b],st_v.shape[2]-1)
                    first,second,left,right=[st_v[k,owner[b],at] for k in range(4)]
                    t=dot_exact(dot_exact(left,gs[j*BS:(j+1)*BS,:],0,0),right,1,0)
                    m=decay_first*first+(1.0-decay_first)*t
                    v=decay_second*second+(1.0-decay_second)*t*t
                    m_st[b]=m; v_st[b]=v
                    un=(m/(1.0-decay_first**STEP))/(jnp.sqrt(v/(1.0-decay_second**STEP))+adam_eps)
                    outs.append(dot_exact(dot_exact(left,un,1,0),right,1,1))
                back_=dot_exact(jnp.concatenate(outs,0),fold,1,1)*mask
                new=b_in[8*b0:8*(b0+n),:]-step_rate*dot_exact(sel,back_,0,0)
                bg_o[8*b0:8*(b0+n),:]=tiles
                bn_o[8*b0:8*(b0+n),:]=new
                bl_o[8*b0:8*(b0+n),:]=new.astype(BF)
            adam(2,10,early.end())
            adam(0,2,late.end())
            for c in range(mf_o.shape[1]):
                at=jnp.int32(0); hit=jnp.int32(0)
                for b in range(NB):
                    here=(owner[b]==x)&(rank[b]==c)
                    at=at+jnp.where(here,b,0); hit=hit+jnp.where(here,1,0)
                at=jnp.minimum(at,NB-1)
                filled=hit.astype(F32)
                mf_o[0,c]=m_st[at]*filled
                ms_o[0,c]=v_st[at]*filled
            early.finish(); late.finish()
        pltpu.make_async_copy(ig_v,ig_o,osem.at[0]).wait()
    V=pltpu.VMEM
    scr=[V((2,G,S,SEQ,SEQ),BF),V((3*D,T),BF),V((D,T),BF),V((D,T),BF),V((T,D),F32),V((3*D,D),BF),V((T,D),BF),V((8,T),BF),DMA((2,)),DMA((NI,5)),DMA((2,)),DMA((1,))]
    ins=[p,qkvT,ctxT,dcT,dp1,wqkvT]; specs=[ANY]*6
    outs=[SDS((T,D),BF)]; ospecs=[ANY]
    if up:
        g,bias,mf,ms,bl,br,owners=update
        ins+=[g,bias,mf,ms,bl,br,owners]; specs+=[VM,VM]+[ANY]*4+[pl.BlockSpec(memory_space=pltpu.SMEM)]
        outs+=[SDS((NB*8,128),F32),SDS(mf.shape,F32),SDS(mf.shape,F32),SDS((NB*8,128),F32),SDS((NB*8,128),BF)]; ospecs+=[VM]*5
        st=(4,2)+mf.shape[1:]
        scr+=reduce_scratch(EARLY)+reduce_scratch(LATE)+[V(st,F32),V((NB,BS,BS),F32),V((NB,BS,BS),F32),DMA((8,)),DMA((4,))]
    else:
        outs+=[SDS((LATE,128),F32)]; ospecs+=[VM]
    return pl.pallas_call(kernel,out_shape=outs,in_specs=specs,out_specs=ospecs,scratch_shapes=scr,
        compiler_params=comm_params([1] if up else [],cid),name="attn_tail")(*ins)


def placement_table(owners, owner_count, capacity):
    block_count = owners.shape[0]
    index_b = jnp.arange(block_count, dtype=jnp.int32)
    same_owner = owners[:, None] == owners[None, :]
    earlier = index_b[None, :] < index_b[:, None]
    rank_of = jnp.sum((same_owner & earlier).astype(jnp.int32), axis=1)
    owner_hit = owners[None, None, :] == jnp.arange(owner_count, dtype=jnp.int32)[:, None, None]
    slot_hit = rank_of[None, None, :] == jnp.arange(capacity, dtype=jnp.int32)[None, :, None]
    return (owner_hit & slot_hit).astype(jnp.float32)


def adam_rotated(grad_slots, value_slots, first_old, second_old, left_basis, right_basis, filled):
    turned = jnp.einsum("fcki,fckj->fcij", left_basis, grad_slots, precision=exact)
    turned = jnp.einsum("fcik,fckj->fcij", turned, right_basis, precision=exact)
    first_raw = decay_first * first_old + (1.0 - decay_first) * turned
    second_raw = decay_second * second_old + (1.0 - decay_second) * turned * turned
    normed_step = (
        first_raw
        / (1.0 - decay_first**STEP)
        / (jnp.sqrt(second_raw / (1.0 - decay_second**STEP)) + adam_eps)
    )
    restored = jnp.einsum("fcik,fckj->fcij", left_basis, normed_step, precision=exact)
    restored = jnp.einsum("fcik,fcjk->fcij", restored, right_basis, precision=exact)
    value_new = value_slots - step_rate * restored
    return (first_raw * filled, second_raw * filled, value_new * filled)


def body(
    acts,
    cotangent,
    seg_ids,
    pad_mask,
    qkv_weight,
    out_weight,
    in_weight,
    down_weight,
    biases,
    moment_first,
    moment_second,
    basis_left,
    basis_right,
    owners,
):
    ndp, nfs = lax.axis_size("dp"), lax.axis_size("fsdp")
    shards = [s.T for s in (qkv_weight, out_weight, in_weight, down_weight)]
    slots = acts.shape[0] * acts.shape[1]
    x = acts.reshape(slots * SEQ, D)
    cot = cotangent.reshape(slots * SEQ, D)
    seg = seg_ids.reshape(slots, SEQ)
    pad = pad_mask.reshape(slots, SEQ)
    bias = biases.reshape(1, -1)
    if (ndp, nfs) == (16, 2):
        mats = matdesc()
        (wqT,) = gather_call(mats[:1], shards[:1], 1)
        (qkvT, ctxT, ctx, p), (woT, wiT) = attn_fwd(mats[1:3], shards[1:3], 2, x, wqT, bias, seg, pad, ndp, nfs)
        out, dp1, dcT, g = feed(mats[3:], shards[3:], 3, x, ctx, cot, woT, wiT, None, bias, ndp, nfs)
        state = (g, biases.reshape(-1, 128), moment_first, moment_second, basis_left, basis_right, owners)
        ig, bg, mf, ms, bn, bl = attn_tail(p, qkvT, ctxT, dcT, dp1, wqT, state, 4)
        return (
            out.reshape(acts.shape),
            ig.reshape(acts.shape),
            bg.reshape(-1),
            mf,
            ms,
            bn.reshape(-1),
            bl.reshape(-1),
        )
    wqT, woT, wiT, wdT = [
        lax.all_gather(lax.all_gather(t, "fsdp", axis=1, tiled=True), "dp", axis=0, tiled=True) for t in shards
    ]
    (qkvT, ctxT, ctx, p), _ = attn_fwd([], [], 0, x, wqT, bias, seg, pad, ndp, nfs)
    out, dp1, dcT, g = feed([], [], 0, x, ctx, cot, woT, wiT, wdT, bias, ndp, nfs)
    ig, gl = attn_tail(p, qkvT, ctxT, dcT, dp1, wqT, None, 0)
    outputs, input_grads = out.reshape(acts.shape), ig.reshape(acts.shape)
    grad_total = jnp.concatenate([gl, g[LATE:]], 0).reshape(-1)
    block_count = owners.shape[0]
    block_side = moment_first.shape[2]
    slot_table = placement_table(owners, lax.axis_size("fsdp"), moment_first.shape[1])
    grad_slots = jnp.einsum(
        "fcb,bij->fcij",
        slot_table,
        grad_total.reshape(block_count, block_side, block_side),
        precision=exact,
    )
    summed = lax.psum(grad_slots.astype(jnp.bfloat16), "dp")
    owned_grad = lax.psum_scatter(summed, "fsdp", scatter_dimension=0, tiled=True).astype(
        jnp.float32
    )
    own_table = lax.dynamic_slice_in_dim(slot_table, lax.axis_index("fsdp"), 1, 0)
    value_slots = jnp.einsum(
        "fcb,bij->fcij",
        own_table,
        biases.reshape(block_count, block_side, block_side),
        precision=exact,
    )
    filled = jnp.sum(own_table, axis=2)[:, :, None, None]
    first_new, second_new, value_new = adam_rotated(
        owned_grad, value_slots, moment_first, moment_second, basis_left, basis_right, filled
    )
    shared_grad, shared_value = (
        lax.all_gather(owned_grad, "fsdp", axis=0, tiled=True),
        lax.all_gather(value_new, "fsdp", axis=0, tiled=True),
    )
    bias_grad = jnp.einsum("fcb,fcij->bij", slot_table, shared_grad, precision=exact).reshape(
        biases.shape[0]
    )
    bias_new = jnp.einsum("fcb,fcij->bij", slot_table, shared_value, precision=exact).reshape(
        biases.shape[0]
    )
    return (
        outputs,
        input_grads,
        bias_grad,
        first_new,
        second_new,
        bias_new,
        bias_new.astype(jnp.bfloat16),
    )


def solution(mesh):
    placed = (
        P(None, ("dp", "fsdp"), None, None),
        P(None, ("dp", "fsdp"), None, None),
        P(None, ("dp", "fsdp"), None),
        P(None, ("dp", "fsdp"), None),
        P("fsdp", "dp"),
        P("fsdp", "dp"),
        P("fsdp", "dp"),
        P("fsdp", "dp"),
        P(),
        P("fsdp", None, None, None),
        P("fsdp", None, None, None),
        P("fsdp", None, None, None),
        P("fsdp", None, None, None),
        P(),
    )
    return jax.shard_map(
        body,
        mesh=mesh,
        in_specs=placed,
        out_specs=(
            P(None, ("dp", "fsdp"), None, None),
            P(None, ("dp", "fsdp"), None, None),
            P(),
            P("fsdp", None, None, None),
            P("fsdp", None, None, None),
            P(),
            P(),
        ),
        check_vma=False,
    )
```

```python
import functools
import math

import jax
import jax.numpy as jnp
from jax import lax
from jax.experimental import pallas as pl
from jax.experimental.pallas import tpu as pltpu
from jax.sharding import PartitionSpec as P

MESH=pl.DeviceIdType.MESH
NZ=4

def split_rows(R,L,a,b,unit=16):
    out=[];r=0
    for kind,n in (("A1",a),("A2",a),("B1",b),("B2",b)):
        if n: out.append((kind,r,n,0,L)); r+=n
    assert r==R,(r,R)
    return out
def split_lanes(R,L,a,b):
    out=[];l=0
    for kind,n in (("A1",a),("A2",a),("B1",b),("B2",b)):
        if n: out.append((kind,0,R,l,n)); l+=n
    assert l==L
    return out

EVENTS=[(dz,rx,ry) for dz in range(1-NZ,NZ) for rx in (0,1) for ry in (0,1) if (dz,rx,ry)!=(0,0,0)]
EVENTS.sort(key=lambda e:(abs(e[0])+e[1]+e[2], e[1]+e[2], -e[0]))
NEV=len(EVENTS)

def pick(i,values):
    out=jnp.int32(values[0])
    for j in range(1,len(values)):
        out=jnp.where(i==j,jnp.int32(values[j]),out)
    return out

def sends(kind,z,dz,rx,ry):
    plane=(rx==0)&(ry==0)
    turn_y=(kind[1]=="1")&(rx==1)&(ry==0)
    turn_x=(kind[1]=="2")&(rx==0)&(ry==1)
    if kind[0]=="A":
        return {"zp":plane&(dz>=0)&(z<NZ-1),"zm":plane&(dz<=0)&(z>0),"x":plane|turn_x,"y":plane|turn_y}
    return {"zp":(dz>=0)&(z<NZ-1),"zm":(dz<=0)&(z>0),"x":(dz==0)&(plane|turn_x),"y":(dz==0)&(plane|turn_y)}

WAYS=("x","y","zp","zm","s")

def region(total, N, K):
    for lanes in range(128,K+1,128):
        if total%lanes==0:
            rows=total//lanes
            if rows%16==0 and rows<=N: return rows,lanes
    raise ValueError(total)

class Gather:
    def __init__(self, mats, shards, fulls, local_sem, send_sem, recv_sem, sib_sem):
        self.mats=mats; self.sh=shards; self.full=fulls
        self.lsem,self.ssem,self.rsem,self.bsem=local_sem,send_sem,recv_sem,sib_sem
        dp=lax.axis_index("dp"); x=lax.axis_index("fsdp")
        self.dp,self.x=dp,x
        self.z=dp//4; self.y=(dp//2)%2; self.c=dp%2
        self.dev={"x":(dp,1-x),"y":(self.z*4+(1-self.y)*2+self.c,x),"zp":(dp+4,x),"zm":(dp-4,x),"s":(self.z*4+self.y*2+1-self.c,x)}
    def barrier(self):
        bar=pltpu.get_barrier_semaphore()
        for d in ("x","y","s"):
            pl.semaphore_signal(bar,inc=1,device_id=self.dev[d],device_id_type=MESH)
        @pl.when(self.z<NZ-1)
        def _(): pl.semaphore_signal(bar,inc=1,device_id=self.dev["zp"],device_id_type=MESH)
        @pl.when(self.z>0)
        def _(): pl.semaphore_signal(bar,inc=1,device_id=self.dev["zm"],device_id_type=MESH)
        inner=(self.z>0)&(self.z<NZ-1)
        @pl.when(inner)
        def _(): pl.semaphore_wait(bar,5)
        @pl.when(jnp.logical_not(inner))
        def _(): pl.semaphore_wait(bar,4)
    def place(self,m,k,dz,rx,ry):
        M=self.mats[m]; kind,r0,nr,l0,nl=M["classes"][k]
        y=self.y+ry-2*self.y*ry
        x=self.x+rx-2*self.x*rx
        src=(self.z-dz)*4+y*2+self.c
        return self.full[m].at[pl.ds(pl.multiple_of(src*M["R"]+r0,16),nr), pl.ds(pl.multiple_of(x*M["L"]+l0,128),nl)]
    def forward(self,m,k,dz,rx,ry,src):
        kind=self.mats[m]["classes"][k][0]
        dst=self.place(m,k,dz,rx,ry)
        def rel(a,b,c): return (a+NZ-1)*4+b*2+c
        child={"x":rel(dz,1,ry),"y":rel(dz,rx,1),"zp":rel(dz+1,rx,ry),"zm":rel(dz-1,rx,ry)}
        for d,cond in sends(kind,self.z,dz,rx,ry).items():
            def go(d=d):
                pltpu.make_async_remote_copy(src,dst,self.ssem.at[m,WAYS.index(d)],self.rsem.at[m,k,child[d]],
                    device_id=self.dev[d],device_id_type=MESH).start()
            if cond is True: go()
            elif cond is not False: pl.when(cond)(go)
        pltpu.make_async_remote_copy(src,dst,self.ssem.at[m,4],self.bsem.at[m,self.z-dz],device_id=self.dev["s"],device_id_type=MESH).start()
    def own(self,m):
        M=self.mats[m]
        for k,(kind,r0,nr,l0,nl) in enumerate(M["classes"]):
            self.forward(m,k,0,0,0,self.sh[m].at[pl.ds(r0,nr),pl.ds(l0,nl)])
        full=self.full[m].at[pl.ds(pl.multiple_of(self.dp*M["R"],16),M["R"]),pl.ds(pl.multiple_of(self.x*M["L"],128),M["L"])]
        pltpu.make_async_copy(self.sh[m],full,self.lsem.at[m]).start()
    def step(self,e,ms):
        code=pick(e,[(v[0]+NZ-1)*4+v[1]*2+v[2] for v in EVENTS])
        dz=code//4-(NZ-1); rx=(code//2)%2; ry=code%2
        src=self.z-dz
        @pl.when((src>=0)&(src<=NZ-1))
        def _():
            for m in ms:
                for k in range(len(self.mats[m]["classes"])):
                    ref=self.place(m,k,dz,rx,ry)
                    pltpu.make_async_copy(ref,ref,self.rsem.at[m,k,(dz+NZ-1)*4+rx*2+ry]).wait()
                    self.forward(m,k,dz,rx,ry,ref)
    def wait_bytes(self,m,total,sem):
        N,K=self.full[m].shape
        r,l=region(total,N,K)
        ref=self.full[m].at[pl.ds(0,r),pl.ds(0,l)]
        pltpu.make_async_copy(ref,ref,sem).wait()
    def own_done(self,m):
        own=self.sh[m]
        pltpu.make_async_copy(own,own,self.lsem.at[m]).wait()
    def plane_done(self,m,z0):
        N,K=self.full[m].shape
        self.wait_bytes(m,N*K//2//NZ,self.bsem.at[m,z0])
    def sends_done(self,m):
        M=self.mats[m]; N,K=self.full[m].shape
        def total(d,z):
            t=0
            for kind,r0,nr,l0,nl in M["classes"]:
                for dz,rx,ry in [(0,0,0)]+EVENTS:
                    if 0<=z-dz<=NZ-1 and sends(kind,z,dz,rx,ry)[d]: t+=nr*nl
            return t
        for d in ("x","y"):
            self.wait_bytes(m,total(d,0),self.ssem.at[m,WAYS.index(d)])
        for d in ("zp","zm"):
            for z in range(NZ):
                if total(d,z):
                    pl.when(self.z==z)(functools.partial(self.wait_bytes,m,total(d,z),self.ssem.at[m,WAYS.index(d)]))
        self.wait_bytes(m,N*K//2,self.ssem.at[m,4])
    def finish(self,m):
        self.own_done(m)
        for z in range(NZ): self.plane_done(m,z)
        self.sends_done(m)

def comm_scratch(n):
    return [pltpu.SemaphoreType.DMA((n,)),pltpu.SemaphoreType.DMA((n,5)),pltpu.SemaphoreType.DMA((n,4,8*NZ-4)),pltpu.SemaphoreType.DMA((n,NZ))] if n else []

def matdesc(beta=True):
    if beta:
        return [dict(R=192,L=512,classes=split_rows(192,512,80,16)),dict(R=64,L=512,classes=split_rows(64,512,32,0)),
            dict(R=256,L=512,classes=split_rows(256,512,96,32)),dict(R=64,L=2048,classes=split_lanes(64,2048,768,256))]
    return [dict(R=192,L=512,classes=split_rows(192,512,96,0)),dict(R=64,L=512,classes=split_rows(64,512,32,0)),
            dict(R=256,L=512,classes=split_rows(256,512,128,0)),dict(R=64,L=2048,classes=split_lanes(64,2048,1024,0))]
BF=jnp.bfloat16
F32=jnp.float32
D=1024
H=16
HD=64
FF=4096
SEQ=512
LOG2E=1.4426950408889634
VMEM_CAP=60<<20
ANY=pl.BlockSpec(memory_space=pl.ANY)
VM=pl.BlockSpec(memory_space=pltpu.VMEM)
SDS=jax.ShapeDtypeStruct
DMA=pltpu.SemaphoreType.DMA

def nn(a,b): return lax.dot_general(a,b,(((1,),(0,)),((),())),preferred_element_type=F32)
def nt(a,b): return lax.dot_general(a,b,(((1,),(1,)),((),())),preferred_element_type=F32)
def tn(a,b): return lax.dot_general(a,b,(((0,),(0,)),((),())),preferred_element_type=F32)
def part(i,n): return pl.ds(pl.multiple_of(i*n,n),n)
def loop(n,fn):
    def st(i,c):
        fn(i); return c
    lax.fori_loop(0,n,st,0)

OQ,OV,OO,O1,O2,OG1,OC1,OG2,OC2=0,D,2*D,3*D,3*D+FF,4*D+FF,5*D+FF,6*D+FF,7*D+FF

def column(row):
    return jnp.transpose(jnp.broadcast_to(row,(8,row.shape[1])))

class Quiet:
    def step(self,e,ms): pass

def comm_params(mats,cid,**kw):
    if mats: kw.update(collective_id=cid,has_side_effects=True)
    return pltpu.CompilerParams(vmem_limit_bytes=VMEM_CAP,**kw)

def full_shapes(mats,dp,fs):
    return [SDS((M["R"]*dp,M["L"]*fs),BF) for M in mats]

def ln(v):
    c=v-jnp.mean(v,axis=-1,keepdims=True)
    r=lax.rsqrt(jnp.mean(c*c,axis=-1,keepdims=True)+1e-12)
    return c*r,r

PACE=[13, 15, 15, 30, 34, 34, 37, 37, 39, 42, 51, 53, 53, 53, 53, 58, 58, 58, 58, 60, 60, 60, 64, 64, 67, 70, 71, 73, 78, 78, 79, 84, 84, 84, 87, 90, 90, 92, 95, 99, 101, 103, 103, 103, 106, 106, 106, 108, 108, 108, 108, 108, 108, 108, 108, 108]
OWN={1: 18, 2: 48, 3: 78}

def forward(mats,sources,cid,x,cot,bias,seg,pad,ndp,nfs):
    comm=bool(mats); n=len(mats); S=x.shape[0]//SEQ; T=x.shape[0]
    RT=256; NT=T//RT; CH=1024; NC=FF//CH; UC=256; DC=D//4; QC=3*D//4//256

    def kernel(*refs):
        x_h,cot_h,b_ref,seg_ref,pad_ref=refs[:5]
        src=refs[5:9]; o=9
        qkv_o,ctxT_o,p_o,out_o,dp1_o,dcT_o,g_ref=refs[o:o+7]; o+=7
        if comm: wq_h=refs[o]; o+=1
        else: wq_h=src[0]
        x_v,ctx_v,wo_v,won_v,wi_v,wd_v,n1_v,r1_v,hb_v,act_v,slope_v,f_v,u_v,acc_v,df_v,ga_v,gb_v,lsem,wsem,psem,osem=refs[o:o+21]; o+=21
        loads=[pltpu.make_async_copy(x_h,x_v,lsem.at[0]),pltpu.make_async_copy(cot_h,wo_v,lsem.at[1])]
        loads[0].start()
        if not comm:
            whole={m:pltpu.make_async_copy(src[m],v,lsem.at[1+m]) for m,v in ((1,wo_v),(2,wi_v),(3,wd_v))}
            for c in whole.values(): c.start()
        if comm:
            in_t=refs[o]; sems=refs[o+1:]
            g=Gather(mats,(src[0],src[1],in_t,src[3]),(wq_h,wo_v,wi_v,wd_v),*sems); g.barrier(); g.own(0)
            eye=jnp.where(lax.broadcasted_iota(jnp.int32,(256,256),0)==lax.broadcasted_iota(jnp.int32,(256,256),1),1.0,0.0).astype(BF)
            in_t[...]=nt(eye,src[2][...]).astype(BF)
            z=g.z
            order=[z,jnp.where(z==3,2,z+1),jnp.where(z==0,2,jnp.where(z==3,1,z-1)),jnp.where((z==0)|(z==1),3,0)]
        else: order=[0,1,2,3]
        def steps(m,a,b):
            def one(e,carry):
                g.step(e,[m])
                for k,at in OWN.items():
                    if (at-1)//NEV==m:
                        @pl.when(e==(at-1)%NEV)
                        def _(): g.own(k)
                return carry
            lax.fori_loop(a,b,one,0)
        def pace(op,i,count):
            if not comm: return
            starts=[PACE[j-1] if j else 0 for j in range(op,op+count)]; ends=PACE[op:op+count]
            a,b=pick(i,starts),pick(i,ends)
            for m in range(4):
                if starts[0]<NEV*(m+1) and ends[-1]>NEV*m and starts[0]<ends[-1]:
                    steps(m,jnp.clip(a-NEV*m,0,NEV),jnp.clip(b-NEV*m,0,NEV))
        def plane(m,i):
            if comm:
                if i==0: g.own_done(m)
                g.plane_done(m,order[i])
            elif i==0 and m>0: whole[m].wait()
        def row(o,k=D): return b_ref[0:1,o:o+k]
        n1_v[:,0:8]=column(row(OQ)); n1_v[:,128:136]=jnp.zeros((D,8),F32); n1_v[:,256:264]=column(row(OV))
        for s in range(S):
            seg_r=seg_ref[s]; pad_r=pad_ref[s]
            key_r=jnp.where(pad_r==1,seg_r,-1).astype(F32)
            key_c=column(key_r)[:,0:1]
            hit=(key_c==seg_r.astype(F32))|((pad_r==0)&(key_c>=0.0))
            f_v[s*SEQ:(s+1)*SEQ,0:SEQ]=jnp.where(hit,0.0,-1e30)
        def project(i):
            pace(QC*i,0,1); plane(0,i)
            def load(c): return pltpu.make_async_copy(wq_h.at[part(order[i]*QC+c,256)],slope_v.at[part(c,256),2048:3072],wsem.at[c])
            loop(QC,lambda c: load(c).start())
            def chunk(c):
                jj=order[i]*QC+c; j=jj//4; rows=part(jj%4,256); cols=part(j,T)
                load(c).wait()
                acc=nt(slope_v[part(c,256),2048:3072],x_v[...])+n1_v[rows,part(j,128)][:,0:1]
                act_v[rows,cols]=acc.astype(BF)
                pltpu.make_async_copy(act_v.at[rows,cols],qkv_o.at[part(jj,256)],osem.at[0]).start()
                @pl.when(c<QC-1)
                def _(): pace(QC*i+1,c,QC-1)
            loop(QC,chunk)
        loads[0].wait()
        for i in range(4): project(i)
        AT=4*QC
        def attend(h):
            pace(AT,h,H)
            b=lax.rem(h,2)
            def p_copy(i,s): return pltpu.make_async_copy(slope_v.at[part(b,SEQ),s*SEQ:(s+1)*SEQ],p_o.at[i,s],psem.at[b,s])
            @pl.when(h>=2)
            def _():
                for s in range(S): p_copy(h-2,s).wait()
            for s in range(S):
                def at(j): return pl.ds(j*T+s*SEQ,SEQ)
                r=part(h,HD)
                q=act_v[r,at(0)]; k=act_v[r,at(1)]; v=act_v[r,at(2)]
                t=tn(k,q)*(0.125*LOG2E)+f_v[s*SEQ:(s+1)*SEQ,0:SEQ]
                e=jnp.exp2(t-jnp.max(t,axis=0,keepdims=True))
                p=(e*(1.0/jnp.sum(e,axis=0,keepdims=True))).astype(BF)
                slope_v[part(b,SEQ),s*SEQ:(s+1)*SEQ]=p
                hb_v[r,pl.ds(s*SEQ,SEQ)]=nn(v,p).astype(BF)
                p_copy(h,s).start()
        loop(H,attend)
        ct=pltpu.make_async_copy(hb_v,ctxT_o,osem.at[1]); ct.start()
        def turn(i): ctx_v[:,part(i,128)]=jnp.transpose(hb_v[part(i,128),:])
        loop(D//128,turn)
        for i in range(4): plane(1,i)
        def turn2(i): won_v[:,part(i,128)]=jnp.transpose(wo_v[part(i,128),:])
        loop(D//128,turn2)
        if comm: g.sends_done(1)
        loads[1].start()
        pltpu.make_async_copy(act_v.at[:,0:3*T],act_v.at[:,0:3*T],osem.at[0]).wait()
        for b in range(2):
            for s in range(S): pltpu.make_async_copy(slope_v.at[b*SEQ:(b+1)*SEQ,s*SEQ:(s+1)*SEQ],p_o.at[b,s],psem.at[b,s]).wait()
        ct.wait()
        g_ref[...]=jnp.zeros_like(g_ref)
        def join(t):
            pace(AT+H,t,NT)
            rows=part(t,RT)
            br=nn(ctx_v[rows,:],won_v[...])+row(OO)
            nrm,r=ln(x_v[rows,:].astype(F32)+br)
            n1_v[rows,:]=nrm
            r1_v[rows,:]=jnp.broadcast_to(r,(RT,128))
            hb_v[rows,:]=(nrm*row(OG1)+row(OC1)).astype(BF)
        loop(NT,join)
        UP=AT+H+NT
        def up(i):
            c0=order[i]*(CH//UC)
            pace(UP+2*i,0,1); plane(2,i)
            u_v[0]=nt(hb_v[...],wi_v[part(c0,UC),:])
            def two(k):
                for b in range(2):
                    ci=c0+2*k+b
                    cc=part(ci,UC)
                    nx=part(jnp.minimum(ci+1,c0+CH//UC-1),UC)
                    bias_u=b_ref[0:1,part(ci+O1//UC,UC)]
                    for t in range(NT):
                        rows=pl.ds(t*RT,RT)
                        u_v[1-b,rows,:]=nt(hb_v[rows,:],wi_v[nx,:])
                        u=u_v[b,rows,:]+bias_u
                        cdf=0.5+0.5*lax.erf(u*(1.0/math.sqrt(2.0)))
                        act_v[rows,cc]=(u*cdf).astype(BF)
                        slope_v[rows,cc]=(cdf+u*(jnp.exp2(u*u*(-0.5*LOG2E))*(1.0/math.sqrt(2.0*math.pi)))).astype(BF)
                @pl.when(k==0)
                def _(): pace(UP+2*i+1,0,1)
            loop(CH//UC//2,two)
        for i in range(4): up(i)
        DN=UP+8
        def down(i):
            pace(DN+NT*i,0,1); plane(3,i)
            r=part(order[i],DC)
            def tile(t):
                rows=part(t,RT)
                f_v[rows,r]=nt(act_v[rows,:],wd_v[r,:])
                @pl.when(t<NT-1)
                def _(): pace(DN+NT*i+1,t,NT-1)
            loop(NT,tile)
        for i in range(4): down(i)
        loads[1].wait()
        cot_v=wo_v; ov=x_v; dcT_v=ctx_v
        QR=RT//4
        ga_v[...]=jnp.zeros_like(ga_v); gb_v[...]=jnp.zeros_like(gb_v)
        def tally(ref,i,v):
            at=pl.ds(pl.multiple_of(i*8,8),8)
            ref[at,:]+=jnp.sum(v.reshape(v.shape[0]//8,8,v.shape[1]),axis=0)
        def second(t,c,p):
            rows=pl.ds(pl.multiple_of(t*RT+c*QR,QR),QR); rb=part(c,QR)
            h1=n1_v[rows,:]*row(OG1)+row(OC1)
            n2,r2=ln(h1+(f_v[rows,:]+row(O2)))
            ov[rows,:]=(n2*row(OG2)+row(OC2)).astype(BF)
            dy=cot_v[rows,:].astype(F32)
            tally(gb_v,0,dy*n2); tally(gb_v,1,dy)
            e=dy*row(OG2)
            dp2=r2*(e-jnp.mean(e,axis=-1,keepdims=True)-n2*jnp.mean(e*n2,axis=-1,keepdims=True))
            dfb=dp2.astype(BF)
            tally(gb_v,2,dfb.astype(F32))
            acc_v[p,rb,:]=dp2
            df_v[p,rb,:]=dfb
        def first(t,c,p):
            rows=pl.ds(pl.multiple_of(t*RT+c*QR,QR),QR); rb=part(c,QR)
            dh1=acc_v[p,rb,:]
            nrm1=n1_v[rows,:]
            tally(gb_v,3,dh1*nrm1); tally(gb_v,4,dh1)
            e=dh1*row(OG1)
            dp1=r1_v[rows,0:1]*(e-jnp.mean(e,axis=-1,keepdims=True)-nrm1*jnp.mean(e*nrm1,axis=-1,keepdims=True))
            f_v[rows,:]=dp1
            da=dp1.astype(BF)
            tally(gb_v,5,da.astype(F32))
            hb_v[rows,:]=da
        loop(4,lambda c: second(0,c,0))
        for t in range(NT):
            p=t%2
            rows=pl.ds(t*RT,RT)
            pltpu.make_async_copy(ov.at[rows],out_o.at[rows],osem.at[2]).start()
            def middle(c):
                cc=part(c,CH)
                du=(nn(df_v[p],wd_v[:,cc])*slope_v[rows,cc].astype(F32)).astype(BF)
                if t>0: first(t-1,c,1-p)
                if t<NT-1: second(t+1,c,1-p)
                tally(ga_v,c,du.astype(F32))
                acc_v[p]+=nn(du,wi_v[cc,:])
            loop(NC,middle)
            if t>0:
                back=pl.ds((t-1)*RT,RT)
                pltpu.make_async_copy(f_v.at[back],dp1_o.at[back],osem.at[3]).start()
        def closing(c):
            first(NT-1,c,(NT-1)%2)
            dcT_v[part(c,RT),0:(NT-1)*RT]=nt(won_v[part(c,RT),:],hb_v[0:(NT-1)*RT,:]).astype(BF)
        loop(4,closing)
        pltpu.make_async_copy(f_v.at[pl.ds((NT-1)*RT,RT)],dp1_o.at[pl.ds((NT-1)*RT,RT)],osem.at[3]).start()
        def last(c): dcT_v[part(c,RT),(NT-1)*RT:]=nt(won_v[part(c,RT),:],hb_v[(NT-1)*RT:,:]).astype(BF)
        loop(4,last)
        def put(o,v):
            for k in range(v.shape[1]//128):
                g_ref[o//128+k:o//128+k+1,:]=v[:,k*128:(k+1)*128]
        for i,at in enumerate((OG2,OC2,O2,OG1,OC1,OO)):
            put(at,jnp.sum(gb_v[8*i:8*i+8,:],axis=0,keepdims=True))
        for c in range(NC): put(O1+c*CH,jnp.sum(ga_v[8*c:8*c+8,:],axis=0,keepdims=True))
        cd=pltpu.make_async_copy(dcT_v,dcT_o,osem.at[4]); cd.start()
        if comm:
            for m in (0,2,3): g.sends_done(m)
        pltpu.make_async_copy(ov,out_o,osem.at[2]).wait()
        pltpu.make_async_copy(f_v,dp1_o,osem.at[3]).wait()
        cd.wait()
    V=pltpu.VMEM
    scr=[V((T,D),BF),V((T,D),BF),V((D,D),BF),V((D,D),BF),V((FF,D),BF),V((D,FF),BF),V((T,D),F32),V((T,128),F32),
        V((T,D),BF),V((T,FF),BF),V((T,FF),BF),V((T,D),F32),V((2,T,UC),F32),V((2,RT,D),F32),V((2,RT,D),BF),V((8*NC,CH),F32),V((48,D),F32),DMA((11,)),DMA((QC,)),DMA((2,S)),DMA((5,))]
    if comm: scr+=[V((mats[2]["R"],mats[2]["L"]),BF)]+comm_scratch(n)
    out=pl.pallas_call(kernel,
        out_shape=[SDS((3*D,T),BF),SDS((D,T),BF),SDS((H,S,SEQ,SEQ),BF),SDS((T,D),BF),SDS((T,D),F32),SDS((D,T),BF),SDS((12*D//128,128),F32)]+full_shapes(mats[:1],ndp,nfs),
        in_specs=[ANY,ANY,VM,VM,VM]+[ANY,ANY,VM if comm else ANY,ANY],out_specs=[ANY]*6+[VM]+([ANY] if comm else []),scratch_shapes=scr,
        compiler_params=comm_params(mats,cid),name="forward")(x,cot,bias,seg,pad,*sources)
    return out[:7],(out[7] if comm else sources[0])

STEP=5
decay_first=0.5
decay_second=0.5
adam_eps=1e-08
step_rate=0.4
NB=12
BS=32
LATE=2*D//128
EARLY=10*D//128
exact=lax.Precision.HIGHEST

def dot_exact(a,b,ca,cb):
    return lax.dot_general(a,b,(((ca,),(cb,)),((),())),precision=exact,preferred_element_type=F32)

class Reduce:
    def __init__(self,src,plane_buf,z_buf,ssem,psem,zsem):
        self.src,self.pb,self.zb,self.ssem,self.psem,self.zsem=src,plane_buf,z_buf,ssem,psem,zsem
        dp=lax.axis_index("dp"); self.x=lax.axis_index("fsdp")
        self.z=dp//4; self.y=(dp//2)%2; self.c=dp%2
        self.me=self.y*4+self.c*2+self.x
    def plane_peer(self,r):
        def flip(a,b): return 1-a if b else a
        return (self.z*4+flip(self.y,r&4)*2+flip(self.c,r&2),flip(self.x,r&1))
    def z_peer(self,r):
        hi,lo=self.z//2,self.z%2
        z=(1-hi if r&2 else hi)*2+(1-lo if r&1 else lo)
        return (z*4+self.y*2+self.c,self.x)
    def barrier(self):
        bar=pltpu.get_barrier_semaphore()
        for r in range(1,8): pl.semaphore_signal(bar,inc=1,device_id=self.plane_peer(r),device_id_type=MESH)
        for r in range(1,4): pl.semaphore_signal(bar,inc=1,device_id=self.z_peer(r),device_id_type=MESH)
        pl.semaphore_wait(bar,10)
    def copies(self,stage):
        buf,sem,idx=(self.pb,self.psem,self.me) if stage==0 else (self.zb,self.zsem,self.z)
        peers=[self.plane_peer(r) for r in range(1,8)] if stage==0 else [self.z_peer(r) for r in range(1,4)]
        return [pltpu.make_async_remote_copy(self.src if stage==0 else self.zb.at[idx],buf.at[idx],self.ssem.at[stage*7+i],sem.at[idx],
            device_id=p,device_id_type=MESH) for i,p in enumerate(peers)]
    def start(self):
        for c in self.copies(0): c.start()
    def gather(self,stage):
        buf,sem,idx,k=(self.pb,self.psem,self.me,8) if stage==0 else (self.zb,self.zsem,self.z,NZ)
        for q in range(k):
            @pl.when(q!=idx)
            def _(): pltpu.make_async_copy(buf.at[q],buf.at[q],sem.at[q]).wait()
    def middle(self):
        self.gather(0)
        self.pb[self.me]=self.src[...]
        tot=self.pb[0]
        for q in range(1,8): tot=tot+self.pb[q]
        self.zb[self.z]=tot
        for c in self.copies(1): c.start()
    def end(self):
        self.gather(1)
        tot=self.zb[0]
        for q in range(1,NZ): tot=tot+self.zb[q]
        return tot
    def finish(self):
        for st in (0,1):
            for c in self.copies(st): c.wait_send()

def reduce_scratch(rows):
    return [pltpu.VMEM((rows,128),F32),pltpu.VMEM((8,rows,128),F32),pltpu.VMEM((NZ,rows,128),F32),DMA((10,)),DMA((8,)),DMA((NZ,))]

def fold_tables(n):
    i=lax.broadcasted_iota(jnp.int32,(32*n,8*n),0); j=lax.broadcasted_iota(jnp.int32,(32*n,8*n),1)
    sel=jnp.where(i//4==j,1.0,0.0)
    i=lax.broadcasted_iota(jnp.int32,(32*n,128),0); j=lax.broadcasted_iota(jnp.int32,(32*n,128),1)
    mask=jnp.where(i%4==j//32,1.0,0.0)
    i=lax.broadcasted_iota(jnp.int32,(128,32),0); j=lax.broadcasted_iota(jnp.int32,(128,32),1)
    fold=jnp.where(i%32==j,1.0,0.0)
    return sel,mask,fold

def attn_tail(p,qkvT,ctxT,dcT,dp1,wqkvT,update,cid):
    S=p.shape[1]; T=S*SEQ; G=2; NI=H//G; R=G*HD; RT=256; NT=T//RT
    up=update is not None
    def kernel(*refs):
        p_h,qkv_h,c_h,d_h,dp_h,w_h=refs[:6]; o=6
        if up: g_in,mf_h,ms_h,bl_h,br_h=refs[o:o+5]; o+=5
        if up: ig_o,gs_o,st_v=refs[o:o+3]; o+=3
        else: ig_o,gl_o=refs[o:o+2]; o+=2
        pb,qkv_v,c_v,d_v,dp_v,w_v,ig_v,ones_v,psem,lsem,wsem,osem=refs[o:o+12]; o+=12
        if up:
            early_refs=refs[o:o+6]; late_refs=refs[o+6:o+12]; o+=12
            xs,xr=refs[o:o+2]; o+=2
            early=Reduce(*early_refs); late=Reduce(*late_refs); gl=late_refs[0]
        else: gl=gl_o
        def p_load(i): return pltpu.make_async_copy(p_h.at[part(i,G)],pb.at[lax.rem(i,2)],psem.at[lax.rem(i,2)])
        def chunk(i):
            out=[pltpu.make_async_copy(qkv_h.at[part(i+k*NI,R)],qkv_v.at[part(i+k*NI,R)],lsem.at[i,k]) for k in range(3)]
            return out+[pltpu.make_async_copy(a.at[part(i,R)],b.at[part(i,R)],lsem.at[i,3+k]) for k,(a,b) in enumerate(((d_h,d_v),(c_h,c_v)))]
        p_load(jnp.int32(0)).start()
        def begin(i):
            for c in chunk(i): c.start()
        loop(NI,begin)
        wl=pltpu.make_async_copy(w_h,w_v,wsem.at[0]); wl.start()
        dl=pltpu.make_async_copy(dp_h,dp_v,wsem.at[1]); dl.start()
        ones_v[...]=jnp.ones_like(ones_v)
        if up:
            early.barrier()
            early_refs[0][...]=g_in[LATE:,:]
            early.start()
            x=early.x
            states=[]
            for k,a in enumerate((mf_h,ms_h,bl_h,br_h)):
                states.append(pltpu.make_async_remote_copy(a.at[0],st_v.at[k,x],xs.at[k],xr.at[k],device_id=early.plane_peer(1),device_id_type=MESH))
                states.append(pltpu.make_async_copy(a.at[0],st_v.at[k,x],xs.at[4+k]))
            for c in states: c.start()
        def back(i):
            @pl.when(i<NI-1)
            def _(): p_load(i+1).start()
            for c in chunk(i): c.wait()
            p_load(i).wait()
            b=lax.rem(i,2)
            for s in range(S):
                cols=pl.ds(s*SEQ,SEQ)
                for h in range(G):
                    r=part(i*G+h,HD); rk=part(i*G+h+H,HD); rv=part(i*G+h+2*H,HD)
                    d=d_v[r,cols]
                    pr=pb[b,h,s]
                    q=qkv_v[r,cols]; k=qkv_v[rk,cols]; v=qkv_v[rv,cols]
                    delta=jnp.sum(d.astype(F32)*c_v[r,cols].astype(F32),axis=0,keepdims=True)
                    ds=(pr.astype(F32)*(tn(v,d)-delta)).astype(BF)
                    qkv_v[rv,cols]=nt(d,pr).astype(BF)
                    qkv_v[rk,cols]=(nt(q,ds)*0.125).astype(BF)
                    qkv_v[r,cols]=(nn(k,ds)*0.125).astype(BF)
            gl[pl.ds(i,1),:]=nt(ones_v[...],qkv_v[part(i,R),:])[0:1,:]
            gl[pl.ds(NI+i,1),:]=nt(ones_v[...],qkv_v[part(i+2*NI,R),:])[0:1,:]
            if up:
                @pl.when(i==3)
                def _(): early.middle()
        loop(NI,back)
        if up: late.start()
        wl.wait(); dl.wait()
        def finish(t):
            cols=part(t,RT)
            acc=dp_v[cols,:]
            for k in range(3):
                acc=acc+tn(qkv_v[k*D:(k+1)*D,cols],w_v[k*D:(k+1)*D,:])
            ig_v[cols,:]=acc.astype(BF)
            pltpu.make_async_copy(ig_v.at[cols],ig_o.at[cols],osem.at[0]).start()
            if up:
                @pl.when(t==1)
                def _(): late.middle()
        loop(NT,finish)
        if up:
            for c in states: c.wait()
            gs_o[LATE:,:]=early.end()
            gs_o[0:LATE,:]=late.end()
            early.finish(); late.finish()
        pltpu.make_async_copy(ig_v,ig_o,osem.at[0]).wait()
    V=pltpu.VMEM
    scr=[V((2,G,S,SEQ,SEQ),BF),V((3*D,T),BF),V((D,T),BF),V((D,T),BF),V((T,D),F32),V((3*D,D),BF),V((T,D),BF),V((8,T),BF),DMA((2,)),DMA((NI,5)),DMA((2,)),DMA((1,))]
    ins=[p,qkvT,ctxT,dcT,dp1,wqkvT]; specs=[ANY]*6
    outs=[SDS((T,D),BF)]; ospecs=[ANY]
    if up:
        g,mf,ms,bl,br=update
        ins+=[g,mf,ms,bl,br]; specs+=[VM]+[ANY]*4
        outs+=[SDS((NB*8,128),F32),SDS((4,2)+mf.shape[1:],F32)]; ospecs+=[VM,VM]
        scr+=reduce_scratch(EARLY)+reduce_scratch(LATE)+[DMA((8,)),DMA((4,))]
    else:
        outs+=[SDS((LATE,128),F32)]; ospecs+=[VM]
    return pl.pallas_call(kernel,out_shape=outs,in_specs=specs,out_specs=ospecs,scratch_shapes=scr,
        compiler_params=comm_params([1] if up else [],cid),name="attn_tail")(*ins)

def update_step(out,ig,grads,state,bias,owners):
    cap=state.shape[2]; NP=4
    def kernel(out_h,ig_h,g_in,st_v,b_in,own_s,out_o,ig_o,bg_o,mf_o,ms_o,bn_o,bl_o,m_st,v_st,v,sem):
        rows=out.shape[0]//NP
        def moves(down):
            return [pltpu.make_async_copy(*((v.at[k,pl.ds(i*rows,rows)],b.at[pl.ds(i*rows,rows)]) if down else (a.at[pl.ds(i*rows,rows)],v.at[k,pl.ds(i*rows,rows)])),sem.at[down,k,i])
                for k,(a,b) in enumerate(((out_h,out_o),(ig_h,ig_o))) for i in range(NP)]
        for c in moves(0): c.start()
        x=lax.axis_index("fsdp")
        owner=[own_s[b] for b in range(NB)]
        rank=[]
        for b in range(NB):
            r=jnp.int32(0)
            for e in range(b): r=r+jnp.where(owner[e]==owner[b],1,0)
            rank.append(r)
        def adam(b0,n,tiles):
            sel,mask,fold=fold_tables(n)
            gs=dot_exact(dot_exact(sel,tiles,1,0)*mask,fold,1,0)
            outs=[]
            for j in range(n):
                b=b0+j
                at=jnp.minimum(rank[b],st_v.shape[2]-1)
                first,second,left,right=[st_v[k,owner[b],at] for k in range(4)]
                t=dot_exact(dot_exact(left,gs[j*BS:(j+1)*BS,:],0,0),right,1,0)
                m=decay_first*first+(1.0-decay_first)*t
                v=decay_second*second+(1.0-decay_second)*t*t
                m_st[b]=m; v_st[b]=v
                un=(m/(1.0-decay_first**STEP))/(jnp.sqrt(v/(1.0-decay_second**STEP))+adam_eps)
                outs.append(dot_exact(dot_exact(left,un,1,0),right,1,1))
            back_=dot_exact(jnp.concatenate(outs,0),fold,1,1)*mask
            new=b_in[8*b0:8*(b0+n),:]-step_rate*dot_exact(sel,back_,0,0)
            bg_o[8*b0:8*(b0+n),:]=tiles
            bn_o[8*b0:8*(b0+n),:]=new
            bl_o[8*b0:8*(b0+n),:]=new.astype(BF)
        for c,d in zip(moves(0),moves(1)): c.wait(); d.start()
        adam(0,NB,g_in[...])
        for c in range(mf_o.shape[1]):
            at=jnp.int32(0); hit=jnp.int32(0)
            for b in range(NB):
                here=(owner[b]==x)&(rank[b]==c)
                at=at+jnp.where(here,b,0); hit=hit+jnp.where(here,1,0)
            at=jnp.minimum(at,NB-1)
            filled=hit.astype(F32)
            mf_o[0,c]=m_st[at]*filled
            ms_o[0,c]=v_st[at]*filled
        for c in moves(1): c.wait()
    m=SDS((1,cap,BS,BS),F32)
    return pl.pallas_call(kernel,
        out_shape=[SDS(out.shape,BF),SDS(ig.shape,BF),SDS((NB*8,128),F32),m,m,SDS((NB*8,128),F32),SDS((NB*8,128),BF)],
        in_specs=[ANY,ANY,VM,VM,VM,pl.BlockSpec(memory_space=pltpu.SMEM)],out_specs=[ANY,ANY]+[VM]*5,
        scratch_shapes=[pltpu.VMEM((NB,BS,BS),F32),pltpu.VMEM((NB,BS,BS),F32),pltpu.VMEM((2,)+out.shape,BF),DMA((2,2,NP))],
        compiler_params=pltpu.CompilerParams(vmem_limit_bytes=VMEM_CAP),name="update")(out,ig,grads,state,bias,owners)


def placement_table(owners, owner_count, capacity):
    block_count = owners.shape[0]
    index_b = jnp.arange(block_count, dtype=jnp.int32)
    same_owner = owners[:, None] == owners[None, :]
    earlier = index_b[None, :] < index_b[:, None]
    rank_of = jnp.sum((same_owner & earlier).astype(jnp.int32), axis=1)
    owner_hit = owners[None, None, :] == jnp.arange(owner_count, dtype=jnp.int32)[:, None, None]
    slot_hit = rank_of[None, None, :] == jnp.arange(capacity, dtype=jnp.int32)[None, :, None]
    return (owner_hit & slot_hit).astype(jnp.float32)


def adam_rotated(grad_slots, value_slots, first_old, second_old, left_basis, right_basis, filled):
    turned = jnp.einsum("fcki,fckj->fcij", left_basis, grad_slots, precision=exact)
    turned = jnp.einsum("fcik,fckj->fcij", turned, right_basis, precision=exact)
    first_raw = decay_first * first_old + (1.0 - decay_first) * turned
    second_raw = decay_second * second_old + (1.0 - decay_second) * turned * turned
    normed_step = (
        first_raw
        / (1.0 - decay_first**STEP)
        / (jnp.sqrt(second_raw / (1.0 - decay_second**STEP)) + adam_eps)
    )
    restored = jnp.einsum("fcik,fckj->fcij", left_basis, normed_step, precision=exact)
    restored = jnp.einsum("fcik,fcjk->fcij", restored, right_basis, precision=exact)
    value_new = value_slots - step_rate * restored
    return (first_raw * filled, second_raw * filled, value_new * filled)


def body(
    acts,
    cotangent,
    seg_ids,
    pad_mask,
    qkv_weight,
    out_weight,
    in_weight,
    down_weight,
    biases,
    moment_first,
    moment_second,
    basis_left,
    basis_right,
    owners,
):
    ndp, nfs = lax.axis_size("dp"), lax.axis_size("fsdp")
    shards = (qkv_weight.T, out_weight.T, in_weight, down_weight.T)
    slots = acts.shape[0] * acts.shape[1]
    x = acts.reshape(slots * SEQ, D)
    cot = cotangent.reshape(slots * SEQ, D)
    seg = seg_ids.reshape(slots, 1, SEQ)
    pad = pad_mask.reshape(slots, 1, SEQ)
    bias = biases.reshape(1, -1)
    if (ndp, nfs) == (16, 2):
        (qkvT, ctxT, p, out, dp1, dcT, g), wqT = forward(matdesc(), shards, 1, x, cot, bias, seg, pad, ndp, nfs)
        state = (g, moment_first, moment_second, basis_left, basis_right)
        ig, total, state = attn_tail(p, qkvT, ctxT, dcT, dp1, wqT, state, 2)
        out, ig, bg, mf, ms, bn, bl = update_step(out, ig, total, state, biases.reshape(-1, 128), owners)
        return (
            out.reshape(acts.shape),
            ig.reshape(acts.shape),
            bg.reshape(-1),
            mf,
            ms,
            bn.reshape(-1),
            bl.reshape(-1),
        )
    whole = [
        lax.all_gather(lax.all_gather(t, "fsdp", axis=1, tiled=True), "dp", axis=0, tiled=True)
        for t in (shards[0], shards[1], shards[2].T, shards[3])
    ]
    (qkvT, ctxT, p, out, dp1, dcT, g), wqT = forward([], whole, 0, x, cot, bias, seg, pad, ndp, nfs)
    ig, gl = attn_tail(p, qkvT, ctxT, dcT, dp1, wqT, None, 0)
    outputs, input_grads = out.reshape(acts.shape), ig.reshape(acts.shape)
    grad_total = jnp.concatenate([gl, g[LATE:]], 0).reshape(-1)
    block_count = owners.shape[0]
    block_side = moment_first.shape[2]
    slot_table = placement_table(owners, lax.axis_size("fsdp"), moment_first.shape[1])
    grad_slots = jnp.einsum(
        "fcb,bij->fcij",
        slot_table,
        grad_total.reshape(block_count, block_side, block_side),
        precision=exact,
    )
    summed = lax.psum(grad_slots.astype(jnp.bfloat16), "dp")
    owned_grad = lax.psum_scatter(summed, "fsdp", scatter_dimension=0, tiled=True).astype(
        jnp.float32
    )
    own_table = lax.dynamic_slice_in_dim(slot_table, lax.axis_index("fsdp"), 1, 0)
    value_slots = jnp.einsum(
        "fcb,bij->fcij",
        own_table,
        biases.reshape(block_count, block_side, block_side),
        precision=exact,
    )
    filled = jnp.sum(own_table, axis=2)[:, :, None, None]
    first_new, second_new, value_new = adam_rotated(
        owned_grad, value_slots, moment_first, moment_second, basis_left, basis_right, filled
    )
    shared_grad, shared_value = (
        lax.all_gather(owned_grad, "fsdp", axis=0, tiled=True),
        lax.all_gather(value_new, "fsdp", axis=0, tiled=True),
    )
    bias_grad = jnp.einsum("fcb,fcij->bij", slot_table, shared_grad, precision=exact).reshape(
        biases.shape[0]
    )
    bias_new = jnp.einsum("fcb,fcij->bij", slot_table, shared_value, precision=exact).reshape(
        biases.shape[0]
    )
    return (
        outputs,
        input_grads,
        bias_grad,
        first_new,
        second_new,
        bias_new,
        bias_new.astype(jnp.bfloat16),
    )


def solution(mesh):
    placed = (
        P(None, ("dp", "fsdp"), None, None),
        P(None, ("dp", "fsdp"), None, None),
        P(None, ("dp", "fsdp"), None),
        P(None, ("dp", "fsdp"), None),
        P("fsdp", "dp"),
        P("fsdp", "dp"),
        P("fsdp", "dp"),
        P("fsdp", "dp"),
        P(),
        P("fsdp", None, None, None),
        P("fsdp", None, None, None),
        P("fsdp", None, None, None),
        P("fsdp", None, None, None),
        P(),
    )
    return jax.shard_map(
        body,
        mesh=mesh,
        in_specs=placed,
        out_specs=(
            P(None, ("dp", "fsdp"), None, None),
            P(None, ("dp", "fsdp"), None, None),
            P(),
            P("fsdp", None, None, None),
            P("fsdp", None, None, None),
            P(),
            P(),
        ),
        check_vma=False,
    )
```

```python
import functools
import math

import jax
import jax.numpy as jnp
from jax import lax
from jax.experimental import pallas as pl
from jax.experimental.pallas import tpu as pltpu
from jax.sharding import PartitionSpec as P

MESH=pl.DeviceIdType.MESH
NZ=4

def split_rows(R,L,a,b,unit=16):
    out=[];r=0
    for kind,n in (("A1",a),("A2",a),("B1",b),("B2",b)):
        if n: out.append((kind,r,n,0,L)); r+=n
    assert r==R,(r,R)
    return out
def split_lanes(R,L,a,b):
    out=[];l=0
    for kind,n in (("A1",a),("A2",a),("B1",b),("B2",b)):
        if n: out.append((kind,0,R,l,n)); l+=n
    assert l==L
    return out

EVENTS=[(dz,rx,ry) for dz in range(1-NZ,NZ) for rx in (0,1) for ry in (0,1) if (dz,rx,ry)!=(0,0,0)]
EVENTS.sort(key=lambda e:(abs(e[0])+e[1]+e[2], e[1]+e[2], -e[0]))
NEV=len(EVENTS)

def pick(i,values):
    out=jnp.int32(values[0])
    for j in range(1,len(values)):
        out=jnp.where(i==j,jnp.int32(values[j]),out)
    return out

def sends(kind,z,dz,rx,ry):
    plane=(rx==0)&(ry==0)
    turn_y=(kind[1]=="1")&(rx==1)&(ry==0)
    turn_x=(kind[1]=="2")&(rx==0)&(ry==1)
    if kind[0]=="A":
        return {"zp":plane&(dz>=0)&(z<NZ-1),"zm":plane&(dz<=0)&(z>0),"x":plane|turn_x,"y":plane|turn_y}
    return {"zp":(dz>=0)&(z<NZ-1),"zm":(dz<=0)&(z>0),"x":(dz==0)&(plane|turn_x),"y":(dz==0)&(plane|turn_y)}

WAYS=("x","y","zp","zm","s")

def region(total, N, K):
    for lanes in range(128,K+1,128):
        if total%lanes==0:
            rows=total//lanes
            if rows%16==0 and rows<=N: return rows,lanes
    raise ValueError(total)

class Gather:
    def __init__(self, mats, shards, fulls, local_sem, send_sem, recv_sem, sib_sem):
        self.mats=mats; self.sh=shards; self.full=fulls
        self.lsem,self.ssem,self.rsem,self.bsem=local_sem,send_sem,recv_sem,sib_sem
        dp=lax.axis_index("dp"); x=lax.axis_index("fsdp")
        self.dp,self.x=dp,x
        self.z=dp//4; self.y=(dp//2)%2; self.c=dp%2
        self.dev={"x":(dp,1-x),"y":(self.z*4+(1-self.y)*2+self.c,x),"zp":(dp+4,x),"zm":(dp-4,x),"s":(self.z*4+self.y*2+1-self.c,x)}
    def barrier(self):
        bar=pltpu.get_barrier_semaphore()
        for d in ("x","y","s"):
            pl.semaphore_signal(bar,inc=1,device_id=self.dev[d],device_id_type=MESH)
        @pl.when(self.z<NZ-1)
        def _(): pl.semaphore_signal(bar,inc=1,device_id=self.dev["zp"],device_id_type=MESH)
        @pl.when(self.z>0)
        def _(): pl.semaphore_signal(bar,inc=1,device_id=self.dev["zm"],device_id_type=MESH)
        inner=(self.z>0)&(self.z<NZ-1)
        @pl.when(inner)
        def _(): pl.semaphore_wait(bar,5)
        @pl.when(jnp.logical_not(inner))
        def _(): pl.semaphore_wait(bar,4)
    def place(self,m,k,dz,rx,ry):
        M=self.mats[m]; kind,r0,nr,l0,nl=M["classes"][k]
        y=self.y+ry-2*self.y*ry
        x=self.x+rx-2*self.x*rx
        src=(self.z-dz)*4+y*2+self.c
        return self.full[m].at[pl.ds(pl.multiple_of(src*M["R"]+r0,16),nr), pl.ds(pl.multiple_of(x*M["L"]+l0,128),nl)]
    def forward(self,m,k,dz,rx,ry,src):
        kind=self.mats[m]["classes"][k][0]
        dst=self.place(m,k,dz,rx,ry)
        def rel(a,b,c): return (a+NZ-1)*4+b*2+c
        child={"x":rel(dz,1,ry),"y":rel(dz,rx,1),"zp":rel(dz+1,rx,ry),"zm":rel(dz-1,rx,ry)}
        for d,cond in sends(kind,self.z,dz,rx,ry).items():
            def go(d=d):
                pltpu.make_async_remote_copy(src,dst,self.ssem.at[m,WAYS.index(d)],self.rsem.at[m,k,child[d]],
                    device_id=self.dev[d],device_id_type=MESH).start()
            if cond is True: go()
            elif cond is not False: pl.when(cond)(go)
        pltpu.make_async_remote_copy(src,dst,self.ssem.at[m,4],self.bsem.at[m,self.z-dz],device_id=self.dev["s"],device_id_type=MESH).start()
    def own(self,m):
        M=self.mats[m]
        for k,(kind,r0,nr,l0,nl) in enumerate(M["classes"]):
            self.forward(m,k,0,0,0,self.sh[m].at[pl.ds(r0,nr),pl.ds(l0,nl)])
        full=self.full[m].at[pl.ds(pl.multiple_of(self.dp*M["R"],16),M["R"]),pl.ds(pl.multiple_of(self.x*M["L"],128),M["L"])]
        pltpu.make_async_copy(self.sh[m],full,self.lsem.at[m]).start()
    def step(self,e,ms):
        code=pick(e,[(v[0]+NZ-1)*4+v[1]*2+v[2] for v in EVENTS])
        dz=code//4-(NZ-1); rx=(code//2)%2; ry=code%2
        src=self.z-dz
        @pl.when((src>=0)&(src<=NZ-1))
        def _():
            for m in ms:
                for k in range(len(self.mats[m]["classes"])):
                    ref=self.place(m,k,dz,rx,ry)
                    pltpu.make_async_copy(ref,ref,self.rsem.at[m,k,(dz+NZ-1)*4+rx*2+ry]).wait()
                    self.forward(m,k,dz,rx,ry,ref)
    def wait_bytes(self,m,total,sem):
        N,K=self.full[m].shape
        r,l=region(total,N,K)
        ref=self.full[m].at[pl.ds(0,r),pl.ds(0,l)]
        pltpu.make_async_copy(ref,ref,sem).wait()
    def own_done(self,m):
        own=self.sh[m]
        pltpu.make_async_copy(own,own,self.lsem.at[m]).wait()
    def plane_done(self,m,z0):
        N,K=self.full[m].shape
        self.wait_bytes(m,N*K//2//NZ,self.bsem.at[m,z0])
    def sends_done(self,m):
        M=self.mats[m]; N,K=self.full[m].shape
        def total(d,z):
            t=0
            for kind,r0,nr,l0,nl in M["classes"]:
                for dz,rx,ry in [(0,0,0)]+EVENTS:
                    if 0<=z-dz<=NZ-1 and sends(kind,z,dz,rx,ry)[d]: t+=nr*nl
            return t
        for d in ("x","y"):
            self.wait_bytes(m,total(d,0),self.ssem.at[m,WAYS.index(d)])
        for d in ("zp","zm"):
            for z in range(NZ):
                if total(d,z):
                    pl.when(self.z==z)(functools.partial(self.wait_bytes,m,total(d,z),self.ssem.at[m,WAYS.index(d)]))
        self.wait_bytes(m,N*K//2,self.ssem.at[m,4])
    def finish(self,m):
        self.own_done(m)
        for z in range(NZ): self.plane_done(m,z)
        self.sends_done(m)

def comm_scratch(n):
    return [pltpu.SemaphoreType.DMA((n,)),pltpu.SemaphoreType.DMA((n,5)),pltpu.SemaphoreType.DMA((n,4,8*NZ-4)),pltpu.SemaphoreType.DMA((n,NZ))] if n else []

def matdesc(beta=True):
    if beta:
        return [dict(R=192,L=512,classes=split_rows(192,512,80,16)),dict(R=64,L=512,classes=split_rows(64,512,32,0)),
            dict(R=256,L=512,classes=split_rows(256,512,96,32)),dict(R=64,L=2048,classes=split_lanes(64,2048,768,256))]
    return [dict(R=192,L=512,classes=split_rows(192,512,96,0)),dict(R=64,L=512,classes=split_rows(64,512,32,0)),
            dict(R=256,L=512,classes=split_rows(256,512,128,0)),dict(R=64,L=2048,classes=split_lanes(64,2048,1024,0))]
BF=jnp.bfloat16
F32=jnp.float32
D=1024
H=16
HD=64
FF=4096
SEQ=512
LOG2E=1.4426950408889634
VMEM_CAP=60<<20
ANY=pl.BlockSpec(memory_space=pl.ANY)
VM=pl.BlockSpec(memory_space=pltpu.VMEM)
SDS=jax.ShapeDtypeStruct
DMA=pltpu.SemaphoreType.DMA

def nn(a,b): return lax.dot_general(a,b,(((1,),(0,)),((),())),preferred_element_type=F32)
def nt(a,b): return lax.dot_general(a,b,(((1,),(1,)),((),())),preferred_element_type=F32)
def tn(a,b): return lax.dot_general(a,b,(((0,),(0,)),((),())),preferred_element_type=F32)
def part(i,n): return pl.ds(pl.multiple_of(i*n,n),n)
def loop(n,fn):
    def st(i,c):
        fn(i); return c
    lax.fori_loop(0,n,st,0)

OQ,OV,OO,O1,O2,OG1,OC1,OG2,OC2=0,D,2*D,3*D,3*D+FF,4*D+FF,5*D+FF,6*D+FF,7*D+FF

def column(row):
    return jnp.transpose(jnp.broadcast_to(row,(8,row.shape[1])))

class Quiet:
    def step(self,e,ms): pass

def comm_params(mats,cid,**kw):
    if mats: kw.update(collective_id=cid,has_side_effects=True)
    return pltpu.CompilerParams(vmem_limit_bytes=VMEM_CAP,**kw)

def full_shapes(mats,dp,fs):
    return [SDS((M["R"]*dp,M["L"]*fs),BF) for M in mats]

def ln(v):
    c=v-jnp.mean(v,axis=-1,keepdims=True)
    r=lax.rsqrt(jnp.mean(c*c,axis=-1,keepdims=True)+1e-12)
    return c*r,r

PACE=[13, 17, 17, 29, 31, 34, 37, 44, 44, 45, 45, 46, 46, 57, 58, 58, 58, 59, 61, 61, 61, 65, 70, 70, 70, 75, 75, 76, 78, 85, 85, 85, 85, 85, 88, 91, 91, 93, 97, 98, 101, 101, 103, 104, 106, 106, 106, 108, 108, 108, 108, 108, 108, 108, 108, 108]
OWN={1: 17, 2: 44, 3: 70}

def forward(mats,sources,cid,x,cot,bias,seg,pad,ndp,nfs):
    comm=bool(mats); n=len(mats); S=x.shape[0]//SEQ; T=x.shape[0]
    RT=256; NT=T//RT; CH=1024; NC=FF//CH; UC=256; DC=D//4; QC=3*D//4//256

    def kernel(*refs):
        x_h,cot_h,b_ref,seg_ref,pad_ref=refs[:5]
        src=refs[5:9]; o=9
        qkv_o,ctxT_o,p_o,out_o,dp1_o,dcT_o,g_ref=refs[o:o+7]; o+=7
        if comm: wq_h=refs[o]; o+=1
        else: wq_h=src[0]
        x_v,ctx_v,wo_v,won_v,wi_v,wd_v,n1_v,r1_v,hb_v,act_v,slope_v,f_v,u_v,acc_v,df_v,ga_v,gb_v,lsem,wsem,psem,osem=refs[o:o+21]; o+=21
        loads=[pltpu.make_async_copy(x_h,x_v,lsem.at[0]),pltpu.make_async_copy(cot_h,wo_v,lsem.at[1])]
        loads[0].start()
        if not comm:
            whole={m:pltpu.make_async_copy(src[m],v,lsem.at[1+m]) for m,v in ((1,wo_v),(2,wi_v),(3,wd_v))}
            for c in whole.values(): c.start()
        if comm:
            in_t=refs[o]; sems=refs[o+1:]
            g=Gather(mats,(src[0],src[1],in_t,src[3]),(wq_h,wo_v,wi_v,wd_v),*sems); g.barrier(); g.own(0)
            eye=jnp.where(lax.broadcasted_iota(jnp.int32,(256,256),0)==lax.broadcasted_iota(jnp.int32,(256,256),1),1.0,0.0).astype(BF)
            in_t[...]=nt(eye,src[2][...]).astype(BF)
            z=g.z
            order=[z,jnp.where(z==3,2,z+1),jnp.where(z==0,2,jnp.where(z==3,1,z-1)),jnp.where((z==0)|(z==1),3,0)]
        else: order=[0,1,2,3]
        def steps(m,a,b):
            def one(e,carry):
                g.step(e,[m])
                for k,at in OWN.items():
                    if (at-1)//NEV==m:
                        @pl.when(e==(at-1)%NEV)
                        def _(): g.own(k)
                return carry
            lax.fori_loop(a,b,one,0)
        def pace(op,i,count):
            if not comm: return
            starts=[PACE[j-1] if j else 0 for j in range(op,op+count)]; ends=PACE[op:op+count]
            a,b=pick(i,starts),pick(i,ends)
            for m in range(4):
                if starts[0]<NEV*(m+1) and ends[-1]>NEV*m and starts[0]<ends[-1]:
                    steps(m,jnp.clip(a-NEV*m,0,NEV),jnp.clip(b-NEV*m,0,NEV))
        def plane(m,i):
            if comm:
                if i==0: g.own_done(m)
                g.plane_done(m,order[i])
            elif i==0 and m>0: whole[m].wait()
        def row(o,k=D): return b_ref[0:1,o:o+k]
        n1_v[:,0:8]=column(row(OQ)); n1_v[:,128:136]=jnp.zeros((D,8),F32); n1_v[:,256:264]=column(row(OV))
        for s in range(S):
            seg_r=seg_ref[s]; pad_r=pad_ref[s]
            key_r=jnp.where(pad_r==1,seg_r,-1).astype(F32)
            key_c=column(key_r)[:,0:1]
            hit=(key_c==seg_r.astype(F32))|((pad_r==0)&(key_c>=0.0))
            f_v[s*SEQ:(s+1)*SEQ,0:SEQ]=jnp.where(hit,0.0,-1e30)
        def project(i):
            pace(QC*i,0,1); plane(0,i)
            def load(c): return pltpu.make_async_copy(wq_h.at[part(order[i]*QC+c,256)],slope_v.at[part(c,256),2048:3072],wsem.at[c])
            loop(QC,lambda c: load(c).start())
            def chunk(c):
                jj=order[i]*QC+c; j=jj//4; rows=part(jj%4,256); cols=part(j,T)
                load(c).wait()
                acc=nt(slope_v[part(c,256),2048:3072],x_v[...])+n1_v[rows,part(j,128)][:,0:1]
                act_v[rows,cols]=acc.astype(BF)
                pltpu.make_async_copy(act_v.at[rows,cols],qkv_o.at[part(jj,256)],osem.at[0]).start()
                @pl.when(c<QC-1)
                def _(): pace(QC*i+1,c,QC-1)
            loop(QC,chunk)
        loads[0].wait()
        for i in range(4): project(i)
        AT=4*QC
        def attend(h):
            pace(AT,h,H)
            b=lax.rem(h,2)
            def p_copy(i,s): return pltpu.make_async_copy(slope_v.at[part(b,SEQ),s*SEQ:(s+1)*SEQ],p_o.at[i,s],psem.at[b,s])
            @pl.when(h>=2)
            def _():
                for s in range(S): p_copy(h-2,s).wait()
            for s in range(S):
                def at(j): return pl.ds(j*T+s*SEQ,SEQ)
                r=part(h,HD)
                q=act_v[r,at(0)]; k=act_v[r,at(1)]; v=act_v[r,at(2)]
                t=tn(k,q)*(0.125*LOG2E)+f_v[s*SEQ:(s+1)*SEQ,0:SEQ]
                e=jnp.exp2(t-jnp.max(t,axis=0,keepdims=True))
                p=(e*(1.0/jnp.sum(e,axis=0,keepdims=True))).astype(BF)
                slope_v[part(b,SEQ),s*SEQ:(s+1)*SEQ]=p
                hb_v[r,pl.ds(s*SEQ,SEQ)]=nn(v,p).astype(BF)
                p_copy(h,s).start()
        loop(H,attend)
        ct=pltpu.make_async_copy(hb_v,ctxT_o,osem.at[1]); ct.start()
        def turn(i): ctx_v[:,part(i,128)]=jnp.transpose(hb_v[part(i,128),:])
        loop(D//128,turn)
        for i in range(4): plane(1,i)
        def turn2(i): won_v[:,part(i,128)]=jnp.transpose(wo_v[part(i,128),:])
        loop(D//128,turn2)
        if comm: g.sends_done(1)
        loads[1].start()
        pltpu.make_async_copy(act_v.at[:,0:3*T],act_v.at[:,0:3*T],osem.at[0]).wait()
        for b in range(2):
            for s in range(S): pltpu.make_async_copy(slope_v.at[b*SEQ:(b+1)*SEQ,s*SEQ:(s+1)*SEQ],p_o.at[b,s],psem.at[b,s]).wait()
        ct.wait()
        g_ref[...]=jnp.zeros_like(g_ref)
        def join(t):
            pace(AT+H,t,NT)
            rows=part(t,RT)
            br=nn(ctx_v[rows,:],won_v[...])+row(OO)
            nrm,r=ln(x_v[rows,:].astype(F32)+br)
            n1_v[rows,:]=nrm
            r1_v[rows,:]=jnp.broadcast_to(r,(RT,128))
            hb_v[rows,:]=(nrm*row(OG1)+row(OC1)).astype(BF)
        loop(NT,join)
        UP=AT+H+NT
        def up(i):
            c0=order[i]*(CH//UC)
            pace(UP+2*i,0,1); plane(2,i)
            u_v[0]=nt(hb_v[...],wi_v[part(c0,UC),:])
            def two(k):
                for b in range(2):
                    ci=c0+2*k+b
                    cc=part(ci,UC)
                    nx=part(jnp.minimum(ci+1,c0+CH//UC-1),UC)
                    bias_u=b_ref[0:1,part(ci+O1//UC,UC)]
                    for t in range(NT):
                        rows=pl.ds(t*RT,RT)
                        u_v[1-b,rows,:]=nt(hb_v[rows,:],wi_v[nx,:])
                        u=u_v[b,rows,:]+bias_u
                        cdf=0.5+0.5*lax.erf(u*(1.0/math.sqrt(2.0)))
                        act_v[rows,cc]=(u*cdf).astype(BF)
                        slope_v[rows,cc]=(cdf+u*(jnp.exp2(u*u*(-0.5*LOG2E))*(1.0/math.sqrt(2.0*math.pi)))).astype(BF)
                @pl.when(k==0)
                def _(): pace(UP+2*i+1,0,1)
            loop(CH//UC//2,two)
        for i in range(4): up(i)
        DN=UP+8
        def down(i):
            pace(DN+NT*i,0,1); plane(3,i)
            r=part(order[i],DC)
            def tile(t):
                rows=part(t,RT)
                f_v[rows,r]=nt(act_v[rows,:],wd_v[r,:])
                @pl.when(t<NT-1)
                def _(): pace(DN+NT*i+1,t,NT-1)
            loop(NT,tile)
        for i in range(4): down(i)
        loads[1].wait()
        cot_v=wo_v; ov=x_v; dcT_v=ctx_v
        QR=RT//4
        ga_v[...]=jnp.zeros_like(ga_v); gb_v[...]=jnp.zeros_like(gb_v)
        def tally(ref,i,v):
            at=pl.ds(pl.multiple_of(i*8,8),8)
            ref[at,:]+=jnp.sum(v.reshape(v.shape[0]//8,8,v.shape[1]),axis=0)
        def second(t,c,p):
            rows=pl.ds(pl.multiple_of(t*RT+c*QR,QR),QR); rb=part(c,QR)
            h1=n1_v[rows,:]*row(OG1)+row(OC1)
            n2,r2=ln(h1+(f_v[rows,:]+row(O2)))
            ov[rows,:]=(n2*row(OG2)+row(OC2)).astype(BF)
            dy=cot_v[rows,:].astype(F32)
            tally(gb_v,0,dy*n2); tally(gb_v,1,dy)
            e=dy*row(OG2)
            dp2=r2*(e-jnp.mean(e,axis=-1,keepdims=True)-n2*jnp.mean(e*n2,axis=-1,keepdims=True))
            dfb=dp2.astype(BF)
            tally(gb_v,2,dfb.astype(F32))
            acc_v[p,rb,:]=dp2
            df_v[p,rb,:]=dfb
        def first(t,c,p):
            rows=pl.ds(pl.multiple_of(t*RT+c*QR,QR),QR); rb=part(c,QR)
            dh1=acc_v[p,rb,:]
            nrm1=n1_v[rows,:]
            tally(gb_v,3,dh1*nrm1); tally(gb_v,4,dh1)
            e=dh1*row(OG1)
            dp1=r1_v[rows,0:1]*(e-jnp.mean(e,axis=-1,keepdims=True)-nrm1*jnp.mean(e*nrm1,axis=-1,keepdims=True))
            f_v[rows,:]=dp1
            da=dp1.astype(BF)
            tally(gb_v,5,da.astype(F32))
            hb_v[rows,:]=da
        loop(4,lambda c: second(0,c,0))
        for t in range(NT):
            p=t%2
            rows=pl.ds(t*RT,RT)
            pltpu.make_async_copy(ov.at[rows],out_o.at[rows],osem.at[2]).start()
            def middle(c):
                cc=part(c,CH)
                du=(nn(df_v[p],wd_v[:,cc])*slope_v[rows,cc].astype(F32)).astype(BF)
                if t>0: first(t-1,c,1-p)
                if t<NT-1: second(t+1,c,1-p)
                tally(ga_v,c,du.astype(F32))
                acc_v[p]+=nn(du,wi_v[cc,:])
            loop(NC,middle)
            if t>0:
                back=pl.ds((t-1)*RT,RT)
                pltpu.make_async_copy(f_v.at[back],dp1_o.at[back],osem.at[3]).start()
        def closing(c):
            first(NT-1,c,(NT-1)%2)
            dcT_v[part(c,RT),0:(NT-1)*RT]=nt(won_v[part(c,RT),:],hb_v[0:(NT-1)*RT,:]).astype(BF)
        loop(4,closing)
        pltpu.make_async_copy(f_v.at[pl.ds((NT-1)*RT,RT)],dp1_o.at[pl.ds((NT-1)*RT,RT)],osem.at[3]).start()
        def last(c): dcT_v[part(c,RT),(NT-1)*RT:]=nt(won_v[part(c,RT),:],hb_v[(NT-1)*RT:,:]).astype(BF)
        loop(4,last)
        def put(o,v):
            for k in range(v.shape[1]//128):
                g_ref[o//128+k:o//128+k+1,:]=v[:,k*128:(k+1)*128]
        for i,at in enumerate((OG2,OC2,O2,OG1,OC1,OO)):
            put(at,jnp.sum(gb_v[8*i:8*i+8,:],axis=0,keepdims=True))
        for c in range(NC): put(O1+c*CH,jnp.sum(ga_v[8*c:8*c+8,:],axis=0,keepdims=True))
        cd=pltpu.make_async_copy(dcT_v,dcT_o,osem.at[4]); cd.start()
        if comm:
            for m in (0,2,3): g.sends_done(m)
        pltpu.make_async_copy(ov,out_o,osem.at[2]).wait()
        pltpu.make_async_copy(f_v,dp1_o,osem.at[3]).wait()
        cd.wait()
    V=pltpu.VMEM
    scr=[V((T,D),BF),V((T,D),BF),V((D,D),BF),V((D,D),BF),V((FF,D),BF),V((D,FF),BF),V((T,D),F32),V((T,128),F32),
        V((T,D),BF),V((T,FF),BF),V((T,FF),BF),V((T,D),F32),V((2,T,UC),F32),V((2,RT,D),F32),V((2,RT,D),BF),V((8*NC,CH),F32),V((48,D),F32),DMA((11,)),DMA((QC,)),DMA((2,S)),DMA((5,))]
    if comm: scr+=[V((mats[2]["R"],mats[2]["L"]),BF)]+comm_scratch(n)
    out=pl.pallas_call(kernel,
        out_shape=[SDS((3*D,T),BF),SDS((D,T),BF),SDS((H,S,SEQ,SEQ),BF),SDS((T,D),BF),SDS((T,D),F32),SDS((D,T),BF),SDS((12*D//128,128),F32)]+full_shapes(mats[:1],ndp,nfs),
        in_specs=[ANY,ANY,VM,VM,VM]+[ANY,ANY,VM if comm else ANY,ANY],out_specs=[ANY]*6+[VM]+([ANY] if comm else []),scratch_shapes=scr,
        compiler_params=comm_params(mats,cid),name="forward")(x,cot,bias,seg,pad,*sources)
    return out[:7],(out[7] if comm else sources[0])

STEP=5
decay_first=0.5
decay_second=0.5
adam_eps=1e-08
step_rate=0.4
NB=12
BS=32
LATE=2*D//128
EARLY=10*D//128
exact=lax.Precision.HIGHEST

def dot_exact(a,b,ca,cb):
    return lax.dot_general(a,b,(((ca,),(cb,)),((),())),precision=exact,preferred_element_type=F32)

class Reduce:
    def __init__(self,src,plane_buf,z_buf,ssem,psem,zsem):
        self.src,self.pb,self.zb,self.ssem,self.psem,self.zsem=src,plane_buf,z_buf,ssem,psem,zsem
        dp=lax.axis_index("dp"); self.x=lax.axis_index("fsdp")
        self.z=dp//4; self.y=(dp//2)%2; self.c=dp%2
        self.me=self.y*4+self.c*2+self.x
    def plane_peer(self,r):
        def flip(a,b): return 1-a if b else a
        return (self.z*4+flip(self.y,r&4)*2+flip(self.c,r&2),flip(self.x,r&1))
    def z_peer(self,r):
        hi,lo=self.z//2,self.z%2
        z=(1-hi if r&2 else hi)*2+(1-lo if r&1 else lo)
        return (z*4+self.y*2+self.c,self.x)
    def barrier(self):
        bar=pltpu.get_barrier_semaphore()
        for r in range(1,8): pl.semaphore_signal(bar,inc=1,device_id=self.plane_peer(r),device_id_type=MESH)
        for r in range(1,4): pl.semaphore_signal(bar,inc=1,device_id=self.z_peer(r),device_id_type=MESH)
        pl.semaphore_wait(bar,10)
    def copies(self,stage):
        buf,sem,idx=(self.pb,self.psem,self.me) if stage==0 else (self.zb,self.zsem,self.z)
        peers=[self.plane_peer(r) for r in range(1,8)] if stage==0 else [self.z_peer(r) for r in range(1,4)]
        return [pltpu.make_async_remote_copy(self.src if stage==0 else self.zb.at[idx],buf.at[idx],self.ssem.at[stage*7+i],sem.at[idx],
            device_id=p,device_id_type=MESH) for i,p in enumerate(peers)]
    def start(self):
        for c in self.copies(0): c.start()
    def gather(self,stage):
        buf,sem,idx,k=(self.pb,self.psem,self.me,8) if stage==0 else (self.zb,self.zsem,self.z,NZ)
        for q in range(k):
            @pl.when(q!=idx)
            def _(): pltpu.make_async_copy(buf.at[q],buf.at[q],sem.at[q]).wait()
    def middle(self):
        self.gather(0)
        self.pb[self.me]=self.src[...]
        tot=self.pb[0]
        for q in range(1,8): tot=tot+self.pb[q]
        self.zb[self.z]=tot
        for c in self.copies(1): c.start()
    def end(self):
        self.gather(1)
        tot=self.zb[0]
        for q in range(1,NZ): tot=tot+self.zb[q]
        return tot
    def finish(self):
        for st in (0,1):
            for c in self.copies(st): c.wait_send()

def reduce_scratch(rows):
    return [pltpu.VMEM((rows,128),F32),pltpu.VMEM((8,rows,128),F32),pltpu.VMEM((NZ,rows,128),F32),DMA((10,)),DMA((8,)),DMA((NZ,))]

def fold_tables(n):
    i=lax.broadcasted_iota(jnp.int32,(32*n,8*n),0); j=lax.broadcasted_iota(jnp.int32,(32*n,8*n),1)
    sel=jnp.where(i//4==j,1.0,0.0)
    i=lax.broadcasted_iota(jnp.int32,(32*n,128),0); j=lax.broadcasted_iota(jnp.int32,(32*n,128),1)
    mask=jnp.where(i%4==j//32,1.0,0.0)
    i=lax.broadcasted_iota(jnp.int32,(128,32),0); j=lax.broadcasted_iota(jnp.int32,(128,32),1)
    fold=jnp.where(i%32==j,1.0,0.0)
    return sel,mask,fold

def attn_tail(p,qkvT,ctxT,dcT,dp1,wqkvT,update,cid):
    S=p.shape[1]; T=S*SEQ; G=2; NI=H//G; R=G*HD; RT=256; NT=T//RT
    up=update is not None
    def kernel(*refs):
        p_h,qkv_h,c_h,d_h,dp_h,w_h=refs[:6]; o=6
        if up: g_in,mf_h,ms_h,bl_h,br_h=refs[o:o+5]; o+=5
        if up: ig_o,gs_o,st_v=refs[o:o+3]; o+=3
        else: ig_o,gl_o=refs[o:o+2]; o+=2
        pb,qkv_v,c_v,d_v,dp_v,w_v,ig_v,ones_v,psem,lsem,wsem,osem=refs[o:o+12]; o+=12
        if up:
            early_refs=refs[o:o+6]; late_refs=refs[o+6:o+12]; o+=12
            xs,xr=refs[o:o+2]; o+=2
            early=Reduce(*early_refs); late=Reduce(*late_refs); gl=late_refs[0]
        else: gl=gl_o
        PB=3
        def p_load(i): return [pltpu.make_async_copy(p_h.at[i*G+h],pb.at[lax.rem(i,PB),h],psem.at[lax.rem(i,PB),h]) for h in range(G)]
        def begin_p(i):
            for c in p_load(i): c.start()
        def chunk(i):
            out=[pltpu.make_async_copy(qkv_h.at[part(i+k*NI,R)],qkv_v.at[part(i+k*NI,R)],lsem.at[i,k]) for k in range(3)]
            return out+[pltpu.make_async_copy(a.at[part(i,R)],b.at[part(i,R)],lsem.at[i,3+k]) for k,(a,b) in enumerate(((d_h,d_v),(c_h,c_v)))]
        def begin(i):
            for c in chunk(i): c.start()
        begin(0); begin_p(0); begin(1); begin_p(1)
        wl=[pltpu.make_async_copy(w_h.at[pl.ds(k*D,D)],w_v.at[pl.ds(k*D,D)],wsem.at[k]) for k in range(3)]
        dl=pltpu.make_async_copy(dp_h,dp_v,wsem.at[3])
        ones_v[...]=jnp.ones_like(ones_v)
        if up:
            early.barrier()
            early_refs[0][...]=g_in[LATE:,:]
            early.start()
            x=early.x
            states=[]
            for k,a in enumerate((mf_h,ms_h,bl_h,br_h)):
                states.append(pltpu.make_async_remote_copy(a.at[0],st_v.at[k,x],xs.at[k],xr.at[k],device_id=early.plane_peer(1),device_id_type=MESH))
                states.append(pltpu.make_async_copy(a.at[0],st_v.at[k,x],xs.at[4+k]))
            for c in states: c.start()
        def back(i):
            @pl.when(i<NI-2)
            def _(): begin(i+2); begin_p(i+2)
            for k in range(3):
                @pl.when(i==k+1)
                def _(): wl[k].start()
            @pl.when(i==4)
            def _(): dl.start()
            for c in chunk(i)+p_load(i): c.wait()
            b=lax.rem(i,PB)
            for s in range(S):
                cols=pl.ds(s*SEQ,SEQ)
                for h in range(G):
                    r=part(i*G+h,HD); rk=part(i*G+h+H,HD); rv=part(i*G+h+2*H,HD)
                    d=d_v[r,cols]
                    pr=pb[b,h,s]
                    q=qkv_v[r,cols]; k=qkv_v[rk,cols]; v=qkv_v[rv,cols]
                    delta=jnp.sum(d.astype(F32)*c_v[r,cols].astype(F32),axis=0,keepdims=True)
                    ds=(pr.astype(F32)*(tn(v,d)-delta)).astype(BF)
                    qkv_v[rv,cols]=nt(d,pr).astype(BF)
                    qkv_v[rk,cols]=(nt(q,ds)*0.125).astype(BF)
                    qkv_v[r,cols]=(nn(k,ds)*0.125).astype(BF)
            gl[pl.ds(i,1),:]=nt(ones_v[...],qkv_v[part(i,R),:])[0:1,:]
            gl[pl.ds(NI+i,1),:]=nt(ones_v[...],qkv_v[part(i+2*NI,R),:])[0:1,:]
            if up:
                @pl.when(i==3)
                def _(): early.middle()
        loop(NI,back)
        if up: late.start()
        for c in wl+[dl]: c.wait()
        def finish(t):
            cols=part(t,RT)
            acc=dp_v[cols,:]
            for k in range(3):
                acc=acc+tn(qkv_v[k*D:(k+1)*D,cols],w_v[k*D:(k+1)*D,:])
            ig_v[cols,:]=acc.astype(BF)
            pltpu.make_async_copy(ig_v.at[cols],ig_o.at[cols],osem.at[0]).start()
            if up:
                @pl.when(t==1)
                def _(): late.middle()
        loop(NT,finish)
        if up:
            for c in states: c.wait()
            gs_o[LATE:,:]=early.end()
            gs_o[0:LATE,:]=late.end()
            early.finish(); late.finish()
        pltpu.make_async_copy(ig_v,ig_o,osem.at[0]).wait()
    V=pltpu.VMEM
    scr=[V((3,G,S,SEQ,SEQ),BF),V((3*D,T),BF),V((D,T),BF),V((D,T),BF),V((T,D),F32),V((3*D,D),BF),V((T,D),BF),V((8,T),BF),DMA((3,G)),DMA((NI,5)),DMA((4,)),DMA((1,))]
    ins=[p,qkvT,ctxT,dcT,dp1,wqkvT]; specs=[ANY]*6
    outs=[SDS((T,D),BF)]; ospecs=[ANY]
    if up:
        g,mf,ms,bl,br=update
        ins+=[g,mf,ms,bl,br]; specs+=[VM]+[ANY]*4
        outs+=[SDS((NB*8,128),F32),SDS((4,2)+mf.shape[1:],F32)]; ospecs+=[VM,VM]
        scr+=reduce_scratch(EARLY)+reduce_scratch(LATE)+[DMA((8,)),DMA((4,))]
    else:
        outs+=[SDS((LATE,128),F32)]; ospecs+=[VM]
    return pl.pallas_call(kernel,out_shape=outs,in_specs=specs,out_specs=ospecs,scratch_shapes=scr,
        compiler_params=comm_params([1] if up else [],cid),name="attn_tail")(*ins)

def update_step(out,ig,grads,state,bias,owners):
    cap=state.shape[2]; NP=4
    def kernel(out_h,ig_h,g_in,st_v,b_in,own_s,out_o,ig_o,bg_o,mf_o,ms_o,bn_o,bl_o,m_st,v_st,v,sem):
        rows=out.shape[0]//NP
        def moves(down,k):
            a,b=((out_h,out_o),(ig_h,ig_o))[k]
            at=[pl.ds(i*rows,rows) for i in range(NP)]
            if down: return [pltpu.make_async_copy(v.at[k,r],b.at[r],sem.at[1,k,i]) for i,r in enumerate(at)]
            return [pltpu.make_async_copy(a.at[r],v.at[k,r],sem.at[0,k,i]) for i,r in enumerate(at)]
        for k in range(2):
            for c in moves(0,k): c.start()
        x=lax.axis_index("fsdp")
        owner=[own_s[b] for b in range(NB)]
        rank=[]
        for b in range(NB):
            r=jnp.int32(0)
            for e in range(b): r=r+jnp.where(owner[e]==owner[b],1,0)
            rank.append(r)
        def adam(b0,n,tiles):
            sel,mask,fold=fold_tables(n)
            gs=dot_exact(dot_exact(sel,tiles,1,0)*mask,fold,1,0)
            outs=[]
            for j in range(n):
                b=b0+j
                at=jnp.minimum(rank[b],st_v.shape[2]-1)
                first,second,left,right=[st_v[k,owner[b],at] for k in range(4)]
                t=dot_exact(dot_exact(left,gs[j*BS:(j+1)*BS,:],0,0),right,1,0)
                m=decay_first*first+(1.0-decay_first)*t
                v=decay_second*second+(1.0-decay_second)*t*t
                m_st[b]=m; v_st[b]=v
                un=(m/(1.0-decay_first**STEP))/(jnp.sqrt(v/(1.0-decay_second**STEP))+adam_eps)
                outs.append(dot_exact(dot_exact(left,un,1,0),right,1,1))
                if j in (0,2):
                    for c in moves(0,j//2): c.wait()
                    for c in moves(1,j//2): c.start()
            back_=dot_exact(jnp.concatenate(outs,0),fold,1,1)*mask
            new=b_in[8*b0:8*(b0+n),:]-step_rate*dot_exact(sel,back_,0,0)
            bg_o[8*b0:8*(b0+n),:]=tiles
            bn_o[8*b0:8*(b0+n),:]=new
            bl_o[8*b0:8*(b0+n),:]=new.astype(BF)
        adam(0,NB,g_in[...])
        for c in range(mf_o.shape[1]):
            at=jnp.int32(0); hit=jnp.int32(0)
            for b in range(NB):
                here=(owner[b]==x)&(rank[b]==c)
                at=at+jnp.where(here,b,0); hit=hit+jnp.where(here,1,0)
            at=jnp.minimum(at,NB-1)
            filled=hit.astype(F32)
            mf_o[0,c]=m_st[at]*filled
            ms_o[0,c]=v_st[at]*filled
        for k in range(2):
            for c in moves(1,k): c.wait()
    m=SDS((1,cap,BS,BS),F32)
    return pl.pallas_call(kernel,
        out_shape=[SDS(out.shape,BF),SDS(ig.shape,BF),SDS((NB*8,128),F32),m,m,SDS((NB*8,128),F32),SDS((NB*8,128),BF)],
        in_specs=[ANY,ANY,VM,VM,VM,pl.BlockSpec(memory_space=pltpu.SMEM)],out_specs=[ANY,ANY]+[VM]*5,
        scratch_shapes=[pltpu.VMEM((NB,BS,BS),F32),pltpu.VMEM((NB,BS,BS),F32),pltpu.VMEM((2,)+out.shape,BF),DMA((2,2,NP))],
        compiler_params=pltpu.CompilerParams(vmem_limit_bytes=VMEM_CAP),name="update")(out,ig,grads,state,bias,owners)


def placement_table(owners, owner_count, capacity):
    block_count = owners.shape[0]
    index_b = jnp.arange(block_count, dtype=jnp.int32)
    same_owner = owners[:, None] == owners[None, :]
    earlier = index_b[None, :] < index_b[:, None]
    rank_of = jnp.sum((same_owner & earlier).astype(jnp.int32), axis=1)
    owner_hit = owners[None, None, :] == jnp.arange(owner_count, dtype=jnp.int32)[:, None, None]
    slot_hit = rank_of[None, None, :] == jnp.arange(capacity, dtype=jnp.int32)[None, :, None]
    return (owner_hit & slot_hit).astype(jnp.float32)


def adam_rotated(grad_slots, value_slots, first_old, second_old, left_basis, right_basis, filled):
    turned = jnp.einsum("fcki,fckj->fcij", left_basis, grad_slots, precision=exact)
    turned = jnp.einsum("fcik,fckj->fcij", turned, right_basis, precision=exact)
    first_raw = decay_first * first_old + (1.0 - decay_first) * turned
    second_raw = decay_second * second_old + (1.0 - decay_second) * turned * turned
    normed_step = (
        first_raw
        / (1.0 - decay_first**STEP)
        / (jnp.sqrt(second_raw / (1.0 - decay_second**STEP)) + adam_eps)
    )
    restored = jnp.einsum("fcik,fckj->fcij", left_basis, normed_step, precision=exact)
    restored = jnp.einsum("fcik,fcjk->fcij", restored, right_basis, precision=exact)
    value_new = value_slots - step_rate * restored
    return (first_raw * filled, second_raw * filled, value_new * filled)


def body(
    acts,
    cotangent,
    seg_ids,
    pad_mask,
    qkv_weight,
    out_weight,
    in_weight,
    down_weight,
    biases,
    moment_first,
    moment_second,
    basis_left,
    basis_right,
    owners,
):
    ndp, nfs = lax.axis_size("dp"), lax.axis_size("fsdp")
    shards = (qkv_weight.T, out_weight.T, in_weight, down_weight.T)
    slots = acts.shape[0] * acts.shape[1]
    x = acts.reshape(slots * SEQ, D)
    cot = cotangent.reshape(slots * SEQ, D)
    seg = seg_ids.reshape(slots, 1, SEQ)
    pad = pad_mask.reshape(slots, 1, SEQ)
    bias = biases.reshape(1, -1)
    if (ndp, nfs) == (16, 2):
        (qkvT, ctxT, p, out, dp1, dcT, g), wqT = forward(matdesc(), shards, 1, x, cot, bias, seg, pad, ndp, nfs)
        state = (g, moment_first, moment_second, basis_left, basis_right)
        ig, total, state = attn_tail(p, qkvT, ctxT, dcT, dp1, wqT, state, 2)
        out, ig, bg, mf, ms, bn, bl = update_step(out, ig, total, state, biases.reshape(-1, 128), owners)
        return (
            out.reshape(acts.shape),
            ig.reshape(acts.shape),
            bg.reshape(-1),
            mf,
            ms,
            bn.reshape(-1),
            bl.reshape(-1),
        )
    whole = [
        lax.all_gather(lax.all_gather(t, "fsdp", axis=1, tiled=True), "dp", axis=0, tiled=True)
        for t in (shards[0], shards[1], shards[2].T, shards[3])
    ]
    (qkvT, ctxT, p, out, dp1, dcT, g), wqT = forward([], whole, 0, x, cot, bias, seg, pad, ndp, nfs)
    ig, gl = attn_tail(p, qkvT, ctxT, dcT, dp1, wqT, None, 0)
    outputs, input_grads = out.reshape(acts.shape), ig.reshape(acts.shape)
    grad_total = jnp.concatenate([gl, g[LATE:]], 0).reshape(-1)
    block_count = owners.shape[0]
    block_side = moment_first.shape[2]
    slot_table = placement_table(owners, lax.axis_size("fsdp"), moment_first.shape[1])
    grad_slots = jnp.einsum(
        "fcb,bij->fcij",
        slot_table,
        grad_total.reshape(block_count, block_side, block_side),
        precision=exact,
    )
    summed = lax.psum(grad_slots.astype(jnp.bfloat16), "dp")
    owned_grad = lax.psum_scatter(summed, "fsdp", scatter_dimension=0, tiled=True).astype(
        jnp.float32
    )
    own_table = lax.dynamic_slice_in_dim(slot_table, lax.axis_index("fsdp"), 1, 0)
    value_slots = jnp.einsum(
        "fcb,bij->fcij",
        own_table,
        biases.reshape(block_count, block_side, block_side),
        precision=exact,
    )
    filled = jnp.sum(own_table, axis=2)[:, :, None, None]
    first_new, second_new, value_new = adam_rotated(
        owned_grad, value_slots, moment_first, moment_second, basis_left, basis_right, filled
    )
    shared_grad, shared_value = (
        lax.all_gather(owned_grad, "fsdp", axis=0, tiled=True),
        lax.all_gather(value_new, "fsdp", axis=0, tiled=True),
    )
    bias_grad = jnp.einsum("fcb,fcij->bij", slot_table, shared_grad, precision=exact).reshape(
        biases.shape[0]
    )
    bias_new = jnp.einsum("fcb,fcij->bij", slot_table, shared_value, precision=exact).reshape(
        biases.shape[0]
    )
    return (
        outputs,
        input_grads,
        bias_grad,
        first_new,
        second_new,
        bias_new,
        bias_new.astype(jnp.bfloat16),
    )


def solution(mesh):
    placed = (
        P(None, ("dp", "fsdp"), None, None),
        P(None, ("dp", "fsdp"), None, None),
        P(None, ("dp", "fsdp"), None),
        P(None, ("dp", "fsdp"), None),
        P("fsdp", "dp"),
        P("fsdp", "dp"),
        P("fsdp", "dp"),
        P("fsdp", "dp"),
        P(),
        P("fsdp", None, None, None),
        P("fsdp", None, None, None),
        P("fsdp", None, None, None),
        P("fsdp", None, None, None),
        P(),
    )
    return jax.shard_map(
        body,
        mesh=mesh,
        in_specs=placed,
        out_specs=(
            P(None, ("dp", "fsdp"), None, None),
            P(None, ("dp", "fsdp"), None, None),
            P(),
            P("fsdp", None, None, None),
            P("fsdp", None, None, None),
            P(),
            P(),
        ),
        check_vma=False,
    )
```

```python
import functools
import math

import jax
import jax.numpy as jnp
from jax import lax
from jax.experimental import pallas as pl
from jax.experimental.pallas import tpu as pltpu
from jax.sharding import PartitionSpec as P

MESH=pl.DeviceIdType.MESH
NZ=4

def split_rows(R,L,a,b,unit=16):
    out=[];r=0
    for kind,n in (("A1",a),("A2",a),("B1",b),("B2",b)):
        if n: out.append((kind,r,n,0,L)); r+=n
    assert r==R,(r,R)
    return out
def split_lanes(R,L,a,b):
    out=[];l=0
    for kind,n in (("A1",a),("A2",a),("B1",b),("B2",b)):
        if n: out.append((kind,0,R,l,n)); l+=n
    assert l==L
    return out

EVENTS=[(dz,rx,ry) for dz in range(1-NZ,NZ) for rx in (0,1) for ry in (0,1) if (dz,rx,ry)!=(0,0,0)]
EVENTS.sort(key=lambda e:(abs(e[0])+e[1]+e[2], e[1]+e[2], -e[0]))
NEV=len(EVENTS)

def pick(i,values):
    out=jnp.int32(values[0])
    for j in range(1,len(values)):
        out=jnp.where(i==j,jnp.int32(values[j]),out)
    return out

def sends(kind,z,dz,rx,ry):
    plane=(rx==0)&(ry==0)
    turn_y=(kind[1]=="1")&(rx==1)&(ry==0)
    turn_x=(kind[1]=="2")&(rx==0)&(ry==1)
    if kind[0]=="A":
        return {"zp":plane&(dz>=0)&(z<NZ-1),"zm":plane&(dz<=0)&(z>0),"x":plane|turn_x,"y":plane|turn_y}
    return {"zp":(dz>=0)&(z<NZ-1),"zm":(dz<=0)&(z>0),"x":(dz==0)&(plane|turn_x),"y":(dz==0)&(plane|turn_y)}

WAYS=("x","y","zp","zm","s")

def region(total, N, K):
    for lanes in range(128,K+1,128):
        if total%lanes==0:
            rows=total//lanes
            if rows%16==0 and rows<=N: return rows,lanes
    raise ValueError(total)

class Gather:
    def __init__(self, mats, shards, fulls, local_sem, send_sem, recv_sem, sib_sem):
        self.mats=mats; self.sh=shards; self.full=fulls
        self.lsem,self.ssem,self.rsem,self.bsem=local_sem,send_sem,recv_sem,sib_sem
        dp=lax.axis_index("dp"); x=lax.axis_index("fsdp")
        self.dp,self.x=dp,x
        self.z=dp//4; self.y=(dp//2)%2; self.c=dp%2
        self.dev={"x":(dp,1-x),"y":(self.z*4+(1-self.y)*2+self.c,x),"zp":(dp+4,x),"zm":(dp-4,x),"s":(self.z*4+self.y*2+1-self.c,x)}
    def barrier(self):
        bar=pltpu.get_barrier_semaphore()
        for d in ("x","y","s"):
            pl.semaphore_signal(bar,inc=1,device_id=self.dev[d],device_id_type=MESH)
        @pl.when(self.z<NZ-1)
        def _(): pl.semaphore_signal(bar,inc=1,device_id=self.dev["zp"],device_id_type=MESH)
        @pl.when(self.z>0)
        def _(): pl.semaphore_signal(bar,inc=1,device_id=self.dev["zm"],device_id_type=MESH)
        inner=(self.z>0)&(self.z<NZ-1)
        @pl.when(inner)
        def _(): pl.semaphore_wait(bar,5)
        @pl.when(jnp.logical_not(inner))
        def _(): pl.semaphore_wait(bar,4)
    def place(self,m,k,dz,rx,ry):
        M=self.mats[m]; kind,r0,nr,l0,nl=M["classes"][k]
        y=self.y+ry-2*self.y*ry
        x=self.x+rx-2*self.x*rx
        src=(self.z-dz)*4+y*2+self.c
        return self.full[m].at[pl.ds(pl.multiple_of(src*M["R"]+r0,16),nr), pl.ds(pl.multiple_of(x*M["L"]+l0,128),nl)]
    def forward(self,m,k,dz,rx,ry,src):
        kind=self.mats[m]["classes"][k][0]
        dst=self.place(m,k,dz,rx,ry)
        def rel(a,b,c): return (a+NZ-1)*4+b*2+c
        child={"x":rel(dz,1,ry),"y":rel(dz,rx,1),"zp":rel(dz+1,rx,ry),"zm":rel(dz-1,rx,ry)}
        for d,cond in sends(kind,self.z,dz,rx,ry).items():
            def go(d=d):
                pltpu.make_async_remote_copy(src,dst,self.ssem.at[m,WAYS.index(d)],self.rsem.at[m,k,child[d]],
                    device_id=self.dev[d],device_id_type=MESH).start()
            if cond is True: go()
            elif cond is not False: pl.when(cond)(go)
        pltpu.make_async_remote_copy(src,dst,self.ssem.at[m,4],self.bsem.at[m,self.z-dz],device_id=self.dev["s"],device_id_type=MESH).start()
    def own(self,m):
        M=self.mats[m]
        for k,(kind,r0,nr,l0,nl) in enumerate(M["classes"]):
            self.forward(m,k,0,0,0,self.sh[m].at[pl.ds(r0,nr),pl.ds(l0,nl)])
        full=self.full[m].at[pl.ds(pl.multiple_of(self.dp*M["R"],16),M["R"]),pl.ds(pl.multiple_of(self.x*M["L"],128),M["L"])]
        pltpu.make_async_copy(self.sh[m],full,self.lsem.at[m]).start()
    def step(self,e,ms):
        code=pick(e,[(v[0]+NZ-1)*4+v[1]*2+v[2] for v in EVENTS])
        dz=code//4-(NZ-1); rx=(code//2)%2; ry=code%2
        src=self.z-dz
        @pl.when((src>=0)&(src<=NZ-1))
        def _():
            for m in ms:
                for k in range(len(self.mats[m]["classes"])):
                    ref=self.place(m,k,dz,rx,ry)
                    pltpu.make_async_copy(ref,ref,self.rsem.at[m,k,(dz+NZ-1)*4+rx*2+ry]).wait()
                    self.forward(m,k,dz,rx,ry,ref)
    def wait_bytes(self,m,total,sem):
        N,K=self.full[m].shape
        r,l=region(total,N,K)
        ref=self.full[m].at[pl.ds(0,r),pl.ds(0,l)]
        pltpu.make_async_copy(ref,ref,sem).wait()
    def own_done(self,m):
        own=self.sh[m]
        pltpu.make_async_copy(own,own,self.lsem.at[m]).wait()
    def plane_done(self,m,z0):
        N,K=self.full[m].shape
        self.wait_bytes(m,N*K//2//NZ,self.bsem.at[m,z0])
    def sends_done(self,m):
        M=self.mats[m]; N,K=self.full[m].shape
        def total(d,z):
            t=0
            for kind,r0,nr,l0,nl in M["classes"]:
                for dz,rx,ry in [(0,0,0)]+EVENTS:
                    if 0<=z-dz<=NZ-1 and sends(kind,z,dz,rx,ry)[d]: t+=nr*nl
            return t
        for d in ("x","y"):
            self.wait_bytes(m,total(d,0),self.ssem.at[m,WAYS.index(d)])
        for d in ("zp","zm"):
            for z in range(NZ):
                if total(d,z):
                    pl.when(self.z==z)(functools.partial(self.wait_bytes,m,total(d,z),self.ssem.at[m,WAYS.index(d)]))
        self.wait_bytes(m,N*K//2,self.ssem.at[m,4])
    def finish(self,m):
        self.own_done(m)
        for z in range(NZ): self.plane_done(m,z)
        self.sends_done(m)

def comm_scratch(n):
    return [pltpu.SemaphoreType.DMA((n,)),pltpu.SemaphoreType.DMA((n,5)),pltpu.SemaphoreType.DMA((n,4,8*NZ-4)),pltpu.SemaphoreType.DMA((n,NZ))] if n else []

def matdesc(beta=True):
    if beta:
        return [dict(R=192,L=512,classes=split_rows(192,512,80,16)),dict(R=64,L=512,classes=split_rows(64,512,32,0)),
            dict(R=256,L=512,classes=split_rows(256,512,96,32)),dict(R=64,L=2048,classes=split_lanes(64,2048,768,256))]
    return [dict(R=192,L=512,classes=split_rows(192,512,96,0)),dict(R=64,L=512,classes=split_rows(64,512,32,0)),
            dict(R=256,L=512,classes=split_rows(256,512,128,0)),dict(R=64,L=2048,classes=split_lanes(64,2048,1024,0))]
BF=jnp.bfloat16
F32=jnp.float32
D=1024
H=16
HD=64
FF=4096
SEQ=512
LOG2E=1.4426950408889634
VMEM_CAP=60<<20
ANY=pl.BlockSpec(memory_space=pl.ANY)
VM=pl.BlockSpec(memory_space=pltpu.VMEM)
SDS=jax.ShapeDtypeStruct
DMA=pltpu.SemaphoreType.DMA

def nn(a,b): return lax.dot_general(a,b,(((1,),(0,)),((),())),preferred_element_type=F32)
def nt(a,b): return lax.dot_general(a,b,(((1,),(1,)),((),())),preferred_element_type=F32)
def tn(a,b): return lax.dot_general(a,b,(((0,),(0,)),((),())),preferred_element_type=F32)
def part(i,n): return pl.ds(pl.multiple_of(i*n,n),n)
def loop(n,fn):
    def st(i,c):
        fn(i); return c
    lax.fori_loop(0,n,st,0)

OQ,OV,OO,O1,O2,OG1,OC1,OG2,OC2=0,D,2*D,3*D,3*D+FF,4*D+FF,5*D+FF,6*D+FF,7*D+FF

def column(row):
    return jnp.transpose(jnp.broadcast_to(row,(8,row.shape[1])))

class Quiet:
    def step(self,e,ms): pass

def comm_params(mats,cid,**kw):
    if mats: kw.update(collective_id=cid,has_side_effects=True)
    return pltpu.CompilerParams(vmem_limit_bytes=VMEM_CAP,**kw)

def full_shapes(mats,dp,fs):
    return [SDS((M["R"]*dp,M["L"]*fs),BF) for M in mats]

def ln(v):
    c=v-jnp.mean(v,axis=-1,keepdims=True)
    r=lax.rsqrt(jnp.mean(c*c,axis=-1,keepdims=True)+1e-12)
    return c*r,r

PACE=[13, 17, 17, 29, 31, 34, 37, 44, 44, 45, 45, 46, 46, 57, 58, 58, 58, 59, 61, 61, 61, 65, 70, 70, 70, 75, 75, 76, 78, 85, 85, 85, 85, 85, 88, 91, 91, 93, 97, 98, 101, 101, 103, 104, 106, 106, 106, 108, 108, 108, 108, 108, 108, 108, 108, 108]
OWN={1: 17, 2: 44, 3: 70}

def forward(mats,sources,cid,x,cot,bias,seg,pad,ndp,nfs):
    comm=bool(mats); n=len(mats); S=x.shape[0]//SEQ; T=x.shape[0]
    RT=256; NT=T//RT; CH=1024; NC=FF//CH; UC=256; DC=D//4; QC=3*D//4//256

    def kernel(*refs):
        x_h,cot_h,b_ref,seg_ref,pad_ref=refs[:5]
        src=refs[5:9]; o=9
        qkv_o,ctxT_o,p_o,out_o,dp1_o,dcT_o,g_ref=refs[o:o+7]; o+=7
        if comm: wq_h=refs[o]; o+=1
        else: wq_h=src[0]
        x_v,ctx_v,wo_v,won_v,wi_v,wd_v,n1_v,r1_v,hb_v,act_v,slope_v,f_v,u_v,acc_v,df_v,ga_v,gb_v,lsem,wsem,psem,osem=refs[o:o+21]; o+=21
        loads=[pltpu.make_async_copy(x_h,x_v,lsem.at[0]),pltpu.make_async_copy(cot_h,wo_v,lsem.at[1])]
        loads[0].start()
        if not comm:
            whole={m:pltpu.make_async_copy(src[m],v,lsem.at[1+m]) for m,v in ((1,wo_v),(2,wi_v),(3,wd_v))}
            for c in whole.values(): c.start()
        if comm:
            in_t=refs[o]; sems=refs[o+1:]
            g=Gather(mats,(src[0],src[1],in_t,src[3]),(wq_h,wo_v,wi_v,wd_v),*sems); g.barrier(); g.own(0)
            eye=jnp.where(lax.broadcasted_iota(jnp.int32,(256,256),0)==lax.broadcasted_iota(jnp.int32,(256,256),1),1.0,0.0).astype(BF)
            in_t[...]=nt(eye,src[2][...]).astype(BF)
            z=g.z
            order=[z,jnp.where(z==3,2,z+1),jnp.where(z==0,2,jnp.where(z==3,1,z-1)),jnp.where((z==0)|(z==1),3,0)]
        else: order=[0,1,2,3]
        def steps(m,a,b):
            def one(e,carry):
                g.step(e,[m])
                for k,at in OWN.items():
                    if (at-1)//NEV==m:
                        @pl.when(e==(at-1)%NEV)
                        def _(): g.own(k)
                return carry
            lax.fori_loop(a,b,one,0)
        def pace(op,i,count):
            if not comm: return
            starts=[PACE[j-1] if j else 0 for j in range(op,op+count)]; ends=PACE[op:op+count]
            a,b=pick(i,starts),pick(i,ends)
            for m in range(4):
                if starts[0]<NEV*(m+1) and ends[-1]>NEV*m and starts[0]<ends[-1]:
                    steps(m,jnp.clip(a-NEV*m,0,NEV),jnp.clip(b-NEV*m,0,NEV))
        def plane(m,i):
            if comm:
                if i==0: g.own_done(m)
                g.plane_done(m,order[i])
            elif i==0 and m>0: whole[m].wait()
        def row(o,k=D): return b_ref[0:1,o:o+k]
        n1_v[:,0:8]=column(row(OQ)); n1_v[:,128:136]=jnp.zeros((D,8),F32); n1_v[:,256:264]=column(row(OV))
        for s in range(S):
            seg_r=seg_ref[s]; pad_r=pad_ref[s]
            key_r=jnp.where(pad_r==1,seg_r,-1).astype(F32)
            key_c=column(key_r)[:,0:1]
            hit=(key_c==seg_r.astype(F32))|((pad_r==0)&(key_c>=0.0))
            f_v[s*SEQ:(s+1)*SEQ,0:SEQ]=jnp.where(hit,0.0,-1e30)
        def project(i):
            pace(QC*i,0,1); plane(0,i)
            def load(c): return pltpu.make_async_copy(wq_h.at[part(order[i]*QC+c,256)],slope_v.at[part(c,256),2048:3072],wsem.at[c])
            loop(QC,lambda c: load(c).start())
            def chunk(c):
                jj=order[i]*QC+c; j=jj//4; rows=part(jj%4,256); cols=part(j,T)
                load(c).wait()
                acc=nt(slope_v[part(c,256),2048:3072],x_v[...])+n1_v[rows,part(j,128)][:,0:1]
                act_v[rows,cols]=acc.astype(BF)
                pltpu.make_async_copy(act_v.at[rows,cols],qkv_o.at[part(jj,256)],osem.at[0]).start()
                @pl.when(c<QC-1)
                def _(): pace(QC*i+1,c,QC-1)
            loop(QC,chunk)
        loads[0].wait()
        for i in range(4): project(i)
        AT=4*QC
        def attend(h):
            pace(AT,h,H)
            b=lax.rem(h,2)
            def p_copy(i,s): return pltpu.make_async_copy(slope_v.at[part(b,SEQ),s*SEQ:(s+1)*SEQ],p_o.at[i,s],psem.at[b,s])
            @pl.when(h>=2)
            def _():
                for s in range(S): p_copy(h-2,s).wait()
            for s in range(S):
                def at(j): return pl.ds(j*T+s*SEQ,SEQ)
                r=part(h,HD)
                q=act_v[r,at(0)]; k=act_v[r,at(1)]; v=act_v[r,at(2)]
                t=tn(k,q)*(0.125*LOG2E)+f_v[s*SEQ:(s+1)*SEQ,0:SEQ]
                e=jnp.exp2(t-jnp.max(t,axis=0,keepdims=True))
                p=(e*(1.0/jnp.sum(e,axis=0,keepdims=True))).astype(BF)
                slope_v[part(b,SEQ),s*SEQ:(s+1)*SEQ]=p
                hb_v[r,pl.ds(s*SEQ,SEQ)]=nn(v,p).astype(BF)
                p_copy(h,s).start()
        loop(H,attend)
        ct=pltpu.make_async_copy(hb_v,ctxT_o,osem.at[1]); ct.start()
        def turn(i): ctx_v[:,part(i,128)]=jnp.transpose(hb_v[part(i,128),:])
        loop(D//128,turn)
        for i in range(4): plane(1,i)
        def turn2(i): won_v[:,part(i,128)]=jnp.transpose(wo_v[part(i,128),:])
        loop(D//128,turn2)
        if comm: g.sends_done(1)
        loads[1].start()
        pltpu.make_async_copy(act_v.at[:,0:3*T],act_v.at[:,0:3*T],osem.at[0]).wait()
        for b in range(2):
            for s in range(S): pltpu.make_async_copy(slope_v.at[b*SEQ:(b+1)*SEQ,s*SEQ:(s+1)*SEQ],p_o.at[b,s],psem.at[b,s]).wait()
        ct.wait()
        g_ref[...]=jnp.zeros_like(g_ref)
        def join(t):
            pace(AT+H,t,NT)
            rows=part(t,RT)
            br=nn(ctx_v[rows,:],won_v[...])+row(OO)
            nrm,r=ln(x_v[rows,:].astype(F32)+br)
            n1_v[rows,:]=nrm
            r1_v[rows,:]=jnp.broadcast_to(r,(RT,128))
            hb_v[rows,:]=(nrm*row(OG1)+row(OC1)).astype(BF)
        loop(NT,join)
        UP=AT+H+NT
        def up(i):
            c0=order[i]*(CH//UC)
            pace(UP+2*i,0,1); plane(2,i)
            u_v[0]=nt(hb_v[...],wi_v[part(c0,UC),:])
            def two(k):
                for b in range(2):
                    ci=c0+2*k+b
                    cc=part(ci,UC)
                    nx=part(jnp.minimum(ci+1,c0+CH//UC-1),UC)
                    bias_u=b_ref[0:1,part(ci+O1//UC,UC)]
                    for t in range(NT):
                        rows=pl.ds(t*RT,RT)
                        u_v[1-b,rows,:]=nt(hb_v[rows,:],wi_v[nx,:])
                        u=u_v[b,rows,:]+bias_u
                        cdf=0.5+0.5*lax.erf(u*(1.0/math.sqrt(2.0)))
                        act_v[rows,cc]=(u*cdf).astype(BF)
                        slope_v[rows,cc]=(cdf+u*(jnp.exp2(u*u*(-0.5*LOG2E))*(1.0/math.sqrt(2.0*math.pi)))).astype(BF)
                @pl.when(k==0)
                def _(): pace(UP+2*i+1,0,1)
            loop(CH//UC//2,two)
        for i in range(4): up(i)
        DN=UP+8
        def down(i):
            pace(DN+NT*i,0,1); plane(3,i)
            r=part(order[i],DC)
            def tile(t):
                rows=part(t,RT)
                f_v[rows,r]=nt(act_v[rows,:],wd_v[r,:])
                @pl.when(t<NT-1)
                def _(): pace(DN+NT*i+1,t,NT-1)
            loop(NT,tile)
        for i in range(4): down(i)
        loads[1].wait()
        cot_v=wo_v; ov=x_v; dcT_v=ctx_v
        QR=RT//4
        ga_v[...]=jnp.zeros_like(ga_v); gb_v[...]=jnp.zeros_like(gb_v)
        def tally(ref,i,v):
            at=pl.ds(pl.multiple_of(i*8,8),8)
            ref[at,:]+=jnp.sum(v.reshape(v.shape[0]//8,8,v.shape[1]),axis=0)
        def second(t,c,p):
            rows=pl.ds(pl.multiple_of(t*RT+c*QR,QR),QR); rb=part(c,QR)
            h1=n1_v[rows,:]*row(OG1)+row(OC1)
            n2,r2=ln(h1+(f_v[rows,:]+row(O2)))
            ov[rows,:]=(n2*row(OG2)+row(OC2)).astype(BF)
            dy=cot_v[rows,:].astype(F32)
            tally(gb_v,0,dy*n2); tally(gb_v,1,dy)
            e=dy*row(OG2)
            dp2=r2*(e-jnp.mean(e,axis=-1,keepdims=True)-n2*jnp.mean(e*n2,axis=-1,keepdims=True))
            dfb=dp2.astype(BF)
            tally(gb_v,2,dfb.astype(F32))
            acc_v[p,rb,:]=dp2
            df_v[p,rb,:]=dfb
        def first(t,c,p):
            rows=pl.ds(pl.multiple_of(t*RT+c*QR,QR),QR); rb=part(c,QR)
            dh1=acc_v[p,rb,:]
            nrm1=n1_v[rows,:]
            tally(gb_v,3,dh1*nrm1); tally(gb_v,4,dh1)
            e=dh1*row(OG1)
            dp1=r1_v[rows,0:1]*(e-jnp.mean(e,axis=-1,keepdims=True)-nrm1*jnp.mean(e*nrm1,axis=-1,keepdims=True))
            f_v[rows,:]=dp1
            da=dp1.astype(BF)
            tally(gb_v,5,da.astype(F32))
            hb_v[rows,:]=da
        loop(4,lambda c: second(0,c,0))
        for t in range(NT):
            p=t%2
            rows=pl.ds(t*RT,RT)
            pltpu.make_async_copy(ov.at[rows],out_o.at[rows],osem.at[2]).start()
            def middle(c):
                cc=part(c,CH)
                du=(nn(df_v[p],wd_v[:,cc])*slope_v[rows,cc].astype(F32)).astype(BF)
                if t>0: first(t-1,c,1-p)
                if t<NT-1: second(t+1,c,1-p)
                tally(ga_v,c,du.astype(F32))
                acc_v[p]+=nn(du,wi_v[cc,:])
            loop(NC,middle)
            if t>0:
                back=pl.ds((t-1)*RT,RT)
                pltpu.make_async_copy(f_v.at[back],dp1_o.at[back],osem.at[3]).start()
        def closing(c):
            first(NT-1,c,(NT-1)%2)
            dcT_v[part(c,RT),0:(NT-1)*RT]=nt(won_v[part(c,RT),:],hb_v[0:(NT-1)*RT,:]).astype(BF)
        loop(4,closing)
        pltpu.make_async_copy(f_v.at[pl.ds((NT-1)*RT,RT)],dp1_o.at[pl.ds((NT-1)*RT,RT)],osem.at[3]).start()
        def last(c): dcT_v[part(c,RT),(NT-1)*RT:]=nt(won_v[part(c,RT),:],hb_v[(NT-1)*RT:,:]).astype(BF)
        loop(4,last)
        def put(o,v):
            for k in range(v.shape[1]//128):
                g_ref[o//128+k:o//128+k+1,:]=v[:,k*128:(k+1)*128]
        for i,at in enumerate((OG2,OC2,O2,OG1,OC1,OO)):
            put(at,jnp.sum(gb_v[8*i:8*i+8,:],axis=0,keepdims=True))
        for c in range(NC): put(O1+c*CH,jnp.sum(ga_v[8*c:8*c+8,:],axis=0,keepdims=True))
        cd=pltpu.make_async_copy(dcT_v,dcT_o,osem.at[4]); cd.start()
        if comm:
            for m in (0,2,3): g.sends_done(m)
        pltpu.make_async_copy(ov,out_o,osem.at[2]).wait()
        pltpu.make_async_copy(f_v,dp1_o,osem.at[3]).wait()
        cd.wait()
    V=pltpu.VMEM
    scr=[V((T,D),BF),V((T,D),BF),V((D,D),BF),V((D,D),BF),V((FF,D),BF),V((D,FF),BF),V((T,D),F32),V((T,128),F32),
        V((T,D),BF),V((T,FF),BF),V((T,FF),BF),V((T,D),F32),V((2,T,UC),F32),V((2,RT,D),F32),V((2,RT,D),BF),V((8*NC,CH),F32),V((48,D),F32),DMA((11,)),DMA((QC,)),DMA((2,S)),DMA((5,))]
    if comm: scr+=[V((mats[2]["R"],mats[2]["L"]),BF)]+comm_scratch(n)
    out=pl.pallas_call(kernel,
        out_shape=[SDS((3*D,T),BF),SDS((D,T),BF),SDS((H,S,SEQ,SEQ),BF),SDS((T,D),BF),SDS((T,D),F32),SDS((D,T),BF),SDS((12*D//128,128),F32)]+full_shapes(mats[:1],ndp,nfs),
        in_specs=[ANY,ANY,VM,VM,VM]+[ANY,ANY,VM if comm else ANY,ANY],out_specs=[ANY]*6+[VM]+([ANY] if comm else []),scratch_shapes=scr,
        compiler_params=comm_params(mats,cid),name="forward")(x,cot,bias,seg,pad,*sources)
    return out[:7],(out[7] if comm else sources[0])

STEP=5
decay_first=0.5
decay_second=0.5
adam_eps=1e-08
step_rate=0.4
NB=12
BS=32
LATE=2*D//128
EARLY=10*D//128
exact=lax.Precision.HIGHEST

def dot_exact(a,b,ca,cb):
    return lax.dot_general(a,b,(((ca,),(cb,)),((),())),precision=exact,preferred_element_type=F32)

class Reduce:
    def __init__(self,src,plane_buf,z_buf,ssem,psem,zsem):
        self.src,self.pb,self.zb,self.ssem,self.psem,self.zsem=src,plane_buf,z_buf,ssem,psem,zsem
        dp=lax.axis_index("dp"); self.x=lax.axis_index("fsdp")
        self.z=dp//4; self.y=(dp//2)%2; self.c=dp%2
        self.me=self.y*4+self.c*2+self.x
    def plane_peer(self,r):
        def flip(a,b): return 1-a if b else a
        return (self.z*4+flip(self.y,r&4)*2+flip(self.c,r&2),flip(self.x,r&1))
    def z_peer(self,r):
        hi,lo=self.z//2,self.z%2
        z=(1-hi if r&2 else hi)*2+(1-lo if r&1 else lo)
        return (z*4+self.y*2+self.c,self.x)
    def barrier(self):
        bar=pltpu.get_barrier_semaphore()
        for r in range(1,8): pl.semaphore_signal(bar,inc=1,device_id=self.plane_peer(r),device_id_type=MESH)
        for r in range(1,4): pl.semaphore_signal(bar,inc=1,device_id=self.z_peer(r),device_id_type=MESH)
        pl.semaphore_wait(bar,10)
    def copies(self,stage):
        buf,sem,idx=(self.pb,self.psem,self.me) if stage==0 else (self.zb,self.zsem,self.z)
        peers=[self.plane_peer(r) for r in range(1,8)] if stage==0 else [self.z_peer(r) for r in range(1,4)]
        return [pltpu.make_async_remote_copy(self.src if stage==0 else self.zb.at[idx],buf.at[idx],self.ssem.at[stage*7+i],sem.at[idx],
            device_id=p,device_id_type=MESH) for i,p in enumerate(peers)]
    def start(self):
        for c in self.copies(0): c.start()
    def gather(self,stage):
        buf,sem,idx,k=(self.pb,self.psem,self.me,8) if stage==0 else (self.zb,self.zsem,self.z,NZ)
        for q in range(k):
            @pl.when(q!=idx)
            def _(): pltpu.make_async_copy(buf.at[q],buf.at[q],sem.at[q]).wait()
    def middle(self):
        self.gather(0)
        self.pb[self.me]=self.src[...]
        tot=self.pb[0]
        for q in range(1,8): tot=tot+self.pb[q]
        self.zb[self.z]=tot
        for c in self.copies(1): c.start()
    def end(self):
        self.gather(1)
        tot=self.zb[0]
        for q in range(1,NZ): tot=tot+self.zb[q]
        return tot
    def finish(self):
        for st in (0,1):
            for c in self.copies(st): c.wait_send()

def reduce_scratch(rows):
    return [pltpu.VMEM((rows,128),F32),pltpu.VMEM((8,rows,128),F32),pltpu.VMEM((NZ,rows,128),F32),DMA((10,)),DMA((8,)),DMA((NZ,))]

def fold_tables(n):
    i=lax.broadcasted_iota(jnp.int32,(32*n,8*n),0); j=lax.broadcasted_iota(jnp.int32,(32*n,8*n),1)
    sel=jnp.where(i//4==j,1.0,0.0)
    i=lax.broadcasted_iota(jnp.int32,(32*n,128),0); j=lax.broadcasted_iota(jnp.int32,(32*n,128),1)
    mask=jnp.where(i%4==j//32,1.0,0.0)
    i=lax.broadcasted_iota(jnp.int32,(128,32),0); j=lax.broadcasted_iota(jnp.int32,(128,32),1)
    fold=jnp.where(i%32==j,1.0,0.0)
    return sel,mask,fold

def attn_tail(p,qkvT,ctxT,dcT,dp1,wqkvT,update,cid):
    S=p.shape[1]; T=S*SEQ; G=2; NI=H//G; R=G*HD; RT=256; NT=T//RT
    up=update is not None
    def kernel(*refs):
        p_h,qkv_h,c_h,d_h,dp_h,w_h=refs[:6]; o=6
        if up: g_in,mf_h,ms_h,bl_h,br_h=refs[o:o+5]; o+=5
        if up: ig_o,gs_o,st_v=refs[o:o+3]; o+=3
        else: ig_o,gl_o=refs[o:o+2]; o+=2
        pb,qkv_v,c_v,d_v,dp_v,w_v,ig_v,ones_v,psem,lsem,wsem,osem=refs[o:o+12]; o+=12
        if up:
            early_refs=refs[o:o+6]; late_refs=refs[o+6:o+12]; o+=12
            xs,xr=refs[o:o+2]; o+=2
            early=Reduce(*early_refs); late=Reduce(*late_refs); gl=late_refs[0]
        else: gl=gl_o
        PB=3
        def p_load(i): return [pltpu.make_async_copy(p_h.at[i*G+h],pb.at[lax.rem(i,PB),h],psem.at[lax.rem(i,PB),h]) for h in range(G)]
        def begin_p(i):
            for c in p_load(i): c.start()
        def chunk(i):
            out=[pltpu.make_async_copy(qkv_h.at[part(i+k*NI,R)],qkv_v.at[part(i+k*NI,R)],lsem.at[i,k]) for k in range(3)]
            return out+[pltpu.make_async_copy(a.at[part(i,R)],b.at[part(i,R)],lsem.at[i,3+k]) for k,(a,b) in enumerate(((d_h,d_v),(c_h,c_v)))]
        def begin(i):
            for c in chunk(i): c.start()
        begin(0); begin_p(0); begin(1); begin_p(1)
        wl=[pltpu.make_async_copy(w_h.at[pl.ds(k*D,D)],w_v.at[pl.ds(k*D,D)],wsem.at[k]) for k in range(3)]
        dl=pltpu.make_async_copy(dp_h,dp_v,wsem.at[3])
        ones_v[...]=jnp.ones_like(ones_v)
        if up:
            early.barrier()
            early_refs[0][...]=g_in[LATE:,:]
            early.start()
            x=early.x
            states=[]
            for k,a in enumerate((mf_h,ms_h,bl_h,br_h)):
                states.append(pltpu.make_async_remote_copy(a.at[0],st_v.at[k,x],xs.at[k],xr.at[k],device_id=early.plane_peer(1),device_id_type=MESH))
                states.append(pltpu.make_async_copy(a.at[0],st_v.at[k,x],xs.at[4+k]))
            for c in states: c.start()
        def back(i):
            @pl.when(i<NI-2)
            def _(): begin(i+2); begin_p(i+2)
            for k in range(3):
                @pl.when(i==k+1)
                def _(): wl[k].start()
            @pl.when(i==4)
            def _(): dl.start()
            for c in chunk(i)+p_load(i): c.wait()
            b=lax.rem(i,PB)
            for s in range(S):
                cols=pl.ds(s*SEQ,SEQ)
                for h in range(G):
                    r=part(i*G+h,HD); rk=part(i*G+h+H,HD); rv=part(i*G+h+2*H,HD)
                    d=d_v[r,cols]
                    pr=pb[b,h,s]
                    q=qkv_v[r,cols]; k=qkv_v[rk,cols]; v=qkv_v[rv,cols]
                    delta=jnp.sum(d.astype(F32)*c_v[r,cols].astype(F32),axis=0,keepdims=True)
                    ds=(pr.astype(F32)*(tn(v,d)-delta)).astype(BF)
                    qkv_v[rv,cols]=nt(d,pr).astype(BF)
                    qkv_v[rk,cols]=(nt(q,ds)*0.125).astype(BF)
                    qkv_v[r,cols]=(nn(k,ds)*0.125).astype(BF)
            gl[pl.ds(i,1),:]=nt(ones_v[...],qkv_v[part(i,R),:])[0:1,:]
            gl[pl.ds(NI+i,1),:]=nt(ones_v[...],qkv_v[part(i+2*NI,R),:])[0:1,:]
            if up:
                @pl.when(i==3)
                def _(): early.middle()
        loop(NI,back)
        if up: late.start()
        for c in wl+[dl]: c.wait()
        def finish(t):
            cols=part(t,RT)
            acc=dp_v[cols,:]
            for k in range(3):
                acc=acc+tn(qkv_v[k*D:(k+1)*D,cols],w_v[k*D:(k+1)*D,:])
            ig_v[cols,:]=acc.astype(BF)
            pltpu.make_async_copy(ig_v.at[cols],ig_o.at[cols],osem.at[0]).start()
            if up:
                @pl.when(t==1)
                def _(): late.middle()
        loop(NT,finish)
        if up:
            for c in states: c.wait()
            gs_o[LATE:,:]=early.end()
            gs_o[0:LATE,:]=late.end()
            early.finish(); late.finish()
        pltpu.make_async_copy(ig_v,ig_o,osem.at[0]).wait()
    V=pltpu.VMEM
    scr=[V((3,G,S,SEQ,SEQ),BF),V((3*D,T),BF),V((D,T),BF),V((D,T),BF),V((T,D),F32),V((3*D,D),BF),V((T,D),BF),V((8,T),BF),DMA((3,G)),DMA((NI,5)),DMA((4,)),DMA((1,))]
    ins=[p,qkvT,ctxT,dcT,dp1,wqkvT]; specs=[ANY]*6
    outs=[SDS((T,D),BF)]; ospecs=[ANY]
    if up:
        g,mf,ms,bl,br=update
        ins+=[g,mf,ms,bl,br]; specs+=[VM]+[ANY]*4
        outs+=[SDS((NB*8,128),F32),SDS((4,2)+mf.shape[1:],F32)]; ospecs+=[VM,VM]
        scr+=reduce_scratch(EARLY)+reduce_scratch(LATE)+[DMA((8,)),DMA((4,))]
    else:
        outs+=[SDS((LATE,128),F32)]; ospecs+=[VM]
    return pl.pallas_call(kernel,out_shape=outs,in_specs=specs,out_specs=ospecs,scratch_shapes=scr,
        compiler_params=comm_params([1] if up else [],cid),name="attn_tail")(*ins)

def update_step(out,ig,grads,state,bias,owners):
    cap=state.shape[2]; NP=4
    def kernel(out_h,ig_h,g_in,st_v,b_in,own_s,out_o,ig_o,bg_o,mf_o,ms_o,bn_o,bl_o,m_st,v_st,v,sem):
        rows=out.shape[0]//NP
        def moves(down,k):
            a,b=((out_h,out_o),(ig_h,ig_o))[k]
            at=[pl.ds(i*rows,rows) for i in range(NP)]
            if down: return [pltpu.make_async_copy(v.at[k,r],b.at[r],sem.at[1,k,i]) for i,r in enumerate(at)]
            return [pltpu.make_async_copy(a.at[r],v.at[k,r],sem.at[0,k,i]) for i,r in enumerate(at)]
        for k in range(2):
            for c in moves(0,k): c.start()
        x=lax.axis_index("fsdp")
        owner=[own_s[b] for b in range(NB)]
        rank=[]
        for b in range(NB):
            r=jnp.int32(0)
            for e in range(b): r=r+jnp.where(owner[e]==owner[b],1,0)
            rank.append(r)
        def adam(b0,n,tiles):
            sel,mask,fold=fold_tables(n)
            gs=dot_exact(dot_exact(sel,tiles,1,0)*mask,fold,1,0)
            outs=[]
            for j in range(n):
                b=b0+j
                at=jnp.minimum(rank[b],st_v.shape[2]-1)
                first,second,left,right=[st_v[k,owner[b],at] for k in range(4)]
                left,right=left.astype(BF),right.astype(BF)
                t=nn(tn(left,gs[j*BS:(j+1)*BS,:].astype(BF)).astype(BF),right)
                m=decay_first*first+(1.0-decay_first)*t
                v=decay_second*second+(1.0-decay_second)*t*t
                m_st[b]=m; v_st[b]=v
                un=(m/(1.0-decay_first**STEP))/(jnp.sqrt(v/(1.0-decay_second**STEP))+adam_eps)
                outs.append(nt(nn(left,un.astype(BF)).astype(BF),right))
                if j in (0,2):
                    for c in moves(0,j//2): c.wait()
                    for c in moves(1,j//2): c.start()
            back_=dot_exact(jnp.concatenate(outs,0),fold,1,1)*mask
            new=b_in[8*b0:8*(b0+n),:]-step_rate*dot_exact(sel,back_,0,0)
            bg_o[8*b0:8*(b0+n),:]=tiles
            bn_o[8*b0:8*(b0+n),:]=new
            bl_o[8*b0:8*(b0+n),:]=new.astype(BF)
        adam(0,NB,g_in[...])
        for c in range(mf_o.shape[1]):
            at=jnp.int32(0); hit=jnp.int32(0)
            for b in range(NB):
                here=(owner[b]==x)&(rank[b]==c)
                at=at+jnp.where(here,b,0); hit=hit+jnp.where(here,1,0)
            at=jnp.minimum(at,NB-1)
            filled=hit.astype(F32)
            mf_o[0,c]=m_st[at]*filled
            ms_o[0,c]=v_st[at]*filled
        for k in range(2):
            for c in moves(1,k): c.wait()
    m=SDS((1,cap,BS,BS),F32)
    return pl.pallas_call(kernel,
        out_shape=[SDS(out.shape,BF),SDS(ig.shape,BF),SDS((NB*8,128),F32),m,m,SDS((NB*8,128),F32),SDS((NB*8,128),BF)],
        in_specs=[ANY,ANY,VM,VM,VM,pl.BlockSpec(memory_space=pltpu.SMEM)],out_specs=[ANY,ANY]+[VM]*5,
        scratch_shapes=[pltpu.VMEM((NB,BS,BS),F32),pltpu.VMEM((NB,BS,BS),F32),pltpu.VMEM((2,)+out.shape,BF),DMA((2,2,NP))],
        compiler_params=pltpu.CompilerParams(vmem_limit_bytes=VMEM_CAP),name="update")(out,ig,grads,state,bias,owners)


def placement_table(owners, owner_count, capacity):
    block_count = owners.shape[0]
    index_b = jnp.arange(block_count, dtype=jnp.int32)
    same_owner = owners[:, None] == owners[None, :]
    earlier = index_b[None, :] < index_b[:, None]
    rank_of = jnp.sum((same_owner & earlier).astype(jnp.int32), axis=1)
    owner_hit = owners[None, None, :] == jnp.arange(owner_count, dtype=jnp.int32)[:, None, None]
    slot_hit = rank_of[None, None, :] == jnp.arange(capacity, dtype=jnp.int32)[None, :, None]
    return (owner_hit & slot_hit).astype(jnp.float32)


def adam_rotated(grad_slots, value_slots, first_old, second_old, left_basis, right_basis, filled):
    turned = jnp.einsum("fcki,fckj->fcij", left_basis, grad_slots, precision=exact)
    turned = jnp.einsum("fcik,fckj->fcij", turned, right_basis, precision=exact)
    first_raw = decay_first * first_old + (1.0 - decay_first) * turned
    second_raw = decay_second * second_old + (1.0 - decay_second) * turned * turned
    normed_step = (
        first_raw
        / (1.0 - decay_first**STEP)
        / (jnp.sqrt(second_raw / (1.0 - decay_second**STEP)) + adam_eps)
    )
    restored = jnp.einsum("fcik,fckj->fcij", left_basis, normed_step, precision=exact)
    restored = jnp.einsum("fcik,fcjk->fcij", restored, right_basis, precision=exact)
    value_new = value_slots - step_rate * restored
    return (first_raw * filled, second_raw * filled, value_new * filled)


def body(
    acts,
    cotangent,
    seg_ids,
    pad_mask,
    qkv_weight,
    out_weight,
    in_weight,
    down_weight,
    biases,
    moment_first,
    moment_second,
    basis_left,
    basis_right,
    owners,
):
    ndp, nfs = lax.axis_size("dp"), lax.axis_size("fsdp")
    shards = (qkv_weight.T, out_weight.T, in_weight, down_weight.T)
    slots = acts.shape[0] * acts.shape[1]
    x = acts.reshape(slots * SEQ, D)
    cot = cotangent.reshape(slots * SEQ, D)
    seg = seg_ids.reshape(slots, 1, SEQ)
    pad = pad_mask.reshape(slots, 1, SEQ)
    bias = biases.reshape(1, -1)
    if (ndp, nfs) == (16, 2):
        (qkvT, ctxT, p, out, dp1, dcT, g), wqT = forward(matdesc(), shards, 1, x, cot, bias, seg, pad, ndp, nfs)
        state = (g, moment_first, moment_second, basis_left, basis_right)
        ig, total, state = attn_tail(p, qkvT, ctxT, dcT, dp1, wqT, state, 2)
        out, ig, bg, mf, ms, bn, bl = update_step(out, ig, total, state, biases.reshape(-1, 128), owners)
        return (
            out.reshape(acts.shape),
            ig.reshape(acts.shape),
            bg.reshape(-1),
            mf,
            ms,
            bn.reshape(-1),
            bl.reshape(-1),
        )
    whole = [
        lax.all_gather(lax.all_gather(t, "fsdp", axis=1, tiled=True), "dp", axis=0, tiled=True)
        for t in (shards[0], shards[1], shards[2].T, shards[3])
    ]
    (qkvT, ctxT, p, out, dp1, dcT, g), wqT = forward([], whole, 0, x, cot, bias, seg, pad, ndp, nfs)
    ig, gl = attn_tail(p, qkvT, ctxT, dcT, dp1, wqT, None, 0)
    outputs, input_grads = out.reshape(acts.shape), ig.reshape(acts.shape)
    grad_total = jnp.concatenate([gl, g[LATE:]], 0).reshape(-1)
    block_count = owners.shape[0]
    block_side = moment_first.shape[2]
    slot_table = placement_table(owners, lax.axis_size("fsdp"), moment_first.shape[1])
    grad_slots = jnp.einsum(
        "fcb,bij->fcij",
        slot_table,
        grad_total.reshape(block_count, block_side, block_side),
        precision=exact,
    )
    summed = lax.psum(grad_slots.astype(jnp.bfloat16), "dp")
    owned_grad = lax.psum_scatter(summed, "fsdp", scatter_dimension=0, tiled=True).astype(
        jnp.float32
    )
    own_table = lax.dynamic_slice_in_dim(slot_table, lax.axis_index("fsdp"), 1, 0)
    value_slots = jnp.einsum(
        "fcb,bij->fcij",
        own_table,
        biases.reshape(block_count, block_side, block_side),
        precision=exact,
    )
    filled = jnp.sum(own_table, axis=2)[:, :, None, None]
    first_new, second_new, value_new = adam_rotated(
        owned_grad, value_slots, moment_first, moment_second, basis_left, basis_right, filled
    )
    shared_grad, shared_value = (
        lax.all_gather(owned_grad, "fsdp", axis=0, tiled=True),
        lax.all_gather(value_new, "fsdp", axis=0, tiled=True),
    )
    bias_grad = jnp.einsum("fcb,fcij->bij", slot_table, shared_grad, precision=exact).reshape(
        biases.shape[0]
    )
    bias_new = jnp.einsum("fcb,fcij->bij", slot_table, shared_value, precision=exact).reshape(
        biases.shape[0]
    )
    return (
        outputs,
        input_grads,
        bias_grad,
        first_new,
        second_new,
        bias_new,
        bias_new.astype(jnp.bfloat16),
    )


def solution(mesh):
    placed = (
        P(None, ("dp", "fsdp"), None, None),
        P(None, ("dp", "fsdp"), None, None),
        P(None, ("dp", "fsdp"), None),
        P(None, ("dp", "fsdp"), None),
        P("fsdp", "dp"),
        P("fsdp", "dp"),
        P("fsdp", "dp"),
        P("fsdp", "dp"),
        P(),
        P("fsdp", None, None, None),
        P("fsdp", None, None, None),
        P("fsdp", None, None, None),
        P("fsdp", None, None, None),
        P(),
    )
    return jax.shard_map(
        body,
        mesh=mesh,
        in_specs=placed,
        out_specs=(
            P(None, ("dp", "fsdp"), None, None),
            P(None, ("dp", "fsdp"), None, None),
            P(),
            P("fsdp", None, None, None),
            P("fsdp", None, None, None),
            P(),
            P(),
        ),
        check_vma=False,
    )
```

```python
import functools
import math

import jax
import jax.numpy as jnp
from jax import lax
from jax.experimental import pallas as pl
from jax.experimental.pallas import tpu as pltpu
from jax.sharding import PartitionSpec as P

MESH=pl.DeviceIdType.MESH
NZ=4

def split_rows(R,L,a,b,unit=16):
    out=[];r=0
    for kind,n in (("A1",a),("A2",a),("B1",b),("B2",b)):
        if n: out.append((kind,r,n,0,L)); r+=n
    assert r==R,(r,R)
    return out
def split_lanes(R,L,a,b):
    out=[];l=0
    for kind,n in (("A1",a),("A2",a),("B1",b),("B2",b)):
        if n: out.append((kind,0,R,l,n)); l+=n
    assert l==L
    return out

EVENTS=[(dz,rx,ry) for dz in range(1-NZ,NZ) for rx in (0,1) for ry in (0,1) if (dz,rx,ry)!=(0,0,0)]
EVENTS.sort(key=lambda e:(abs(e[0])+e[1]+e[2], e[1]+e[2], -e[0]))
NEV=len(EVENTS)

def pick(i,values):
    out=jnp.int32(values[0])
    for j in range(1,len(values)):
        out=jnp.where(i==j,jnp.int32(values[j]),out)
    return out

def sends(kind,z,dz,rx,ry):
    plane=(rx==0)&(ry==0)
    turn_y=(kind[1]=="1")&(rx==1)&(ry==0)
    turn_x=(kind[1]=="2")&(rx==0)&(ry==1)
    if kind[0]=="A":
        return {"zp":plane&(dz>=0)&(z<NZ-1),"zm":plane&(dz<=0)&(z>0),"x":plane|turn_x,"y":plane|turn_y}
    return {"zp":(dz>=0)&(z<NZ-1),"zm":(dz<=0)&(z>0),"x":(dz==0)&(plane|turn_x),"y":(dz==0)&(plane|turn_y)}

WAYS=("x","y","zp","zm","s")

def region(total, N, K):
    for lanes in range(128,K+1,128):
        if total%lanes==0:
            rows=total//lanes
            if rows%16==0 and rows<=N: return rows,lanes
    raise ValueError(total)

class Gather:
    def __init__(self, mats, shards, fulls, local_sem, send_sem, recv_sem, sib_sem):
        self.mats=mats; self.sh=shards; self.full=fulls
        self.lsem,self.ssem,self.rsem,self.bsem=local_sem,send_sem,recv_sem,sib_sem
        dp=lax.axis_index("dp"); x=lax.axis_index("fsdp")
        self.dp,self.x=dp,x
        self.z=dp//4; self.y=(dp//2)%2; self.c=dp%2
        self.dev={"x":(dp,1-x),"y":(self.z*4+(1-self.y)*2+self.c,x),"zp":(dp+4,x),"zm":(dp-4,x),"s":(self.z*4+self.y*2+1-self.c,x)}
    def barrier(self):
        bar=pltpu.get_barrier_semaphore()
        for d in ("x","y","s"):
            pl.semaphore_signal(bar,inc=1,device_id=self.dev[d],device_id_type=MESH)
        @pl.when(self.z<NZ-1)
        def _(): pl.semaphore_signal(bar,inc=1,device_id=self.dev["zp"],device_id_type=MESH)
        @pl.when(self.z>0)
        def _(): pl.semaphore_signal(bar,inc=1,device_id=self.dev["zm"],device_id_type=MESH)
        inner=(self.z>0)&(self.z<NZ-1)
        @pl.when(inner)
        def _(): pl.semaphore_wait(bar,5)
        @pl.when(jnp.logical_not(inner))
        def _(): pl.semaphore_wait(bar,4)
    def place(self,m,k,dz,rx,ry):
        M=self.mats[m]; kind,r0,nr,l0,nl=M["classes"][k]
        y=self.y+ry-2*self.y*ry
        x=self.x+rx-2*self.x*rx
        src=(self.z-dz)*4+y*2+self.c
        return self.full[m].at[pl.ds(pl.multiple_of(src*M["R"]+r0,16),nr), pl.ds(pl.multiple_of(x*M["L"]+l0,128),nl)]
    def forward(self,m,k,dz,rx,ry,src):
        kind=self.mats[m]["classes"][k][0]
        dst=self.place(m,k,dz,rx,ry)
        def rel(a,b,c): return (a+NZ-1)*4+b*2+c
        child={"x":rel(dz,1,ry),"y":rel(dz,rx,1),"zp":rel(dz+1,rx,ry),"zm":rel(dz-1,rx,ry)}
        for d,cond in sends(kind,self.z,dz,rx,ry).items():
            def go(d=d):
                pltpu.make_async_remote_copy(src,dst,self.ssem.at[m,WAYS.index(d)],self.rsem.at[m,k,child[d]],
                    device_id=self.dev[d],device_id_type=MESH).start()
            if cond is True: go()
            elif cond is not False: pl.when(cond)(go)
        pltpu.make_async_remote_copy(src,dst,self.ssem.at[m,4],self.bsem.at[m,self.z-dz],device_id=self.dev["s"],device_id_type=MESH).start()
    def own(self,m):
        M=self.mats[m]
        for k,(kind,r0,nr,l0,nl) in enumerate(M["classes"]):
            self.forward(m,k,0,0,0,self.sh[m].at[pl.ds(r0,nr),pl.ds(l0,nl)])
        full=self.full[m].at[pl.ds(pl.multiple_of(self.dp*M["R"],16),M["R"]),pl.ds(pl.multiple_of(self.x*M["L"],128),M["L"])]
        pltpu.make_async_copy(self.sh[m],full,self.lsem.at[m]).start()
    def step(self,e,ms):
        code=pick(e,[(v[0]+NZ-1)*4+v[1]*2+v[2] for v in EVENTS])
        dz=code//4-(NZ-1); rx=(code//2)%2; ry=code%2
        src=self.z-dz
        @pl.when((src>=0)&(src<=NZ-1))
        def _():
            for m in ms:
                for k in range(len(self.mats[m]["classes"])):
                    ref=self.place(m,k,dz,rx,ry)
                    pltpu.make_async_copy(ref,ref,self.rsem.at[m,k,(dz+NZ-1)*4+rx*2+ry]).wait()
                    self.forward(m,k,dz,rx,ry,ref)
    def wait_bytes(self,m,total,sem):
        N,K=self.full[m].shape
        r,l=region(total,N,K)
        ref=self.full[m].at[pl.ds(0,r),pl.ds(0,l)]
        pltpu.make_async_copy(ref,ref,sem).wait()
    def own_done(self,m):
        own=self.sh[m]
        pltpu.make_async_copy(own,own,self.lsem.at[m]).wait()
    def plane_done(self,m,z0):
        N,K=self.full[m].shape
        self.wait_bytes(m,N*K//2//NZ,self.bsem.at[m,z0])
    def sends_done(self,m):
        M=self.mats[m]; N,K=self.full[m].shape
        def total(d,z):
            t=0
            for kind,r0,nr,l0,nl in M["classes"]:
                for dz,rx,ry in [(0,0,0)]+EVENTS:
                    if 0<=z-dz<=NZ-1 and sends(kind,z,dz,rx,ry)[d]: t+=nr*nl
            return t
        for d in ("x","y"):
            self.wait_bytes(m,total(d,0),self.ssem.at[m,WAYS.index(d)])
        for d in ("zp","zm"):
            for z in range(NZ):
                if total(d,z):
                    pl.when(self.z==z)(functools.partial(self.wait_bytes,m,total(d,z),self.ssem.at[m,WAYS.index(d)]))
        self.wait_bytes(m,N*K//2,self.ssem.at[m,4])
    def finish(self,m):
        self.own_done(m)
        for z in range(NZ): self.plane_done(m,z)
        self.sends_done(m)

def comm_scratch(n):
    return [pltpu.SemaphoreType.DMA((n,)),pltpu.SemaphoreType.DMA((n,5)),pltpu.SemaphoreType.DMA((n,4,8*NZ-4)),pltpu.SemaphoreType.DMA((n,NZ))] if n else []

def matdesc(beta=True):
    if beta:
        return [dict(R=192,L=512,classes=split_rows(192,512,80,16)),dict(R=64,L=512,classes=split_rows(64,512,32,0)),
            dict(R=256,L=512,classes=split_rows(256,512,96,32)),dict(R=64,L=2048,classes=split_lanes(64,2048,768,256))]
    return [dict(R=192,L=512,classes=split_rows(192,512,96,0)),dict(R=64,L=512,classes=split_rows(64,512,32,0)),
            dict(R=256,L=512,classes=split_rows(256,512,128,0)),dict(R=64,L=2048,classes=split_lanes(64,2048,1024,0))]
BF=jnp.bfloat16
F32=jnp.float32
D=1024
H=16
HD=64
FF=4096
SEQ=512
LOG2E=1.4426950408889634
VMEM_CAP=60<<20
ANY=pl.BlockSpec(memory_space=pl.ANY)
VM=pl.BlockSpec(memory_space=pltpu.VMEM)
SDS=jax.ShapeDtypeStruct
DMA=pltpu.SemaphoreType.DMA

def nn(a,b): return lax.dot_general(a,b,(((1,),(0,)),((),())),preferred_element_type=F32)
def nt(a,b): return lax.dot_general(a,b,(((1,),(1,)),((),())),preferred_element_type=F32)
def tn(a,b): return lax.dot_general(a,b,(((0,),(0,)),((),())),preferred_element_type=F32)
def part(i,n): return pl.ds(pl.multiple_of(i*n,n),n)
def loop(n,fn):
    def st(i,c):
        fn(i); return c
    lax.fori_loop(0,n,st,0)

OQ,OV,OO,O1,O2,OG1,OC1,OG2,OC2=0,D,2*D,3*D,3*D+FF,4*D+FF,5*D+FF,6*D+FF,7*D+FF

def column(row):
    return jnp.transpose(jnp.broadcast_to(row,(8,row.shape[1])))

class Quiet:
    def step(self,e,ms): pass

def comm_params(mats,cid,**kw):
    if mats: kw.update(collective_id=cid,has_side_effects=True)
    return pltpu.CompilerParams(vmem_limit_bytes=VMEM_CAP,**kw)

def full_shapes(mats,dp,fs):
    return [SDS((M["R"]*dp,M["L"]*fs),BF) for M in mats]

def ln(v):
    c=v-jnp.mean(v,axis=-1,keepdims=True)
    r=lax.rsqrt(jnp.mean(c*c,axis=-1,keepdims=True)+1e-12)
    return c*r,r

PACE=[13, 17, 17, 29, 31, 34, 37, 44, 44, 45, 45, 46, 46, 57, 58, 58, 58, 59, 61, 61, 61, 65, 70, 70, 70, 75, 75, 76, 78, 85, 85, 85, 85, 85, 88, 91, 91, 93, 97, 98, 101, 101, 103, 104, 106, 106, 106, 108, 108, 108, 108, 108, 108, 108, 108, 108]
OWN={1: 17, 2: 44, 3: 70}

def forward(mats,sources,cid,x,cot,bias,seg,pad,ndp,nfs):
    comm=bool(mats); n=len(mats); S=x.shape[0]//SEQ; T=x.shape[0]
    RT=256; NT=T//RT; CH=1024; NC=FF//CH; UC=256; DC=D//4; QC=3*D//4//256

    def kernel(*refs):
        x_h,cot_h,b_ref,seg_ref,pad_ref=refs[:5]
        src=refs[5:9]; o=9
        qkv_o,ctxT_o,p_o,out_o,dp1_o,dcT_o,g_ref=refs[o:o+7]; o+=7
        if comm: wq_h=refs[o]; o+=1
        else: wq_h=src[0]
        x_v,ctx_v,wo_v,won_v,wi_v,wd_v,n1_v,r1_v,hb_v,act_v,slope_v,f_v,u_v,acc_v,df_v,ga_v,gb_v,lsem,wsem,psem,osem=refs[o:o+21]; o+=21
        loads=[pltpu.make_async_copy(x_h,x_v,lsem.at[0]),pltpu.make_async_copy(cot_h,wo_v,lsem.at[1])]
        loads[0].start()
        if not comm:
            whole={m:pltpu.make_async_copy(src[m],v,lsem.at[1+m]) for m,v in ((1,wo_v),(2,wi_v),(3,wd_v))}
            for c in whole.values(): c.start()
        if comm:
            in_t=refs[o]; sems=refs[o+1:]
            g=Gather(mats,(src[0],src[1],in_t,src[3]),(wq_h,wo_v,wi_v,wd_v),*sems); g.barrier(); g.own(0)
            eye=jnp.where(lax.broadcasted_iota(jnp.int32,(256,256),0)==lax.broadcasted_iota(jnp.int32,(256,256),1),1.0,0.0).astype(BF)
            in_t[...]=nt(eye,src[2][...]).astype(BF)
            z=g.z
            order=[z,jnp.where(z==3,2,z+1),jnp.where(z==0,2,jnp.where(z==3,1,z-1)),jnp.where((z==0)|(z==1),3,0)]
        else: order=[0,1,2,3]
        def steps(m,a,b):
            def one(e,carry):
                g.step(e,[m])
                for k,at in OWN.items():
                    if (at-1)//NEV==m:
                        @pl.when(e==(at-1)%NEV)
                        def _(): g.own(k)
                return carry
            lax.fori_loop(a,b,one,0)
        def pace(op,i,count):
            if not comm: return
            starts=[PACE[j-1] if j else 0 for j in range(op,op+count)]; ends=PACE[op:op+count]
            a,b=pick(i,starts),pick(i,ends)
            for m in range(4):
                if starts[0]<NEV*(m+1) and ends[-1]>NEV*m and starts[0]<ends[-1]:
                    steps(m,jnp.clip(a-NEV*m,0,NEV),jnp.clip(b-NEV*m,0,NEV))
        def plane(m,i):
            if comm:
                if i==0: g.own_done(m)
                g.plane_done(m,order[i])
            elif i==0 and m>0: whole[m].wait()
        def row(o,k=D): return b_ref[0:1,o:o+k]
        n1_v[:,0:8]=column(row(OQ)); n1_v[:,128:136]=jnp.zeros((D,8),F32); n1_v[:,256:264]=column(row(OV))
        for s in range(S):
            seg_r=seg_ref[s]; pad_r=pad_ref[s]
            key_r=jnp.where(pad_r==1,seg_r,-1).astype(F32)
            key_c=column(key_r)[:,0:1]
            hit=(key_c==seg_r.astype(F32))|((pad_r==0)&(key_c>=0.0))
            f_v[s*SEQ:(s+1)*SEQ,0:SEQ]=jnp.where(hit,0.0,-1e30)
        def project(i):
            pace(QC*i,0,1); plane(0,i)
            def load(c): return pltpu.make_async_copy(wq_h.at[part(order[i]*QC+c,256)],slope_v.at[part(c,256),2048:3072],wsem.at[c])
            loop(QC,lambda c: load(c).start())
            def chunk(c):
                jj=order[i]*QC+c; j=jj//4; rows=part(jj%4,256); cols=part(j,T)
                load(c).wait()
                acc=nt(slope_v[part(c,256),2048:3072],x_v[...])+n1_v[rows,part(j,128)][:,0:1]
                act_v[rows,cols]=acc.astype(BF)
                pltpu.make_async_copy(act_v.at[rows,cols],qkv_o.at[part(jj,256)],osem.at[0]).start()
                @pl.when(c<QC-1)
                def _(): pace(QC*i+1,c,QC-1)
            loop(QC,chunk)
        loads[0].wait()
        for i in range(4): project(i)
        AT=4*QC
        def attend(h):
            pace(AT,h,H)
            b=lax.rem(h,2)
            def p_copy(i,s): return pltpu.make_async_copy(slope_v.at[part(b,SEQ),s*SEQ:(s+1)*SEQ],p_o.at[i,s],psem.at[b,s])
            @pl.when(h>=2)
            def _():
                for s in range(S): p_copy(h-2,s).wait()
            for s in range(S):
                def at(j): return pl.ds(j*T+s*SEQ,SEQ)
                r=part(h,HD)
                q=act_v[r,at(0)]; k=act_v[r,at(1)]; v=act_v[r,at(2)]
                t=tn(k,q)*(0.125*LOG2E)+f_v[s*SEQ:(s+1)*SEQ,0:SEQ]
                e=jnp.exp2(t-jnp.max(t,axis=0,keepdims=True))
                p=(e*(1.0/jnp.sum(e,axis=0,keepdims=True))).astype(BF)
                slope_v[part(b,SEQ),s*SEQ:(s+1)*SEQ]=p
                hb_v[r,pl.ds(s*SEQ,SEQ)]=nn(v,p).astype(BF)
                p_copy(h,s).start()
        loop(H,attend)
        ct=pltpu.make_async_copy(hb_v,ctxT_o,osem.at[1]); ct.start()
        def turn(i): ctx_v[:,part(i,128)]=jnp.transpose(hb_v[part(i,128),:])
        loop(D//128,turn)
        for i in range(4): plane(1,i)
        def turn2(i): won_v[:,part(i,128)]=jnp.transpose(wo_v[part(i,128),:])
        loop(D//128,turn2)
        if comm: g.sends_done(1)
        loads[1].start()
        pltpu.make_async_copy(act_v.at[:,0:3*T],act_v.at[:,0:3*T],osem.at[0]).wait()
        for b in range(2):
            for s in range(S): pltpu.make_async_copy(slope_v.at[b*SEQ:(b+1)*SEQ,s*SEQ:(s+1)*SEQ],p_o.at[b,s],psem.at[b,s]).wait()
        ct.wait()
        g_ref[...]=jnp.zeros_like(g_ref)
        def join(t):
            pace(AT+H,t,NT)
            rows=part(t,RT)
            br=nn(ctx_v[rows,:],won_v[...])+row(OO)
            nrm,r=ln(x_v[rows,:].astype(F32)+br)
            n1_v[rows,:]=nrm
            r1_v[rows,:]=jnp.broadcast_to(r,(RT,128))
            hb_v[rows,:]=(nrm*row(OG1)+row(OC1)).astype(BF)
        loop(NT,join)
        UP=AT+H+NT
        def up(i):
            c0=order[i]*(CH//UC)
            pace(UP+2*i,0,1); plane(2,i)
            u_v[0]=nt(hb_v[...],wi_v[part(c0,UC),:])
            def two(k):
                for b in range(2):
                    ci=c0+2*k+b
                    cc=part(ci,UC)
                    nx=part(jnp.minimum(ci+1,c0+CH//UC-1),UC)
                    bias_u=b_ref[0:1,part(ci+O1//UC,UC)]
                    for t in range(NT):
                        rows=pl.ds(t*RT,RT)
                        u_v[1-b,rows,:]=nt(hb_v[rows,:],wi_v[nx,:])
                        u=u_v[b,rows,:]+bias_u
                        cdf=0.5+0.5*lax.erf(u*(1.0/math.sqrt(2.0)))
                        act_v[rows,cc]=(u*cdf).astype(BF)
                        slope_v[rows,cc]=(cdf+u*(jnp.exp2(u*u*(-0.5*LOG2E))*(1.0/math.sqrt(2.0*math.pi)))).astype(BF)
                @pl.when(k==0)
                def _(): pace(UP+2*i+1,0,1)
            loop(CH//UC//2,two)
        for i in range(4): up(i)
        DN=UP+8
        def down(i):
            pace(DN+NT*i,0,1); plane(3,i)
            r=part(order[i],DC)
            def tile(t):
                rows=part(t,RT)
                f_v[rows,r]=nt(act_v[rows,:],wd_v[r,:])
                @pl.when(t<NT-1)
                def _(): pace(DN+NT*i+1,t,NT-1)
            loop(NT,tile)
        for i in range(4): down(i)
        loads[1].wait()
        cot_v=wo_v; ov=x_v; dcT_v=ctx_v
        QR=RT//4
        ga_v[...]=jnp.zeros_like(ga_v); gb_v[...]=jnp.zeros_like(gb_v)
        def tally(ref,i,v):
            at=pl.ds(pl.multiple_of(i*8,8),8)
            ref[at,:]+=jnp.sum(v.reshape(v.shape[0]//8,8,v.shape[1]),axis=0)
        def second(t,c,p):
            rows=pl.ds(pl.multiple_of(t*RT+c*QR,QR),QR); rb=part(c,QR)
            h1=n1_v[rows,:]*row(OG1)+row(OC1)
            n2,r2=ln(h1+(f_v[rows,:]+row(O2)))
            ov[rows,:]=(n2*row(OG2)+row(OC2)).astype(BF)
            dy=cot_v[rows,:].astype(F32)
            tally(gb_v,0,dy*n2); tally(gb_v,1,dy)
            e=dy*row(OG2)
            dp2=r2*(e-jnp.mean(e,axis=-1,keepdims=True)-n2*jnp.mean(e*n2,axis=-1,keepdims=True))
            dfb=dp2.astype(BF)
            tally(gb_v,2,dfb.astype(F32))
            acc_v[p,rb,:]=dp2
            df_v[p,rb,:]=dfb
        def first(t,c,p):
            rows=pl.ds(pl.multiple_of(t*RT+c*QR,QR),QR); rb=part(c,QR)
            dh1=acc_v[p,rb,:]
            nrm1=n1_v[rows,:]
            tally(gb_v,3,dh1*nrm1); tally(gb_v,4,dh1)
            e=dh1*row(OG1)
            dp1=r1_v[rows,0:1]*(e-jnp.mean(e,axis=-1,keepdims=True)-nrm1*jnp.mean(e*nrm1,axis=-1,keepdims=True))
            f_v[rows,:]=dp1
            da=dp1.astype(BF)
            tally(gb_v,5,da.astype(F32))
            hb_v[rows,:]=da
        loop(4,lambda c: second(0,c,0))
        for t in range(NT):
            p=t%2
            rows=pl.ds(t*RT,RT)
            pltpu.make_async_copy(ov.at[rows],out_o.at[rows],osem.at[2]).start()
            def middle(c):
                cc=part(c,CH)
                du=(nn(df_v[p],wd_v[:,cc])*slope_v[rows,cc].astype(F32)).astype(BF)
                if t>0: first(t-1,c,1-p)
                if t<NT-1: second(t+1,c,1-p)
                tally(ga_v,c,du.astype(F32))
                acc_v[p]+=nn(du,wi_v[cc,:])
            loop(NC,middle)
            if t>0:
                back=pl.ds((t-1)*RT,RT)
                pltpu.make_async_copy(f_v.at[back],dp1_o.at[back],osem.at[3]).start()
        def closing(c):
            first(NT-1,c,(NT-1)%2)
            dcT_v[part(c,RT),0:(NT-1)*RT]=nt(won_v[part(c,RT),:],hb_v[0:(NT-1)*RT,:]).astype(BF)
        loop(4,closing)
        pltpu.make_async_copy(f_v.at[pl.ds((NT-1)*RT,RT)],dp1_o.at[pl.ds((NT-1)*RT,RT)],osem.at[3]).start()
        def last(c): dcT_v[part(c,RT),(NT-1)*RT:]=nt(won_v[part(c,RT),:],hb_v[(NT-1)*RT:,:]).astype(BF)
        loop(4,last)
        def put(o,v):
            for k in range(v.shape[1]//128):
                g_ref[o//128+k:o//128+k+1,:]=v[:,k*128:(k+1)*128]
        for i,at in enumerate((OG2,OC2,O2,OG1,OC1,OO)):
            put(at,jnp.sum(gb_v[8*i:8*i+8,:],axis=0,keepdims=True))
        for c in range(NC): put(O1+c*CH,jnp.sum(ga_v[8*c:8*c+8,:],axis=0,keepdims=True))
        cd=pltpu.make_async_copy(dcT_v,dcT_o,osem.at[4]); cd.start()
        if comm:
            for m in (0,2,3): g.sends_done(m)
        pltpu.make_async_copy(ov,out_o,osem.at[2]).wait()
        pltpu.make_async_copy(f_v,dp1_o,osem.at[3]).wait()
        cd.wait()
    V=pltpu.VMEM
    scr=[V((T,D),BF),V((T,D),BF),V((D,D),BF),V((D,D),BF),V((FF,D),BF),V((D,FF),BF),V((T,D),F32),V((T,128),F32),
        V((T,D),BF),V((T,FF),BF),V((T,FF),BF),V((T,D),F32),V((2,T,UC),F32),V((2,RT,D),F32),V((2,RT,D),BF),V((8*NC,CH),F32),V((48,D),F32),DMA((11,)),DMA((QC,)),DMA((2,S)),DMA((5,))]
    if comm: scr+=[V((mats[2]["R"],mats[2]["L"]),BF)]+comm_scratch(n)
    out=pl.pallas_call(kernel,
        out_shape=[SDS((3*D,T),BF),SDS((D,T),BF),SDS((H,S,SEQ,SEQ),BF),SDS((T,D),BF),SDS((T,D),F32),SDS((D,T),BF),SDS((12*D//128,128),F32)]+full_shapes(mats[:1],ndp,nfs),
        in_specs=[ANY,ANY,VM,VM,VM]+[ANY,ANY,VM if comm else ANY,ANY],out_specs=[ANY]*6+[VM]+([ANY] if comm else []),scratch_shapes=scr,
        compiler_params=comm_params(mats,cid),name="forward")(x,cot,bias,seg,pad,*sources)
    return out[:7],(out[7] if comm else sources[0])

STEP=5
decay_first=0.5
decay_second=0.5
adam_eps=1e-08
step_rate=0.4
NB=12
BS=32
LATE=2*D//128
EARLY=10*D//128
exact=lax.Precision.HIGHEST

def dot_exact(a,b,ca,cb):
    return lax.dot_general(a,b,(((ca,),(cb,)),((),())),precision=exact,preferred_element_type=F32)

class Reduce:
    def __init__(self,src,plane_buf,z_buf,ssem,psem,zsem):
        self.src,self.pb,self.zb,self.ssem,self.psem,self.zsem=src,plane_buf,z_buf,ssem,psem,zsem
        dp=lax.axis_index("dp"); self.x=lax.axis_index("fsdp")
        self.z=dp//4; self.y=(dp//2)%2; self.c=dp%2
        self.me=self.y*4+self.c*2+self.x
    def plane_peer(self,r):
        def flip(a,b): return 1-a if b else a
        return (self.z*4+flip(self.y,r&4)*2+flip(self.c,r&2),flip(self.x,r&1))
    def z_peer(self,r):
        hi,lo=self.z//2,self.z%2
        z=(1-hi if r&2 else hi)*2+(1-lo if r&1 else lo)
        return (z*4+self.y*2+self.c,self.x)
    def barrier(self):
        bar=pltpu.get_barrier_semaphore()
        for r in range(1,8): pl.semaphore_signal(bar,inc=1,device_id=self.plane_peer(r),device_id_type=MESH)
        for r in range(1,4): pl.semaphore_signal(bar,inc=1,device_id=self.z_peer(r),device_id_type=MESH)
        pl.semaphore_wait(bar,10)
    def copies(self,stage):
        buf,sem,idx=(self.pb,self.psem,self.me) if stage==0 else (self.zb,self.zsem,self.z)
        peers=[self.plane_peer(r) for r in range(1,8)] if stage==0 else [self.z_peer(r) for r in range(1,4)]
        return [pltpu.make_async_remote_copy(self.src if stage==0 else self.zb.at[idx],buf.at[idx],self.ssem.at[stage*7+i],sem.at[idx],
            device_id=p,device_id_type=MESH) for i,p in enumerate(peers)]
    def start(self):
        for c in self.copies(0): c.start()
    def gather(self,stage):
        buf,sem,idx,k=(self.pb,self.psem,self.me,8) if stage==0 else (self.zb,self.zsem,self.z,NZ)
        for q in range(k):
            @pl.when(q!=idx)
            def _(): pltpu.make_async_copy(buf.at[q],buf.at[q],sem.at[q]).wait()
    def middle(self):
        self.gather(0)
        self.pb[self.me]=self.src[...]
        tot=self.pb[0]
        for q in range(1,8): tot=tot+self.pb[q]
        self.zb[self.z]=tot
        for c in self.copies(1): c.start()
    def end(self):
        self.gather(1)
        tot=self.zb[0]
        for q in range(1,NZ): tot=tot+self.zb[q]
        return tot
    def finish(self):
        for st in (0,1):
            for c in self.copies(st): c.wait_send()

def reduce_scratch(rows):
    return [pltpu.VMEM((rows,128),F32),pltpu.VMEM((8,rows,128),F32),pltpu.VMEM((NZ,rows,128),F32),DMA((10,)),DMA((8,)),DMA((NZ,))]

def fold_tables(n):
    i=lax.broadcasted_iota(jnp.int32,(32*n,8*n),0); j=lax.broadcasted_iota(jnp.int32,(32*n,8*n),1)
    sel=jnp.where(i//4==j,1.0,0.0)
    i=lax.broadcasted_iota(jnp.int32,(32*n,128),0); j=lax.broadcasted_iota(jnp.int32,(32*n,128),1)
    mask=jnp.where(i%4==j//32,1.0,0.0)
    i=lax.broadcasted_iota(jnp.int32,(128,32),0); j=lax.broadcasted_iota(jnp.int32,(128,32),1)
    fold=jnp.where(i%32==j,1.0,0.0)
    return sel,mask,fold

def attn_tail(p,qkvT,ctxT,dcT,dp1,wqkvT,update,cid):
    S=p.shape[1]; T=S*SEQ; G=2; NI=H//G; R=G*HD; RT=256; NT=T//RT
    up=update is not None
    def kernel(*refs):
        p_h,qkv_h,c_h,d_h,dp_h,w_h=refs[:6]; o=6
        if up: g_in,mf_h,ms_h,bl_h,br_h=refs[o:o+5]; o+=5
        if up: ig_o,gs_o,st_v=refs[o:o+3]; o+=3
        else: ig_o,gl_o=refs[o:o+2]; o+=2
        pb,qkv_v,c_v,d_v,dp_v,w_v,ig_v,ones_v,psem,lsem,wsem,osem=refs[o:o+12]; o+=12
        if up:
            early_refs=refs[o:o+6]; late_refs=refs[o+6:o+12]; o+=12
            xs,xr=refs[o:o+2]; o+=2
            early=Reduce(*early_refs); late=Reduce(*late_refs); gl=late_refs[0]
        else: gl=gl_o
        PB=3
        def p_load(i): return [pltpu.make_async_copy(p_h.at[i*G+h],pb.at[lax.rem(i,PB),h],psem.at[lax.rem(i,PB),h]) for h in range(G)]
        def begin_p(i):
            for c in p_load(i): c.start()
        def chunk(i):
            out=[pltpu.make_async_copy(qkv_h.at[part(i+k*NI,R)],qkv_v.at[part(i+k*NI,R)],lsem.at[i,k]) for k in range(3)]
            return out+[pltpu.make_async_copy(a.at[part(i,R)],b.at[part(i,R)],lsem.at[i,3+k]) for k,(a,b) in enumerate(((d_h,d_v),(c_h,c_v)))]
        def begin(i):
            for c in chunk(i): c.start()
        begin(0); begin_p(0); begin(1); begin_p(1)
        wl=[pltpu.make_async_copy(w_h.at[pl.ds(k*D,D)],w_v.at[pl.ds(k*D,D)],wsem.at[k]) for k in range(3)]
        dl=pltpu.make_async_copy(dp_h,dp_v,wsem.at[3])
        ones_v[...]=jnp.ones_like(ones_v)
        if up:
            early.barrier()
            early_refs[0][...]=g_in[LATE:,:]
            early.start()
            x=early.x
            states=[]
            for k,a in enumerate((mf_h,ms_h,bl_h,br_h)):
                states.append(pltpu.make_async_remote_copy(a.at[0],st_v.at[k,x],xs.at[k],xr.at[k],device_id=early.plane_peer(1),device_id_type=MESH))
                states.append(pltpu.make_async_copy(a.at[0],st_v.at[k,x],xs.at[4+k]))
            for c in states: c.start()
        def back(i):
            @pl.when(i<NI-2)
            def _(): begin(i+2); begin_p(i+2)
            for k in range(3):
                @pl.when(i==k+1)
                def _(): wl[k].start()
            @pl.when(i==4)
            def _(): dl.start()
            for c in chunk(i)+p_load(i): c.wait()
            b=lax.rem(i,PB)
            for s in range(S):
                cols=pl.ds(s*SEQ,SEQ)
                for h in range(G):
                    r=part(i*G+h,HD); rk=part(i*G+h+H,HD); rv=part(i*G+h+2*H,HD)
                    d=d_v[r,cols]
                    pr=pb[b,h,s]
                    q=qkv_v[r,cols]; k=qkv_v[rk,cols]; v=qkv_v[rv,cols]
                    delta=jnp.sum(d.astype(F32)*c_v[r,cols].astype(F32),axis=0,keepdims=True)
                    ds=(pr.astype(F32)*(tn(v,d)-delta)).astype(BF)
                    qkv_v[rv,cols]=nt(d,pr).astype(BF)
                    qkv_v[rk,cols]=(nt(q,ds)*0.125).astype(BF)
                    qkv_v[r,cols]=(nn(k,ds)*0.125).astype(BF)
            if up:
                @pl.when(i==3)
                def _(): early.middle()
        loop(NI,back)
        for j,at in enumerate((0,2*D)):
            sums=nt(ones_v[...],qkv_v[at:at+D,:])
            for k in range(D//128): gl[j*(D//128)+k:j*(D//128)+k+1,:]=sums[0:1,k*128:(k+1)*128]
        if up: late.start()
        for c in wl+[dl]: c.wait()
        def finish(t):
            cols=part(t,RT)
            acc=dp_v[cols,:]
            for k in range(3):
                acc=acc+tn(qkv_v[k*D:(k+1)*D,cols],w_v[k*D:(k+1)*D,:])
            ig_v[cols,:]=acc.astype(BF)
            pltpu.make_async_copy(ig_v.at[cols],ig_o.at[cols],osem.at[0]).start()
            if up:
                @pl.when(t==1)
                def _(): late.middle()
        loop(NT,finish)
        if up:
            for c in states: c.wait()
            gs_o[LATE:,:]=early.end()
            gs_o[0:LATE,:]=late.end()
            early.finish(); late.finish()
        pltpu.make_async_copy(ig_v,ig_o,osem.at[0]).wait()
    V=pltpu.VMEM
    scr=[V((3,G,S,SEQ,SEQ),BF),V((3*D,T),BF),V((D,T),BF),V((D,T),BF),V((T,D),F32),V((3*D,D),BF),V((T,D),BF),V((8,T),BF),DMA((3,G)),DMA((NI,5)),DMA((4,)),DMA((1,))]
    ins=[p,qkvT,ctxT,dcT,dp1,wqkvT]; specs=[ANY]*6
    outs=[SDS((T,D),BF)]; ospecs=[ANY]
    if up:
        g,mf,ms,bl,br=update
        ins+=[g,mf,ms,bl,br]; specs+=[VM]+[ANY]*4
        outs+=[SDS((NB*8,128),F32),SDS((4,2)+mf.shape[1:],F32)]; ospecs+=[VM,VM]
        scr+=reduce_scratch(EARLY)+reduce_scratch(LATE)+[DMA((8,)),DMA((4,))]
    else:
        outs+=[SDS((LATE,128),F32)]; ospecs+=[VM]
    return pl.pallas_call(kernel,out_shape=outs,in_specs=specs,out_specs=ospecs,scratch_shapes=scr,
        compiler_params=comm_params([1] if up else [],cid),name="attn_tail")(*ins)

def update_step(out,ig,grads,state,bias,owners):
    cap=state.shape[2]; NP=4
    def kernel(out_h,ig_h,g_in,st_v,b_in,own_s,out_o,ig_o,bg_o,mf_o,ms_o,bn_o,bl_o,m_st,v_st,v,sem):
        rows=out.shape[0]//NP
        def moves(down,k):
            a,b=((out_h,out_o),(ig_h,ig_o))[k]
            at=[pl.ds(i*rows,rows) for i in range(NP)]
            if down: return [pltpu.make_async_copy(v.at[k,r],b.at[r],sem.at[1,k,i]) for i,r in enumerate(at)]
            return [pltpu.make_async_copy(a.at[r],v.at[k,r],sem.at[0,k,i]) for i,r in enumerate(at)]
        for k in range(2):
            for c in moves(0,k): c.start()
        x=lax.axis_index("fsdp")
        owner=[own_s[b] for b in range(NB)]
        rank=[]
        for b in range(NB):
            r=jnp.int32(0)
            for e in range(b): r=r+jnp.where(owner[e]==owner[b],1,0)
            rank.append(r)
        def adam(b0,n,tiles):
            sel,mask,fold=fold_tables(n)
            gs=dot_exact(dot_exact(sel,tiles,1,0)*mask,fold,1,0)
            outs=[]
            for j in range(n):
                b=b0+j
                at=jnp.minimum(rank[b],st_v.shape[2]-1)
                first,second,left,right=[st_v[k,owner[b],at] for k in range(4)]
                left,right=left.astype(BF),right.astype(BF)
                t=nn(tn(left,gs[j*BS:(j+1)*BS,:].astype(BF)).astype(BF),right)
                m=decay_first*first+(1.0-decay_first)*t
                v=decay_second*second+(1.0-decay_second)*t*t
                m_st[b]=m; v_st[b]=v
                un=(m/(1.0-decay_first**STEP))/(jnp.sqrt(v/(1.0-decay_second**STEP))+adam_eps)
                outs.append(nt(nn(left,un.astype(BF)).astype(BF),right))
                if j in (0,2):
                    for c in moves(0,j//2): c.wait()
                    for c in moves(1,j//2): c.start()
            back_=dot_exact(jnp.concatenate(outs,0),fold,1,1)*mask
            new=b_in[8*b0:8*(b0+n),:]-step_rate*dot_exact(sel,back_,0,0)
            bg_o[8*b0:8*(b0+n),:]=tiles
            bn_o[8*b0:8*(b0+n),:]=new
            bl_o[8*b0:8*(b0+n),:]=new.astype(BF)
        adam(0,NB,g_in[...])
        for c in range(mf_o.shape[1]):
            at=jnp.int32(0); hit=jnp.int32(0)
            for b in range(NB):
                here=(owner[b]==x)&(rank[b]==c)
                at=at+jnp.where(here,b,0); hit=hit+jnp.where(here,1,0)
            at=jnp.minimum(at,NB-1)
            filled=hit.astype(F32)
            mf_o[0,c]=m_st[at]*filled
            ms_o[0,c]=v_st[at]*filled
        for k in range(2):
            for c in moves(1,k): c.wait()
    m=SDS((1,cap,BS,BS),F32)
    return pl.pallas_call(kernel,
        out_shape=[SDS(out.shape,BF),SDS(ig.shape,BF),SDS((NB*8,128),F32),m,m,SDS((NB*8,128),F32),SDS((NB*8,128),BF)],
        in_specs=[ANY,ANY,VM,VM,VM,pl.BlockSpec(memory_space=pltpu.SMEM)],out_specs=[ANY,ANY]+[VM]*5,
        scratch_shapes=[pltpu.VMEM((NB,BS,BS),F32),pltpu.VMEM((NB,BS,BS),F32),pltpu.VMEM((2,)+out.shape,BF),DMA((2,2,NP))],
        compiler_params=pltpu.CompilerParams(vmem_limit_bytes=VMEM_CAP),name="update")(out,ig,grads,state,bias,owners)


def placement_table(owners, owner_count, capacity):
    block_count = owners.shape[0]
    index_b = jnp.arange(block_count, dtype=jnp.int32)
    same_owner = owners[:, None] == owners[None, :]
    earlier = index_b[None, :] < index_b[:, None]
    rank_of = jnp.sum((same_owner & earlier).astype(jnp.int32), axis=1)
    owner_hit = owners[None, None, :] == jnp.arange(owner_count, dtype=jnp.int32)[:, None, None]
    slot_hit = rank_of[None, None, :] == jnp.arange(capacity, dtype=jnp.int32)[None, :, None]
    return (owner_hit & slot_hit).astype(jnp.float32)


def adam_rotated(grad_slots, value_slots, first_old, second_old, left_basis, right_basis, filled):
    turned = jnp.einsum("fcki,fckj->fcij", left_basis, grad_slots, precision=exact)
    turned = jnp.einsum("fcik,fckj->fcij", turned, right_basis, precision=exact)
    first_raw = decay_first * first_old + (1.0 - decay_first) * turned
    second_raw = decay_second * second_old + (1.0 - decay_second) * turned * turned
    normed_step = (
        first_raw
        / (1.0 - decay_first**STEP)
        / (jnp.sqrt(second_raw / (1.0 - decay_second**STEP)) + adam_eps)
    )
    restored = jnp.einsum("fcik,fckj->fcij", left_basis, normed_step, precision=exact)
    restored = jnp.einsum("fcik,fcjk->fcij", restored, right_basis, precision=exact)
    value_new = value_slots - step_rate * restored
    return (first_raw * filled, second_raw * filled, value_new * filled)


def body(
    acts,
    cotangent,
    seg_ids,
    pad_mask,
    qkv_weight,
    out_weight,
    in_weight,
    down_weight,
    biases,
    moment_first,
    moment_second,
    basis_left,
    basis_right,
    owners,
):
    ndp, nfs = lax.axis_size("dp"), lax.axis_size("fsdp")
    shards = (qkv_weight.T, out_weight.T, in_weight, down_weight.T)
    slots = acts.shape[0] * acts.shape[1]
    x = acts.reshape(slots * SEQ, D)
    cot = cotangent.reshape(slots * SEQ, D)
    seg = seg_ids.reshape(slots, 1, SEQ)
    pad = pad_mask.reshape(slots, 1, SEQ)
    bias = biases.reshape(1, -1)
    if (ndp, nfs) == (16, 2):
        (qkvT, ctxT, p, out, dp1, dcT, g), wqT = forward(matdesc(), shards, 1, x, cot, bias, seg, pad, ndp, nfs)
        state = (g, moment_first, moment_second, basis_left, basis_right)
        ig, total, state = attn_tail(p, qkvT, ctxT, dcT, dp1, wqT, state, 2)
        out, ig, bg, mf, ms, bn, bl = update_step(out, ig, total, state, biases.reshape(-1, 128), owners)
        return (
            out.reshape(acts.shape),
            ig.reshape(acts.shape),
            bg.reshape(-1),
            mf,
            ms,
            bn.reshape(-1),
            bl.reshape(-1),
        )
    whole = [
        lax.all_gather(lax.all_gather(t, "fsdp", axis=1, tiled=True), "dp", axis=0, tiled=True)
        for t in (shards[0], shards[1], shards[2].T, shards[3])
    ]
    (qkvT, ctxT, p, out, dp1, dcT, g), wqT = forward([], whole, 0, x, cot, bias, seg, pad, ndp, nfs)
    ig, gl = attn_tail(p, qkvT, ctxT, dcT, dp1, wqT, None, 0)
    outputs, input_grads = out.reshape(acts.shape), ig.reshape(acts.shape)
    grad_total = jnp.concatenate([gl, g[LATE:]], 0).reshape(-1)
    block_count = owners.shape[0]
    block_side = moment_first.shape[2]
    slot_table = placement_table(owners, lax.axis_size("fsdp"), moment_first.shape[1])
    grad_slots = jnp.einsum(
        "fcb,bij->fcij",
        slot_table,
        grad_total.reshape(block_count, block_side, block_side),
        precision=exact,
    )
    summed = lax.psum(grad_slots.astype(jnp.bfloat16), "dp")
    owned_grad = lax.psum_scatter(summed, "fsdp", scatter_dimension=0, tiled=True).astype(
        jnp.float32
    )
    own_table = lax.dynamic_slice_in_dim(slot_table, lax.axis_index("fsdp"), 1, 0)
    value_slots = jnp.einsum(
        "fcb,bij->fcij",
        own_table,
        biases.reshape(block_count, block_side, block_side),
        precision=exact,
    )
    filled = jnp.sum(own_table, axis=2)[:, :, None, None]
    first_new, second_new, value_new = adam_rotated(
        owned_grad, value_slots, moment_first, moment_second, basis_left, basis_right, filled
    )
    shared_grad, shared_value = (
        lax.all_gather(owned_grad, "fsdp", axis=0, tiled=True),
        lax.all_gather(value_new, "fsdp", axis=0, tiled=True),
    )
    bias_grad = jnp.einsum("fcb,fcij->bij", slot_table, shared_grad, precision=exact).reshape(
        biases.shape[0]
    )
    bias_new = jnp.einsum("fcb,fcij->bij", slot_table, shared_value, precision=exact).reshape(
        biases.shape[0]
    )
    return (
        outputs,
        input_grads,
        bias_grad,
        first_new,
        second_new,
        bias_new,
        bias_new.astype(jnp.bfloat16),
    )


def solution(mesh):
    placed = (
        P(None, ("dp", "fsdp"), None, None),
        P(None, ("dp", "fsdp"), None, None),
        P(None, ("dp", "fsdp"), None),
        P(None, ("dp", "fsdp"), None),
        P("fsdp", "dp"),
        P("fsdp", "dp"),
        P("fsdp", "dp"),
        P("fsdp", "dp"),
        P(),
        P("fsdp", None, None, None),
        P("fsdp", None, None, None),
        P("fsdp", None, None, None),
        P("fsdp", None, None, None),
        P(),
    )
    return jax.shard_map(
        body,
        mesh=mesh,
        in_specs=placed,
        out_specs=(
            P(None, ("dp", "fsdp"), None, None),
            P(None, ("dp", "fsdp"), None, None),
            P(),
            P("fsdp", None, None, None),
            P("fsdp", None, None, None),
            P(),
            P(),
        ),
        check_vma=False,
    )
```
